128 devices in a mesh: pts: 8 (over x, core), cam: 16 (over z, y).
Axes of the slice: x: 4, y: 4, z: 4, core: 2. Of those that a mesh axis runs over, the one named last changes fastest.
Arguments:
- camera_jacobian_rows: float32 [18, 32768, 128], P(None, ('pts', 'cam')), may hold values from -3 to 3
- jac_pt: float32 [6, 32768, 128], P(None, ('pts', 'cam')), may hold values from -3 to 3
- obs_cam: int32 [32768, 128], P(('pts', 'cam')), may hold values from 0 to 127
- obs_pt: int32 [32768, 128], P(('pts', 'cam')), may hold values from 0 to 127
- block_slot_entry: int32 [32768], P(('pts', 'cam')), may hold values from 0 to 255
- cov: int32 [2048, 16], P(('pts', 'cam')), may hold values from 0 to 31, as said below
- cam_grad: float32 [9, 65536], P(None, 'cam'), may hold values from -6 to 6
- cam_damp: float32 [9, 65536], P(None, 'cam'), may hold values from 2 to 40
- pt_grad: float32 [3, 524288], P(None, ('pts', 'cam')), may hold values from -6 to 6
- pt_damp: float32 [3, 524288], P(None, ('pts', 'cam')), may hold values from 0.5 to 4
Outputs:
- cam_step: float32 [9, 65536], P(None, 'cam')
- cam_resid: float32 [9, 65536], P(None, 'cam')
- pt_step: float32 [3, 524288], P(None, ('pts', 'cam'))
The draws below stay inside these ranges and needn't reach their ends.
Inputs may be any that keep to these rules, and one draw needn't show every extreme that they name: `cov`: the 16 block numbers of one row are distinct.
All inputs are finite; a program needn't handle non-finite values.
Results may differ from the reference program's by a relative error of at most 0.00017.
Values sent between devices are 32-bit elements; how exact they have to be, the bound alone decides.
No kernel may reach another device: no remote copies, remote signals or barrier semaphores. Data moves between devices by JAX's collectives and lax.ppermute only.
A program may use at most 64 MiB of HBM per device.

```python
import math
import jax
import jax.numpy as jnp

BLK = 128
BPT = 8
ITERS = 2
CBD = 32
KJ = 16
OBLK = 256
SLOT_COUNT = 256
NCAM = 65536
NPTS = 524288
OBSERVATION_BLKS = 32768
N_CAM = 16
DEVICES = 128


def draw_cov(key, part):
    key = jax.random.fold_in(key, 7)
    scores = jax.random.randint(key, (DEVICES * N_CAM, CBD), 0, 1 << 20) * CBD + jnp.arange(CBD, dtype=jnp.int32)[None, :]
    order = jnp.argsort(scores, axis=1)
    return order[:, :KJ].astype(jnp.int32)


def plant(array, rng, smallest, largest):
    place = [jax.random.randint(jax.random.fold_in(rng, axis), (), 0, length) for axis, length in enumerate(array.shape)]
    main_axis = array.shape.index(max(array.shape))
    next_to = place[:main_axis] + [(place[main_axis] + 1) % array.shape[main_axis]] + place[main_axis + 1:]
    return array.at[tuple(place)].set(smallest).at[tuple(next_to)].set(largest)


def level_of(stream_key, dims, shards, least, high):
    def one(axis_at, parts):
        heights = jax.random.uniform(jax.random.fold_in(jax.random.fold_in(stream_key, 6), axis_at), (parts,), jnp.float32, least / len(shards), high / len(shards))
        return jnp.repeat(jnp.exp(heights), dims[axis_at] // parts).reshape((-1,) + (1,) * (len(dims) - axis_at - 1))

    loudness = one(*shards[0])
    for cut in shards[1:]:
        loudness = loudness * one(*cut)
    return loudness


def normal_values(own_key, extent, scale, limit, split=(), kind=jnp.bfloat16):
    loudness = level_of(own_key, extent, split, -0.22, 0.18) if split else 1.0
    drawn = jax.random.normal(own_key, extent, jnp.float32) * scale * loudness
    return jnp.minimum(jnp.maximum(drawn, -limit), limit).astype(kind)


def setup_inputs(seed: int = 0) -> dict:
    keys = jax.random.split(jax.random.key(seed), 11)
    return {
        "camera_jacobian_rows": normal_values(keys[0], (18, OBSERVATION_BLKS, BLK), 0.5, 3.0, ((1, 128),), jnp.float32),
        "jac_pt": normal_values(keys[1], (6, OBSERVATION_BLKS, BLK), 0.5, 3.0, ((1, 128),), jnp.float32),
        "obs_cam": plant(jax.random.randint(keys[2], (OBSERVATION_BLKS, BLK), 0, BLK), jax.random.fold_in(keys[2], 1), 0, BLK - 1).astype(jnp.int32),
        "obs_pt": plant(jax.random.randint(keys[3], (OBSERVATION_BLKS, BLK), 0, BLK), jax.random.fold_in(keys[3], 1), 0, BLK - 1).astype(jnp.int32),
        "block_slot_entry": plant(jax.random.randint(keys[4], (OBSERVATION_BLKS,), 0, SLOT_COUNT), jax.random.fold_in(keys[4], 1), 0, SLOT_COUNT - 1).astype(jnp.int32),
        "cov": draw_cov(jax.random.fold_in(keys[10], 71), 0),
        "cam_grad": normal_values(keys[6], (9, NCAM), 1.0, 6.0, ((1, 16),), jnp.float32),
        "cam_damp": jnp.clip(jnp.exp(math.log(40.0) - 2.9957323 * jax.random.uniform(keys[7], (9, NCAM), jnp.float32) ** level_of(keys[7], (9, NCAM), ((1, 16),), -0.2, 0.2)), 2.0, 40.0),
        "pt_grad": normal_values(keys[8], (3, NPTS), 1.0, 6.0, ((1, 128),), jnp.float32),
        "pt_damp": jnp.clip(jnp.exp(math.log(4.0) - 2.0794415 * jax.random.uniform(keys[9], (3, NPTS), jnp.float32) ** level_of(keys[9], (3, NPTS), ((1, 128),), -0.2, 0.2)), 0.5, 4.0),
    }


def block_sums(values, ids, total):
    count_rows = values.shape[0]
    flat = values.reshape(count_rows, -1).T
    return jax.ops.segment_sum(flat, ids.reshape(-1), num_segments=total).T


def cam_rows(cam_jac, values):
    shaped = cam_jac.reshape((2, 9) + cam_jac.shape[1:])
    return jnp.sum(shaped * values[None], axis=1)


def cam_cols(cam_jac, values):
    shaped = cam_jac.reshape((2, 9) + cam_jac.shape[1:])
    return jnp.sum(shaped * values[:, None], axis=0)


def pt_rows(pt_jac, values):
    shaped = pt_jac.reshape((2, 3) + pt_jac.shape[1:])
    return jnp.sum(shaped * values[None], axis=1)


def pt_cols(pt_jac, values):
    shaped = pt_jac.reshape((2, 3) + pt_jac.shape[1:])
    return jnp.sum(shaped * values[:, None], axis=0)


def point_inverse(pt_jac, pt_damp, point_ids, total):
    shaped = pt_jac.reshape((2, 3) + pt_jac.shape[1:])
    pairs = [(0, 0), (0, 1), (0, 2), (1, 1), (1, 2), (2, 2)]
    terms = jnp.stack([jnp.sum(shaped[:, a] * shaped[:, b], axis=0) for a, b in pairs])
    entry = block_sums(terms, point_ids, total)
    c00 = entry[0] + pt_damp[0]
    c01 = entry[1]
    c02 = entry[2]
    c11 = entry[3] + pt_damp[1]
    c12 = entry[4]
    c22 = entry[5] + pt_damp[2]
    a00 = c11 * c22 - c12 * c12
    a01 = c02 * c12 - c01 * c22
    a02 = c01 * c12 - c02 * c11
    a11 = c00 * c22 - c02 * c02
    a12 = c01 * c02 - c00 * c12
    a22 = c00 * c11 - c01 * c01
    recip = 1.0 / (c00 * a00 + c01 * a01 + c02 * a02)
    return jnp.stack([a00, a01, a02, a11, a12, a22]) * recip[None]


def apply_three(inverse, values):
    first = inverse[0] * values[0] + inverse[1] * values[1] + inverse[2] * values[2]
    second = inverse[1] * values[0] + inverse[3] * values[1] + inverse[4] * values[2]
    third = inverse[2] * values[0] + inverse[4] * values[1] + inverse[5] * values[2]
    return jnp.stack([first, second, third])


def point_pass(camera_jacobian_rows, jac_pt, camera_vals, point_ids, inverse, total):
    projected = cam_rows(camera_jacobian_rows, camera_vals)
    collected = block_sums(pt_cols(jac_pt, projected), point_ids, total)
    solved = apply_three(inverse, collected)
    corrected = projected - pt_rows(jac_pt, solved[:, point_ids])
    return cam_cols(camera_jacobian_rows, corrected)


def reference(camera_jacobian_rows, jac_pt, obs_cam, obs_pt, block_slot_entry, cov, cam_grad, cam_damp, pt_grad, pt_damp):
    nblocks = obs_cam.shape[0]
    blocks = jnp.arange(nblocks, dtype=jnp.int32)
    device_ids = blocks // OBLK
    owner_index = block_slot_entry // KJ
    slot_pos = block_slot_entry % KJ
    local_block = cov[device_ids * N_CAM + owner_index, slot_pos]
    camera_ids = ((owner_index * CBD + local_block) * BLK)[:, None] + obs_cam
    point_ids = (blocks // BPT * BLK)[:, None] + obs_pt
    ncams = cam_grad.shape[1]
    npoints = pt_grad.shape[1]
    inverse = point_inverse(jac_pt, pt_damp, point_ids, npoints)
    preconditioned_gradient = apply_three(inverse, pt_grad)
    rhs_obs = cam_cols(camera_jacobian_rows, pt_rows(jac_pt, preconditioned_gradient[:, point_ids]))
    diag_obs = jnp.sum(camera_jacobian_rows.reshape((2, 9) + camera_jacobian_rows.shape[1:]) ** 2, axis=0)
    setup = block_sums(jnp.concatenate([rhs_obs, diag_obs], axis=0), camera_ids, ncams)
    rhs = cam_grad - setup[:9]
    precond = cam_damp + setup[9:]
    solution = jnp.zeros_like(cam_grad)
    resid = rhs
    direction = resid / precond
    current_norm = jnp.sum(resid * resid / precond)
    for step in range(ITERS):
        image = cam_damp * direction + block_sums(point_pass(camera_jacobian_rows, jac_pt, direction[:, camera_ids], point_ids, inverse, npoints), camera_ids, ncams)
        step_len = current_norm / jnp.sum(direction * image)
        solution = solution + step_len * direction
        resid = resid - step_len * image
        if step + 1 < ITERS:
            following_norm = jnp.sum(resid * resid / precond)
            direction = resid / precond + (following_norm / current_norm) * direction
            current_norm = following_norm
    projected = cam_rows(camera_jacobian_rows, solution[:, camera_ids])
    collected = block_sums(pt_cols(jac_pt, projected), point_ids, npoints)
    pt_step = apply_three(inverse, pt_grad - collected)
    return solution, resid, pt_step
```

```python
import functools

import jax
import jax.numpy as jnp
from jax import lax
from jax.experimental import pallas as pl
from jax.experimental.pallas import tpu as pltpu
from jax.sharding import PartitionSpec as P

BLK = 128
BPT = 8
NP = 9
EXTRA = 8
F32 = jnp.float32
BF16 = jnp.bfloat16
VMEM_LIMIT = 48 * 1024 * 1024


def split3(x):
    hi = x.astype(BF16).astype(F32)
    rest = x - hi
    mid = rest.astype(BF16).astype(F32)
    return hi, mid, rest - mid


def apply_three(inverse, values):
    first = inverse[0] * values[0] + inverse[1] * values[1] + inverse[2] * values[2]
    second = inverse[1] * values[0] + inverse[3] * values[1] + inverse[4] * values[2]
    third = inverse[2] * values[0] + inverse[4] * values[1] + inverse[5] * values[2]
    return [first, second, third]


def lane_pick(table, idx):
    return jnp.take_along_axis(table, idx, axis=1, mode="promise_in_bounds")


def onehot_rows(idx_row):
    rows = lax.broadcasted_iota(jnp.int32, (BLK, BLK), 0)
    return jnp.where(rows == idx_row, 1.0, 0.0).astype(BF16)


NT = (((1,), (1,)), ((), ()))


def point_scatter(stage, vals, idx_ref, t):
    for j, val in enumerate(vals):
        for s, piece in enumerate(split3(val)):
            stage[(s * 8 + j) * BPT : (s * 8 + j + 1) * BPT, :] = piece
    lhs, rhs = [], []
    for b in range(BPT):
        lhs.append(stage[pl.ds(b, 24, stride=BPT), :].astype(BF16))
        rhs.append(onehot_rows(idx_ref[pl.ds(t * BPT + b, 1), :]))
    res = lax.dot_general(
        jnp.concatenate(lhs, axis=1), jnp.concatenate(rhs, axis=1), NT, preferred_element_type=F32
    )
    return res[0:8] + res[8:16] + res[16:24]


def cam_scatter(stage, vals, idx_ref, t, pblk, pad):
    for k, val in enumerate(vals):
        for s, piece in enumerate(split3(val)):
            stage[(s * pad + k) * BPT : (s * pad + k + 1) * BPT, :] = piece
    for b in range(BPT):
        lhs = stage[pl.ds(b, 3 * pad, stride=BPT), :].astype(BF16)
        res = lax.dot_general(
            lhs, onehot_rows(idx_ref[pl.ds(t * BPT + b, 1), :]), NT, preferred_element_type=F32
        )
        start = pl.multiple_of((t * BPT + b) * pad, 8)
        pblk[pl.ds(start, pad), :] = res[0:pad] + res[pad : 2 * pad] + res[2 * pad : 3 * pad]


def blocks_to_dense(pblk, bt_ref, count, pad, mine_ref, other_ref):
    nblocks = bt_ref.shape[1]
    half = bt_ref.shape[0] // 2
    owners, held = mine_ref.shape[0], half // mine_ref.shape[0]
    for k in range(count):
        x = pblk[pl.ds(k, nblocks, stride=pad), :]
        rhs = jnp.concatenate(split3(x), axis=1).astype(BF16)
        res = jnp.dot(bt_ref[...], rhs, preferred_element_type=F32)
        res = res[:, :BLK] + res[:, BLK : 2 * BLK] + res[:, 2 * BLK :]
        rows = slice(k * held, (k + 1) * held)
        mine_ref[:, rows, :] = res[:half].reshape(owners, held, BLK)
        other_ref[:, rows, :] = res[half:].reshape(owners, held, BLK)


def setup_kernel(
    jac, jp, oc, op, bt, pt_grad, pt_damp, mine, other, inv_out, pg_out, stage, stage2, col, pblk
):
    tiles = jac.shape[1] // BPT

    def terms(t, carry):
        rows = pl.ds(pl.multiple_of(t * BPT, BPT), BPT)
        a = [jp[j, rows, :] for j in range(6)]
        vals = [
            a[p] * a[q] + a[3 + p] * a[3 + q]
            for p, q in [(0, 0), (0, 1), (0, 2), (1, 1), (1, 2), (2, 2)]
        ]
        col[pl.ds(pl.multiple_of(t * 8, 8), 8), :] = point_scatter(stage, vals, op, t)
        return carry

    lax.fori_loop(0, tiles, terms, 0)
    entry = [col[pl.ds(j, tiles, stride=8), :] for j in range(6)]
    c00 = entry[0] + pt_damp[0]
    c01 = entry[1]
    c02 = entry[2]
    c11 = entry[3] + pt_damp[1]
    c12 = entry[4]
    c22 = entry[5] + pt_damp[2]
    a00 = c11 * c22 - c12 * c12
    a01 = c02 * c12 - c01 * c22
    a02 = c01 * c12 - c02 * c11
    a11 = c00 * c22 - c02 * c02
    a12 = c01 * c02 - c00 * c12
    a22 = c00 * c11 - c01 * c01
    recip = 1.0 / (c00 * a00 + c01 * a01 + c02 * a02)
    inv = [a * recip for a in (a00, a01, a02, a11, a12, a22)]
    for j in range(6):
        inv_out[j] = inv[j]
    pg = apply_three(inv, [pt_grad[j] for j in range(3)])
    for j in range(3):
        pg_out[j] = pg[j]

    def rhs_terms(t, carry):
        rows = pl.ds(pl.multiple_of(t * BPT, BPT), BPT)
        pidx = op[rows, :]
        g = [
            lane_pick(jnp.broadcast_to(pg_out[j, pl.ds(t, 1), :], (BPT, BLK)), pidx)
            for j in range(3)
        ]
        c0 = jp[0, rows, :] * g[0] + jp[1, rows, :] * g[1] + jp[2, rows, :] * g[2]
        c1 = jp[3, rows, :] * g[0] + jp[4, rows, :] * g[1] + jp[5, rows, :] * g[2]
        vals = []
        diag = []
        for k in range(NP):
            j0 = jac[k, rows, :]
            j1 = jac[NP + k, rows, :]
            vals.append(j0 * c0 + j1 * c1)
            diag.append(j0 * j0 + j1 * j1)
        cam_scatter(stage2, vals + diag, oc, t, pblk, 24)
        return carry

    lax.fori_loop(0, tiles, rhs_terms, 0)
    blocks_to_dense(pblk, bt, 2 * NP, 24, mine, other)


def setup_call(jac, jp, oc, op, bt, pt_grad, pt_damp, owners):
    nblocks = jac.shape[1]
    tiles = nblocks // BPT
    held = bt.shape[0] // 2 // owners
    msg = jax.ShapeDtypeStruct((owners, 2 * NP * held, BLK), F32)
    return pl.pallas_call(
        setup_kernel,
        out_shape=[
            msg,
            msg,
            jax.ShapeDtypeStruct((6, tiles, BLK), F32),
            jax.ShapeDtypeStruct((3, tiles, BLK), F32),
        ],
        scratch_shapes=[
            pltpu.VMEM((24 * BPT, BLK), F32),
            pltpu.VMEM((72 * BPT, BLK), F32),
            pltpu.VMEM((tiles * 8, BLK), F32),
            pltpu.VMEM((nblocks * 24, BLK), F32),
        ],
        compiler_params=pltpu.CompilerParams(vmem_limit_bytes=VMEM_LIMIT),
        name="setup_pass",
    )(jac, jp, oc, op, bt, pt_grad, pt_damp)


def operator_kernel(second, *refs):
    if second:
        (jac, jp, oc, op, b_mat, bt, inv, mine_in, other_in, proj_in, scal_in, own,
         mine, other, sol_out, proj, stage, stage2, pick, col, pblk) = refs
    else:
        (jac, jp, oc, op, b_mat, bt, inv, mine_in, other_in,
         mine, other, sol_out, proj, stage, stage2, pick, col, pblk) = refs
    nblocks = jac.shape[1]
    tiles = nblocks // BPT
    owners = mine_in.shape[0]
    held = b_mat.shape[1] // 2 // owners
    half = owners * held
    for k in range(NP):
        rows = slice(k * held, (k + 1) * held)
        x = jnp.concatenate(
            [mine_in[:, rows, :].reshape(half, BLK), other_in[:, rows, :].reshape(half, BLK)], axis=0
        )
        rhs = jnp.concatenate(split3(x), axis=1).astype(BF16)
        res = jnp.dot(b_mat[...], rhs, preferred_element_type=F32)
        pick[k] = res[:, :BLK] + res[:, BLK : 2 * BLK] + res[:, 2 * BLK :]
    if second:
        step_len = scal_in[0]

    def project(t, carry):
        rows = pl.ds(pl.multiple_of(t * BPT, BPT), BPT)
        cidx = oc[rows, :]
        p0 = jnp.zeros((BPT, BLK), F32)
        p1 = jnp.zeros((BPT, BLK), F32)
        for k in range(NP):
            v = lane_pick(pick[k, rows, :], cidx)
            p0 += jac[k, rows, :] * v
            p1 += jac[NP + k, rows, :] * v
        if second:
            p0 = proj_in[0, rows, :] - step_len * p0
            p1 = proj_in[1, rows, :] - step_len * p1
        proj[0, rows, :] = p0
        proj[1, rows, :] = p1
        vals = [jp[j, rows, :] * p0 + jp[3 + j, rows, :] * p1 for j in range(3)]
        col[pl.ds(pl.multiple_of(t * 8, 8), 8), :] = point_scatter(stage, vals, op, t)
        return carry

    lax.fori_loop(0, tiles, project, 0)
    sol = apply_three(
        [inv[j] for j in range(6)], [col[pl.ds(j, tiles, stride=8), :] for j in range(3)]
    )
    for j in range(3):
        sol_out[j] = sol[j]

    def correct(t, carry):
        rows = pl.ds(pl.multiple_of(t * BPT, BPT), BPT)
        pidx = op[rows, :]
        g = [
            lane_pick(jnp.broadcast_to(sol_out[j, pl.ds(t, 1), :], (BPT, BLK)), pidx)
            for j in range(3)
        ]
        p0 = proj[0, rows, :]
        p1 = proj[1, rows, :]
        c0 = p0 - (jp[0, rows, :] * g[0] + jp[1, rows, :] * g[1] + jp[2, rows, :] * g[2])
        c1 = p1 - (jp[3, rows, :] * g[0] + jp[4, rows, :] * g[1] + jp[5, rows, :] * g[2])
        if second:
            zz, zd = carry
            zz = zz + (p0 * c0 + p1 * c1)
            zd = zd + (proj_in[0, rows, :] * c0 + proj_in[1, rows, :] * c1)
            carry = (zz, zd)
        vals = [jac[k, rows, :] * c0 + jac[NP + k, rows, :] * c1 for k in range(NP)]
        cam_scatter(stage2, vals, oc, t, pblk, 16)
        return carry

    zero = jnp.zeros((BPT, BLK), F32)
    sums = lax.fori_loop(0, tiles, correct, (zero, zero) if second else 0)
    blocks_to_dense(pblk, bt, NP, 16, mine, other)
    if second:
        sub = lax.broadcasted_iota(jnp.int32, (EXTRA, BLK), 0)
        row0 = jnp.sum(sums[0], axis=0, keepdims=True)
        row1 = jnp.sum(sums[1], axis=0, keepdims=True)
        extra = jnp.where(sub == 0, row0, jnp.where(sub == 1, row1, own[...]))
        extra = jnp.broadcast_to(extra[None], (owners, EXTRA, BLK))
        mine[:, NP * held :, :] = extra
        other[:, NP * held :, :] = extra


def operator_call(jac, jp, oc, op, b_mat, bt, inv, mine, other, later=None):
    nblocks = jac.shape[1]
    tiles = nblocks // BPT
    owners = mine.shape[0]
    held = bt.shape[0] // 2 // owners
    rows = NP * held + (EXTRA if later else 0)
    msg = jax.ShapeDtypeStruct((owners, rows, BLK), F32)
    operands = [jac, jp, oc, op, b_mat, bt, inv, mine, other]
    vmem = pl.BlockSpec(memory_space=pltpu.VMEM)
    in_specs = [vmem] * len(operands)
    if later:
        operands += list(later)
        in_specs += [vmem, pl.BlockSpec(memory_space=pltpu.SMEM), vmem]
    return pl.pallas_call(
        functools.partial(operator_kernel, bool(later)),
        in_specs=in_specs,
        out_shape=[
            msg,
            msg,
            jax.ShapeDtypeStruct((3, tiles, BLK), F32),
            jax.ShapeDtypeStruct((2, nblocks, BLK), F32),
        ],
        scratch_shapes=[
            pltpu.VMEM((24 * BPT, BLK), F32),
            pltpu.VMEM((48 * BPT, BLK), F32),
            pltpu.VMEM((NP, nblocks, BLK), F32),
            pltpu.VMEM((tiles * 8, BLK), F32),
            pltpu.VMEM((nblocks * 16, BLK), F32),
        ],
        compiler_params=pltpu.CompilerParams(vmem_limit_bytes=VMEM_LIMIT),
        name="second_pass" if later else "first_pass",
    )(*operands)


def local(jac, jp, oc, op, entry, cov, cam_grad, cam_damp, pt_grad, pt_damp):
    owners = lax.axis_size("cam")
    pts = lax.axis_size("pts")
    core = lax.axis_index("pts") % 2
    per_owner = cov.shape[1]
    nblocks = oc.shape[0]
    tiles = nblocks // BPT
    shard = cam_grad.shape[1]
    held = shard // BLK // 2
    half = owners * held

    owner = entry // per_owner
    local_block = cov[owner, entry % per_owner]
    place = ((local_block // held) ^ core) * half + owner * held + local_block % held
    places = jnp.arange(2 * half, dtype=jnp.int32)
    b_mat = (place[:, None] == places[None, :]).astype(BF16)
    bt = (places[:, None] == place[None, :]).astype(BF16)

    swap = [(i, i ^ 1) for i in range(pts)]

    def exchange(x):
        return lax.ppermute(x, "pts", swap)

    def own_half(x):
        shaped = x.reshape(NP, 2, held, BLK)
        return lax.dynamic_index_in_dim(shaped, core, 1, keepdims=False)

    def reduce_sum(mine, other):
        both = mine + exchange(other)
        got = lax.all_to_all(both, "cam", 0, 0, tiled=False).sum(axis=0)
        total = got
        for shift in range(2, pts, 2):
            total = total + lax.ppermute(got, "pts", [(i, (i + shift) % pts) for i in range(pts)])
        return total

    def spread(values, scalar):
        row = jnp.sum(scalar, axis=(0, 1)).reshape(1, BLK)
        chunk = jnp.concatenate(
            [values.reshape(NP * held, BLK), row, jnp.zeros((EXTRA - 1, BLK), F32)], axis=0
        )
        mine = lax.all_to_all(
            jnp.broadcast_to(chunk[None], (owners,) + chunk.shape), "cam", 0, 0, tiled=False
        )
        other = exchange(mine)
        return mine, other, jnp.sum(mine[:, NP * held] + other[:, NP * held])

    mine, other, inv, pg = setup_call(
        jac, jp, oc, op, bt, pt_grad.reshape(3, tiles, BLK), pt_damp.reshape(3, tiles, BLK), owners
    )
    setup = reduce_sum(mine, other).reshape(2, NP, held, BLK)
    damp = own_half(cam_damp)
    rhs = own_half(cam_grad) - setup[0]
    precond = damp + setup[1]
    direction = rhs / precond
    mine, other, norm0 = spread(direction, rhs * direction)
    mine, other, sol0, proj0 = operator_call(jac, jp, oc, op, b_mat, bt, inv, mine, other)
    image0 = damp * direction + reduce_sum(mine, other).reshape(NP, held, BLK)
    scaled = image0 / precond
    mine, other, curvature0 = spread(scaled, direction * image0)
    step0 = norm0 / curvature0
    resid1 = rhs - step0 * image0
    z1 = resid1 / precond
    share = 2.0 / pts

    def lanes(x):
        return jnp.sum(x, axis=(0, 1)).reshape(1, BLK) * share

    own = jnp.concatenate(
        [
            jnp.zeros((2, BLK), F32),
            lanes(resid1 * z1),
            lanes(damp * z1 * z1),
            lanes(damp * z1 * direction),
            jnp.zeros((EXTRA - 5, BLK), F32),
        ],
        axis=0,
    )
    mine, other, sol1, _ = operator_call(
        jac, jp, oc, op, b_mat, bt, inv, mine, other, (proj0, step0.reshape(1), own)
    )
    got = reduce_sum(mine, other)
    image_z = damp * z1 + got[: NP * held].reshape(NP, held, BLK)
    sums = jnp.sum(got[NP * held :], axis=1)
    norm1 = sums[2]
    beta = norm1 / norm0
    curvature1 = (sums[0] + sums[3]) + 2.0 * beta * (sums[1] + sums[4]) + beta * beta * curvature0
    step1 = norm1 / curvature1
    direction1 = z1 + beta * direction
    image1 = image_z + beta * image0
    out = jnp.stack([step0 * direction + step1 * direction1, resid1 - step1 * image1])
    theirs = exchange(out)
    first = jnp.where(core == 0, out, theirs)
    last = jnp.where(core == 0, theirs, out)
    full = jnp.stack([first, last], axis=2).reshape(2, NP, shard)
    pt_step = pg - step0 * sol0 - step1 * (sol1 + beta * sol0)
    return full[0], full[1], pt_step.reshape(3, tiles * BLK)


def solution(mesh):
    in_specs = (
        P(None, ("pts", "cam"), None),
        P(None, ("pts", "cam"), None),
        P(("pts", "cam"), None),
        P(("pts", "cam"), None),
        P(("pts", "cam")),
        P(("pts", "cam"), None),
        P(None, "cam"),
        P(None, "cam"),
        P(None, ("pts", "cam")),
        P(None, ("pts", "cam")),
    )
    out_specs = (P(None, "cam"), P(None, "cam"), P(None, ("pts", "cam")))
    return jax.shard_map(local, mesh=mesh, in_specs=in_specs, out_specs=out_specs, check_vma=False)
```

```python
import functools

import jax
import jax.numpy as jnp
from jax import lax
from jax.experimental import pallas as pl
from jax.experimental.pallas import tpu as pltpu
from jax.sharding import PartitionSpec as P

BLK = 128
BPT = 8
NP = 9
EXTRA = 8
F32 = jnp.float32
BF16 = jnp.bfloat16
GROUP = 64
VMEM_LIMIT = 24 * 1024 * 1024


def split3(x):
    hi = x.astype(BF16).astype(F32)
    rest = x - hi
    mid = rest.astype(BF16).astype(F32)
    return hi, mid, rest - mid


def apply_three(inverse, values):
    first = inverse[0] * values[0] + inverse[1] * values[1] + inverse[2] * values[2]
    second = inverse[1] * values[0] + inverse[3] * values[1] + inverse[4] * values[2]
    third = inverse[2] * values[0] + inverse[4] * values[1] + inverse[5] * values[2]
    return [first, second, third]


def lane_pick(table, idx):
    return jnp.take_along_axis(table, idx, axis=1, mode="promise_in_bounds")


def onehot_rows(idx_row):
    rows = lax.broadcasted_iota(jnp.int32, (BLK, BLK), 0)
    return jnp.where(rows == idx_row, 1.0, 0.0).astype(BF16)


NT = (((1,), (1,)), ((), ()))


def point_stage_rows(count):
    return -(-3 * count // 16) * 16


def cam_stage_rows(count):
    whole = count // 8 * 8
    return -(-(3 * whole + 8) // 16) * 16


def cam_sum_rows(count):
    return count // 8 * 8 + 8


def point_scatter(stage, vals, idx_ref, t, col):
    count = len(vals)
    group = vals[0].shape[0]
    high = point_stage_rows(count)
    for j, val in enumerate(vals):
        for s, piece in enumerate(split3(val)):
            row = s * count + j
            stage[row * group : (row + 1) * group, :] = piece
    tiles = group // BPT
    for u in range(0, tiles, 2):
        lhs, rhs = [], []
        for b in range(BPT):
            pair = [(u + v) * BPT + b for v in range(2)]
            lhs.append(
                jnp.concatenate([stage[pl.ds(c, high, stride=group), :] for c in pair], axis=0).astype(BF16)
            )
            rhs.append(
                jnp.concatenate([onehot_rows(idx_ref[pl.ds(t * group + c, 1), :]) for c in pair], axis=0)
            )
        res = lax.dot_general(
            jnp.concatenate(lhs, axis=1), jnp.concatenate(rhs, axis=1), NT, preferred_element_type=F32
        )
        for v in range(2):
            start = pl.multiple_of((t * tiles + u + v) * high, 16)
            col[pl.ds(start, high), :] = res[v * high : (v + 1) * high, v * BLK : (v + 1) * BLK]


def point_sums(col, count, tiles):
    high = point_stage_rows(count)
    out = []
    for j in range(count):
        pieces = [col[pl.ds(s * count + j, tiles, stride=high), :] for s in range(3)]
        out.append(pieces[0] + (pieces[1] + pieces[2]))
    return out


def cam_scatter(stage, vals, idx_ref, t, pblk):
    count = len(vals)
    whole = count // 8 * 8
    rest = count - whole
    group = vals[0].shape[0]
    high = cam_stage_rows(count)
    keep = cam_sum_rows(count)
    for k, val in enumerate(vals):
        for s, piece in enumerate(split3(val)):
            row = s * whole + k if k < whole else 3 * whole + s * rest + k - whole
            stage[row * group : (row + 1) * group, :] = piece
    for b in range(0, group, 2):
        lhs = jnp.concatenate(
            [stage[pl.ds(b + v, high, stride=group), :] for v in range(2)], axis=0
        ).astype(BF16)
        rhs = jnp.concatenate(
            [onehot_rows(idx_ref[pl.ds(t * group + b + v, 1), :]) for v in range(2)], axis=0
        )
        both = lax.dot_general(lhs, rhs, NT, preferred_element_type=F32)
        for v in range(2):
            res = both[v * high : (v + 1) * high, v * BLK : (v + 1) * BLK]
            start = pl.multiple_of((t * group + b + v) * keep, 8)
            pblk[pl.ds(start, whole), :] = (
                res[0:whole] + res[whole : 2 * whole] + res[2 * whole : 3 * whole]
            )
            pblk[pl.ds(start + whole, 8), :] = res[3 * whole : 3 * whole + 8]


def blocks_to_dense(pblk, bt_ref, count, mine_ref, other_ref):
    nblocks = bt_ref.shape[1]
    half = bt_ref.shape[0] // 2
    owners, held = mine_ref.shape[0], half // mine_ref.shape[0]
    whole = count // 8 * 8
    rest = count - whole
    keep = cam_sum_rows(count)
    for k in range(count):
        if k < whole:
            x = pblk[pl.ds(k, nblocks, stride=keep), :]
        else:
            p = [pblk[pl.ds(k + s * rest, nblocks, stride=keep), :] for s in range(3)]
            x = p[0] + (p[1] + p[2])
        rhs = jnp.concatenate(split3(x), axis=1).astype(BF16)
        res = jnp.dot(bt_ref[...], rhs, preferred_element_type=F32)
        res = res[:, :BLK] + res[:, BLK : 2 * BLK] + res[:, 2 * BLK :]
        rows = slice(k * held, (k + 1) * held)
        mine_ref[:, rows, :] = res[:half].reshape(owners, held, BLK)
        other_ref[:, rows, :] = res[half:].reshape(owners, held, BLK)


def spread_points(ref, t, group, pidx):
    tiles = group // BPT
    out = []
    for j in range(3):
        table = [
            jnp.broadcast_to(ref[j, pl.ds(t * tiles + u, 1), :], (BPT, BLK)) for u in range(tiles)
        ]
        out.append(lane_pick(jnp.concatenate(table, axis=0), pidx))
    return out


def setup_kernel(
    jac, jp, oc, op, bt, pt_grad, pt_damp, mine, other, inv_out, pg_out, stage, stage2, col, pblk
):
    nblocks = jac.shape[1]
    tiles = nblocks // BPT

    def terms(t, carry):
        rows = pl.ds(pl.multiple_of(t * GROUP, GROUP), GROUP)
        a = [jp[j, rows, :] for j in range(6)]
        vals = [
            a[p] * a[q] + a[3 + p] * a[3 + q]
            for p, q in [(0, 0), (0, 1), (0, 2), (1, 1), (1, 2), (2, 2)]
        ]
        point_scatter(stage, vals, op, t, col)
        return carry

    lax.fori_loop(0, nblocks // GROUP, terms, 0)
    entry = point_sums(col, 6, tiles)
    c00 = entry[0] + pt_damp[0]
    c01 = entry[1]
    c02 = entry[2]
    c11 = entry[3] + pt_damp[1]
    c12 = entry[4]
    c22 = entry[5] + pt_damp[2]
    a00 = c11 * c22 - c12 * c12
    a01 = c02 * c12 - c01 * c22
    a02 = c01 * c12 - c02 * c11
    a11 = c00 * c22 - c02 * c02
    a12 = c01 * c02 - c00 * c12
    a22 = c00 * c11 - c01 * c01
    recip = 1.0 / (c00 * a00 + c01 * a01 + c02 * a02)
    inv = [a * recip for a in (a00, a01, a02, a11, a12, a22)]
    for j in range(6):
        inv_out[j] = inv[j]
    pg = apply_three(inv, [pt_grad[j] for j in range(3)])
    for j in range(3):
        pg_out[j] = pg[j]

    def rhs_terms(t, carry):
        rows = pl.ds(pl.multiple_of(t * GROUP, GROUP), GROUP)
        g = spread_points(pg_out, t, GROUP, op[rows, :])
        c0 = jp[0, rows, :] * g[0] + jp[1, rows, :] * g[1] + jp[2, rows, :] * g[2]
        c1 = jp[3, rows, :] * g[0] + jp[4, rows, :] * g[1] + jp[5, rows, :] * g[2]
        vals = []
        diag = []
        for k in range(NP):
            j0 = jac[k, rows, :]
            j1 = jac[NP + k, rows, :]
            vals.append(j0 * c0 + j1 * c1)
            diag.append(j0 * j0 + j1 * j1)
        cam_scatter(stage2, vals + diag, oc, t, pblk)
        return carry

    lax.fori_loop(0, nblocks // GROUP, rhs_terms, 0)
    blocks_to_dense(pblk, bt, 2 * NP, mine, other)


def setup_call(jac, jp, oc, op, bt, pt_grad, pt_damp, owners):
    nblocks = jac.shape[1]
    tiles = nblocks // BPT
    held = bt.shape[0] // 2 // owners
    msg = jax.ShapeDtypeStruct((owners, 2 * NP * held, BLK), F32)
    return pl.pallas_call(
        setup_kernel,
        out_shape=[
            msg,
            msg,
            jax.ShapeDtypeStruct((6, tiles, BLK), F32),
            jax.ShapeDtypeStruct((3, tiles, BLK), F32),
        ],
        scratch_shapes=[
            pltpu.VMEM((point_stage_rows(6) * GROUP, BLK), F32),
            pltpu.VMEM((cam_stage_rows(2 * NP) * GROUP, BLK), F32),
            pltpu.VMEM((tiles * point_stage_rows(6), BLK), F32),
            pltpu.VMEM((nblocks * cam_sum_rows(2 * NP), BLK), F32),
        ],
        compiler_params=pltpu.CompilerParams(vmem_limit_bytes=VMEM_LIMIT),
        name="setup_pass",
    )(jac, jp, oc, op, bt, pt_grad, pt_damp)


def operator_kernel(second, *refs):
    if second:
        (jac, jp, oc, op, b_mat, bt, inv, mine_in, other_in, proj_in, scal_in, own,
         mine, other, sol_out, proj, stage, stage2, pick, col, pblk) = refs
    else:
        (jac, jp, oc, op, b_mat, bt, inv, mine_in, other_in,
         mine, other, sol_out, proj, stage, stage2, pick, col, pblk) = refs
    nblocks = jac.shape[1]
    tiles = nblocks // BPT
    owners = mine_in.shape[0]
    held = b_mat.shape[1] // 2 // owners
    half = owners * held
    for k in range(NP):
        rows = slice(k * held, (k + 1) * held)
        x = jnp.concatenate(
            [mine_in[:, rows, :].reshape(half, BLK), other_in[:, rows, :].reshape(half, BLK)], axis=0
        )
        rhs = jnp.concatenate(split3(x), axis=1).astype(BF16)
        res = jnp.dot(b_mat[...], rhs, preferred_element_type=F32)
        pick[k] = res[:, :BLK] + res[:, BLK : 2 * BLK] + res[:, 2 * BLK :]
    if second:
        step_len = scal_in[0]

    def project(t, carry):
        rows = pl.ds(pl.multiple_of(t * GROUP, GROUP), GROUP)
        cidx = oc[rows, :]
        p0 = jnp.zeros((GROUP, BLK), F32)
        p1 = jnp.zeros((GROUP, BLK), F32)
        for k in range(NP):
            v = lane_pick(pick[k, rows, :], cidx)
            p0 += jac[k, rows, :] * v
            p1 += jac[NP + k, rows, :] * v
        if second:
            p0 = proj_in[0, rows, :] - step_len * p0
            p1 = proj_in[1, rows, :] - step_len * p1
        proj[0, rows, :] = p0
        proj[1, rows, :] = p1
        vals = [jp[j, rows, :] * p0 + jp[3 + j, rows, :] * p1 for j in range(3)]
        point_scatter(stage, vals, op, t, col)
        return carry

    lax.fori_loop(0, nblocks // GROUP, project, 0)
    sol = apply_three([inv[j] for j in range(6)], point_sums(col, 3, tiles))
    for j in range(3):
        sol_out[j] = sol[j]

    def correct(t, carry):
        rows = pl.ds(pl.multiple_of(t * GROUP, GROUP), GROUP)
        g = spread_points(sol_out, t, GROUP, op[rows, :])
        p0 = proj[0, rows, :]
        p1 = proj[1, rows, :]
        c0 = p0 - (jp[0, rows, :] * g[0] + jp[1, rows, :] * g[1] + jp[2, rows, :] * g[2])
        c1 = p1 - (jp[3, rows, :] * g[0] + jp[4, rows, :] * g[1] + jp[5, rows, :] * g[2])
        if second:
            zz, zd = carry
            zz = zz + (p0 * c0 + p1 * c1)
            zd = zd + (proj_in[0, rows, :] * c0 + proj_in[1, rows, :] * c1)
            carry = (zz, zd)
        vals = [jac[k, rows, :] * c0 + jac[NP + k, rows, :] * c1 for k in range(NP)]
        cam_scatter(stage2, vals, oc, t, pblk)
        return carry

    zero = jnp.zeros((GROUP, BLK), F32)
    sums = lax.fori_loop(0, nblocks // GROUP, correct, (zero, zero) if second else 0)
    blocks_to_dense(pblk, bt, NP, mine, other)
    if second:
        sub = lax.broadcasted_iota(jnp.int32, (EXTRA, BLK), 0)
        row0 = jnp.sum(sums[0], axis=0, keepdims=True)
        row1 = jnp.sum(sums[1], axis=0, keepdims=True)
        extra = jnp.where(sub == 0, row0, jnp.where(sub == 1, row1, own[...]))
        extra = jnp.broadcast_to(extra[None], (owners, EXTRA, BLK))
        mine[:, NP * held :, :] = extra
        other[:, NP * held :, :] = extra


def operator_call(jac, jp, oc, op, b_mat, bt, inv, mine, other, later=None):
    nblocks = jac.shape[1]
    tiles = nblocks // BPT
    owners = mine.shape[0]
    held = bt.shape[0] // 2 // owners
    rows = NP * held + (EXTRA if later else 0)
    msg = jax.ShapeDtypeStruct((owners, rows, BLK), F32)
    operands = [jac, jp, oc, op, b_mat, bt, inv, mine, other]
    vmem = pl.BlockSpec(memory_space=pltpu.VMEM)
    in_specs = [vmem] * len(operands)
    if later:
        operands += list(later)
        in_specs += [vmem, pl.BlockSpec(memory_space=pltpu.SMEM), vmem]
    return pl.pallas_call(
        functools.partial(operator_kernel, bool(later)),
        in_specs=in_specs,
        out_shape=[
            msg,
            msg,
            jax.ShapeDtypeStruct((3, tiles, BLK), F32),
            jax.ShapeDtypeStruct((2, nblocks, BLK), F32),
        ],
        scratch_shapes=[
            pltpu.VMEM((point_stage_rows(3) * GROUP, BLK), F32),
            pltpu.VMEM((cam_stage_rows(NP) * GROUP, BLK), F32),
            pltpu.VMEM((NP, nblocks, BLK), F32),
            pltpu.VMEM((tiles * point_stage_rows(3), BLK), F32),
            pltpu.VMEM((nblocks * cam_sum_rows(NP), BLK), F32),
        ],
        compiler_params=pltpu.CompilerParams(vmem_limit_bytes=VMEM_LIMIT),
        name="second_pass" if later else "first_pass",
    )(*operands)


def local(jac, jp, oc, op, entry, cov, cam_grad, cam_damp, pt_grad, pt_damp):
    owners = lax.axis_size("cam")
    pts = lax.axis_size("pts")
    core = lax.axis_index("pts") % 2
    per_owner = cov.shape[1]
    nblocks = oc.shape[0]
    tiles = nblocks // BPT
    shard = cam_grad.shape[1]
    held = shard // BLK // 2
    half = owners * held

    owner = entry // per_owner
    local_block = cov[owner, entry % per_owner]
    place = ((local_block // held) ^ core) * half + owner * held + local_block % held
    places = jnp.arange(2 * half, dtype=jnp.int32)
    b_mat = (place[:, None] == places[None, :]).astype(BF16)
    bt = (places[:, None] == place[None, :]).astype(BF16)

    swap = [(i, i ^ 1) for i in range(pts)]

    def exchange(x):
        return lax.ppermute(x, "pts", swap)

    def own_half(x):
        shaped = x.reshape(NP, 2, held, BLK)
        return lax.dynamic_index_in_dim(shaped, core, 1, keepdims=False)

    def reduce_sum(mine, other):
        both = mine + exchange(other)
        got = lax.all_to_all(both, "cam", 0, 0, tiled=False).sum(axis=0)
        total = got
        for shift in range(2, pts, 2):
            total = total + lax.ppermute(got, "pts", [(i, (i + shift) % pts) for i in range(pts)])
        return total

    def spread(values, scalar):
        row = jnp.sum(scalar, axis=(0, 1)).reshape(1, BLK)
        chunk = jnp.concatenate(
            [values.reshape(NP * held, BLK), row, jnp.zeros((EXTRA - 1, BLK), F32)], axis=0
        )
        mine = lax.all_to_all(
            jnp.broadcast_to(chunk[None], (owners,) + chunk.shape), "cam", 0, 0, tiled=False
        )
        other = exchange(mine)
        return mine, other, jnp.sum(mine[:, NP * held] + other[:, NP * held])

    mine, other, inv, pg = setup_call(
        jac, jp, oc, op, bt, pt_grad.reshape(3, tiles, BLK), pt_damp.reshape(3, tiles, BLK), owners
    )
    setup = reduce_sum(mine, other).reshape(2, NP, held, BLK)
    damp = own_half(cam_damp)
    rhs = own_half(cam_grad) - setup[0]
    precond = damp + setup[1]
    direction = rhs / precond
    mine, other, norm0 = spread(direction, rhs * direction)
    mine, other, sol0, proj0 = operator_call(jac, jp, oc, op, b_mat, bt, inv, mine, other)
    image0 = damp * direction + reduce_sum(mine, other).reshape(NP, held, BLK)
    scaled = image0 / precond
    mine, other, curvature0 = spread(scaled, direction * image0)
    step0 = norm0 / curvature0
    resid1 = rhs - step0 * image0
    z1 = resid1 / precond
    share = 2.0 / pts

    def lanes(x):
        return jnp.sum(x, axis=(0, 1)).reshape(1, BLK) * share

    own = jnp.concatenate(
        [
            jnp.zeros((2, BLK), F32),
            lanes(resid1 * z1),
            lanes(damp * z1 * z1),
            lanes(damp * z1 * direction),
            jnp.zeros((EXTRA - 5, BLK), F32),
        ],
        axis=0,
    )
    mine, other, sol1, _ = operator_call(
        jac, jp, oc, op, b_mat, bt, inv, mine, other, (proj0, step0.reshape(1), own)
    )
    got = reduce_sum(mine, other)
    image_z = damp * z1 + got[: NP * held].reshape(NP, held, BLK)
    sums = jnp.sum(got[NP * held :], axis=1)
    norm1 = sums[2]
    beta = norm1 / norm0
    curvature1 = (sums[0] + sums[3]) + 2.0 * beta * (sums[1] + sums[4]) + beta * beta * curvature0
    step1 = norm1 / curvature1
    direction1 = z1 + beta * direction
    image1 = image_z + beta * image0
    out = jnp.stack([step0 * direction + step1 * direction1, resid1 - step1 * image1])
    theirs = exchange(out)
    first = jnp.where(core == 0, out, theirs)
    last = jnp.where(core == 0, theirs, out)
    full = jnp.stack([first, last], axis=2).reshape(2, NP, shard)
    pt_step = pg - step0 * sol0 - step1 * (sol1 + beta * sol0)
    return full[0], full[1], pt_step.reshape(3, tiles * BLK)


def solution(mesh):
    in_specs = (
        P(None, ("pts", "cam"), None),
        P(None, ("pts", "cam"), None),
        P(("pts", "cam"), None),
        P(("pts", "cam"), None),
        P(("pts", "cam")),
        P(("pts", "cam"), None),
        P(None, "cam"),
        P(None, "cam"),
        P(None, ("pts", "cam")),
        P(None, ("pts", "cam")),
    )
    out_specs = (P(None, "cam"), P(None, "cam"), P(None, ("pts", "cam")))
    return jax.shard_map(local, mesh=mesh, in_specs=in_specs, out_specs=out_specs, check_vma=False)
```

```python
import functools

import jax
import jax.numpy as jnp
from jax import lax
from jax.experimental import pallas as pl
from jax.experimental.pallas import tpu as pltpu
from jax.sharding import Mesh, PartitionSpec as P

BLK = 128
BPT = 8
NP = 9
EXTRA = 4
F32 = jnp.float32
BF16 = jnp.bfloat16
GROUP = 64
VMEM_LIMIT = 24 * 1024 * 1024


def split3(x):
    hi = x.astype(BF16).astype(F32)
    rest = x - hi
    mid = rest.astype(BF16).astype(F32)
    return hi, mid, rest - mid


def apply_three(inverse, values):
    first = inverse[0] * values[0] + inverse[1] * values[1] + inverse[2] * values[2]
    second = inverse[1] * values[0] + inverse[3] * values[1] + inverse[4] * values[2]
    third = inverse[2] * values[0] + inverse[4] * values[1] + inverse[5] * values[2]
    return [first, second, third]


def lane_pick(table, idx):
    return jnp.take_along_axis(table, idx, axis=1, mode="promise_in_bounds")


def onehot_rows(idx_row):
    rows = lax.broadcasted_iota(jnp.int32, (BLK, BLK), 0)
    return jnp.where(rows == idx_row, 1.0, 0.0).astype(BF16)


NT = (((1,), (1,)), ((), ()))


def point_stage_rows(count):
    return -(-3 * count // 16) * 16


def cam_stage_rows(count):
    whole = count // 8 * 8
    return -(-(3 * whole + 8) // 16) * 16


def cam_sum_rows(count):
    return count // 8 * 8 + 8


def point_scatter(stage, vals, idx_ref, t, col):
    count = len(vals)
    group = vals[0].shape[0]
    high = point_stage_rows(count)
    for j, val in enumerate(vals):
        for s, piece in enumerate(split3(val)):
            row = s * count + j
            stage[row * group : (row + 1) * group, :] = piece
    tiles = group // BPT
    for u in range(0, tiles, 2):
        lhs, rhs = [], []
        for b in range(BPT):
            pair = [(u + v) * BPT + b for v in range(2)]
            lhs.append(
                jnp.concatenate([stage[pl.ds(c, high, stride=group), :] for c in pair], axis=0).astype(BF16)
            )
            rhs.append(
                jnp.concatenate([onehot_rows(idx_ref[pl.ds(t * group + c, 1), :]) for c in pair], axis=0)
            )
        res = lax.dot_general(
            jnp.concatenate(lhs, axis=1), jnp.concatenate(rhs, axis=1), NT, preferred_element_type=F32
        )
        for v in range(2):
            start = pl.multiple_of((t * tiles + u + v) * high, 16)
            col[pl.ds(start, high), :] = res[v * high : (v + 1) * high, v * BLK : (v + 1) * BLK]


def point_sums(col, count, tiles):
    high = point_stage_rows(count)
    out = []
    for j in range(count):
        pieces = [col[pl.ds(s * count + j, tiles, stride=high), :] for s in range(3)]
        out.append(pieces[0] + (pieces[1] + pieces[2]))
    return out


def cam_scatter(stage, vals, idx_ref, t, pblk):
    count = len(vals)
    whole = count // 8 * 8
    rest = count - whole
    group = vals[0].shape[0]
    high = cam_stage_rows(count)
    keep = cam_sum_rows(count)
    for k, val in enumerate(vals):
        for s, piece in enumerate(split3(val)):
            row = s * whole + k if k < whole else 3 * whole + s * rest + k - whole
            stage[row * group : (row + 1) * group, :] = piece
    for b in range(0, group, 2):
        lhs = jnp.concatenate(
            [stage[pl.ds(b + v, high, stride=group), :] for v in range(2)], axis=0
        ).astype(BF16)
        rhs = jnp.concatenate(
            [onehot_rows(idx_ref[pl.ds(t * group + b + v, 1), :]) for v in range(2)], axis=0
        )
        both = lax.dot_general(lhs, rhs, NT, preferred_element_type=F32)
        for v in range(2):
            res = both[v * high : (v + 1) * high, v * BLK : (v + 1) * BLK]
            start = pl.multiple_of((t * group + b + v) * keep, 8)
            pblk[pl.ds(start, whole), :] = (
                res[0:whole] + res[whole : 2 * whole] + res[2 * whole : 3 * whole]
            )
            pblk[pl.ds(start + whole, 8), :] = res[3 * whole : 3 * whole + 8]


def blocks_to_dense(pblk, bt_ref, count, mine_ref, other_ref, peers, stride):
    nblocks = bt_ref.shape[1]
    half = bt_ref.shape[0] // 2
    quarter = half // peers
    whole = count // 8 * 8
    rest = count - whole
    keep = cam_sum_rows(count)
    for k in range(count):
        if k < whole:
            x = pblk[pl.ds(k, nblocks, stride=keep), :]
        else:
            p = [pblk[pl.ds(k + s * rest, nblocks, stride=keep), :] for s in range(3)]
            x = p[0] + (p[1] + p[2])
        rhs = jnp.concatenate(split3(x), axis=1).astype(BF16)
        res = jnp.dot(bt_ref[...], rhs, preferred_element_type=F32)
        res = res[:, :BLK] + res[:, BLK : 2 * BLK] + res[:, 2 * BLK :]
        for i in range(quarter):
            rows = pl.ds(k * quarter + i, peers, stride=stride)
            mine_ref[rows, :] = res[i * peers : (i + 1) * peers]
            other_ref[rows, :] = res[half + i * peers : half + (i + 1) * peers]


def fill_extra(mine_ref, other_ref, rows, peers, stride):
    first = stride - EXTRA
    for i in range(EXTRA):
        row = rows[i] if i < len(rows) else jnp.zeros((1, BLK), F32)
        full = jnp.broadcast_to(row, (peers, BLK))
        mine_ref[pl.ds(first + i, peers, stride=stride), :] = full
        other_ref[pl.ds(first + i, peers, stride=stride), :] = full


def extra_sum(refs, index, peers, stride):
    first = stride - EXTRA
    rows = [jnp.sum(r[pl.ds(first + index, peers, stride=stride), :], axis=0, keepdims=True) for r in refs]
    return jnp.sum(functools.reduce(jnp.add, rows), axis=1, keepdims=True)


def spread_points(ref, t, group, pidx):
    tiles = group // BPT
    out = []
    for j in range(3):
        table = [
            jnp.broadcast_to(ref[j, pl.ds(t * tiles + u, 1), :], (BPT, BLK)) for u in range(tiles)
        ]
        out.append(lane_pick(jnp.concatenate(table, axis=0), pidx))
    return out


def setup_kernel(
    peers, jac, jp, oc, op, bt, pt_grad, pt_damp, mine, other, inv_out, pg_out,
    stage, stage2, col, pblk, grad_rows, damp_rows
):
    nblocks = jac.shape[1]
    tiles = nblocks // BPT
    for t in range(tiles):
        lanes = slice(t * BLK, (t + 1) * BLK)
        grad_rows[pl.ds(t, 3, stride=tiles), :] = pt_grad[:, lanes]
        damp_rows[pl.ds(t, 3, stride=tiles), :] = pt_damp[:, lanes]
    grad = [grad_rows[j * tiles : (j + 1) * tiles, :] for j in range(3)]
    damp = [damp_rows[j * tiles : (j + 1) * tiles, :] for j in range(3)]

    def terms(t, carry):
        rows = pl.ds(pl.multiple_of(t * GROUP, GROUP), GROUP)
        a = [jp[j, rows, :] for j in range(6)]
        vals = [
            a[p] * a[q] + a[3 + p] * a[3 + q]
            for p, q in [(0, 0), (0, 1), (0, 2), (1, 1), (1, 2), (2, 2)]
        ]
        point_scatter(stage, vals, op, t, col)
        return carry

    lax.fori_loop(0, nblocks // GROUP, terms, 0)
    entry = point_sums(col, 6, tiles)
    c00 = entry[0] + damp[0]
    c01 = entry[1]
    c02 = entry[2]
    c11 = entry[3] + damp[1]
    c12 = entry[4]
    c22 = entry[5] + damp[2]
    a00 = c11 * c22 - c12 * c12
    a01 = c02 * c12 - c01 * c22
    a02 = c01 * c12 - c02 * c11
    a11 = c00 * c22 - c02 * c02
    a12 = c01 * c02 - c00 * c12
    a22 = c00 * c11 - c01 * c01
    recip = 1.0 / (c00 * a00 + c01 * a01 + c02 * a02)
    inv = [a * recip for a in (a00, a01, a02, a11, a12, a22)]
    for j in range(6):
        inv_out[j] = inv[j]
    pg = apply_three(inv, grad)
    for j in range(3):
        pg_out[j] = pg[j]

    def rhs_terms(t, carry):
        rows = pl.ds(pl.multiple_of(t * GROUP, GROUP), GROUP)
        g = spread_points(pg_out, t, GROUP, op[rows, :])
        c0 = jp[0, rows, :] * g[0] + jp[1, rows, :] * g[1] + jp[2, rows, :] * g[2]
        c1 = jp[3, rows, :] * g[0] + jp[4, rows, :] * g[1] + jp[5, rows, :] * g[2]
        vals = []
        diag = []
        for k in range(NP):
            j0 = jac[k, rows, :]
            j1 = jac[NP + k, rows, :]
            vals.append(j0 * c0 + j1 * c1)
            diag.append(j0 * j0 + j1 * j1)
        cam_scatter(stage2, vals + diag, oc, t, pblk)
        return carry

    lax.fori_loop(0, nblocks // GROUP, rhs_terms, 0)
    blocks_to_dense(pblk, bt, 2 * NP, mine, other, peers, mine.shape[0] // peers)


def call(kernel, name, out_shape, operands, scratch=(), smem=()):
    specs = [
        pl.BlockSpec(memory_space=pltpu.SMEM if i in smem else pltpu.VMEM)
        for i in range(len(operands))
    ]
    return pl.pallas_call(
        kernel,
        in_specs=specs,
        out_shape=out_shape,
        scratch_shapes=scratch,
        compiler_params=pltpu.CompilerParams(vmem_limit_bytes=VMEM_LIMIT),
        name=name,
    )(*operands)


def shape_of(*dims):
    return jax.ShapeDtypeStruct(dims, F32)


def setup_call(jac, jp, oc, op, bt, pt_grad, pt_damp, peers):
    nblocks = jac.shape[1]
    tiles = nblocks // BPT
    msg = shape_of(NP * bt.shape[0], BLK)
    return call(
        functools.partial(setup_kernel, peers),
        "setup_pass",
        [msg, msg, shape_of(6, tiles, BLK), shape_of(3, tiles, BLK)],
        (jac, jp, oc, op, bt, pt_grad, pt_damp),
        [
            pltpu.VMEM((point_stage_rows(6) * GROUP, BLK), F32),
            pltpu.VMEM((cam_stage_rows(2 * NP) * GROUP, BLK), F32),
            pltpu.VMEM((tiles * point_stage_rows(6), BLK), F32),
            pltpu.VMEM((nblocks * cam_sum_rows(2 * NP), BLK), F32),
            pltpu.VMEM((3 * tiles, BLK), F32),
            pltpu.VMEM((3 * tiles, BLK), F32),
        ],
    )


def operator_kernel(second, peers, owners, *refs):
    if second:
        (pos, jac, jp, oc, op, b_mat, bt, inv, mine_in, other_in, proj_in, state, image, norm_in,
         mine, other, sol_out, held_out, scal_out, stage, stage2, pick, col, pblk, proj) = refs
    else:
        (pos, jac, jp, oc, op, b_mat, bt, inv, mine_in, other_in,
         mine, other, sol_out, held_out, scal_out, proj, stage, stage2, pick, col, pblk) = refs
    nblocks = jac.shape[1]
    tiles = nblocks // BPT
    stride = mine_in.shape[0] // peers
    quarter = (stride - EXTRA) // NP
    for k in range(NP):
        x = jnp.concatenate(
            [
                ref[pl.ds(k * quarter + i, peers, stride=stride), :]
                for ref in (mine_in, other_in)
                for i in range(quarter)
            ],
            axis=0,
        )
        rhs = jnp.concatenate(split3(x), axis=1).astype(BF16)
        res = jnp.dot(b_mat[...], rhs, preferred_element_type=F32)
        pick[k] = res[:, :BLK] + res[:, BLK : 2 * BLK] + res[:, 2 * BLK :]
    for h, ref in enumerate((mine_in, other_in)):
        for x in range(peers // owners):
            start = pl.multiple_of((x * owners + pos[2]) * stride, 8)
            held_out[h, x] = ref[pl.ds(start, stride), :]
    total = extra_sum((mine_in, other_in), 0, peers, stride)
    if second:
        norm = norm_in[0:1, 0:1]
        step_len = norm / total
        scal_out[...] = jnp.broadcast_to(total, (8, BLK))
        rhs, precond, damp, direction = (state[i] for i in range(4))
        resid = rhs - step_len * image[...]
        z = resid / precond
        keep = lax.broadcasted_iota(jnp.int32, (stride, BLK), 0) < stride - EXTRA

        def lanes(v):
            return jnp.sum(jnp.where(keep, v, 0.0), axis=0, keepdims=True)

        owner_sums = [lanes(damp * z * z), lanes(damp * z * direction), lanes(resid * z)]
    else:
        scal_out[...] = jnp.broadcast_to(total, (8, BLK))

    def project(t, carry):
        rows = pl.ds(pl.multiple_of(t * GROUP, GROUP), GROUP)
        cidx = oc[rows, :]
        p0 = jnp.zeros((GROUP, BLK), F32)
        p1 = jnp.zeros((GROUP, BLK), F32)
        for k in range(NP):
            v = lane_pick(pick[k, rows, :], cidx)
            p0 += jac[k, rows, :] * v
            p1 += jac[NP + k, rows, :] * v
        if second:
            p0 = proj_in[0, rows, :] - step_len * p0
            p1 = proj_in[1, rows, :] - step_len * p1
        proj[0, rows, :] = p0
        proj[1, rows, :] = p1
        vals = [jp[j, rows, :] * p0 + jp[3 + j, rows, :] * p1 for j in range(3)]
        point_scatter(stage, vals, op, t, col)
        return carry

    lax.fori_loop(0, nblocks // GROUP, project, 0)
    sol = apply_three([inv[j] for j in range(6)], point_sums(col, 3, tiles))
    for j in range(3):
        sol_out[j] = sol[j]

    def correct(t, carry):
        rows = pl.ds(pl.multiple_of(t * GROUP, GROUP), GROUP)
        g = spread_points(sol_out, t, GROUP, op[rows, :])
        p0 = proj[0, rows, :]
        p1 = proj[1, rows, :]
        c0 = p0 - (jp[0, rows, :] * g[0] + jp[1, rows, :] * g[1] + jp[2, rows, :] * g[2])
        c1 = p1 - (jp[3, rows, :] * g[0] + jp[4, rows, :] * g[1] + jp[5, rows, :] * g[2])
        if second:
            zz, zd = carry
            zz = zz + (p0 * c0 + p1 * c1)
            zd = zd + (proj_in[0, rows, :] * c0 + proj_in[1, rows, :] * c1)
            carry = (zz, zd)
        vals = [jac[k, rows, :] * c0 + jac[NP + k, rows, :] * c1 for k in range(NP)]
        cam_scatter(stage2, vals, oc, t, pblk)
        return carry

    zero = jnp.zeros((GROUP, BLK), F32)
    sums = lax.fori_loop(0, nblocks // GROUP, correct, (zero, zero) if second else 0)
    blocks_to_dense(pblk, bt, NP, mine, other, peers, stride)
    rows = []
    if second:
        rows = [
            jnp.sum(sums[0], axis=0, keepdims=True) + owner_sums[0],
            jnp.sum(sums[1], axis=0, keepdims=True) + owner_sums[1],
            owner_sums[2],
        ]
    fill_extra(mine, other, rows, peers, stride)


def operator_call(pos, jac, jp, oc, op, b_mat, bt, inv, mine, other, peers, owners, later=()):
    nblocks = jac.shape[1]
    tiles = nblocks // BPT
    stride = mine.shape[0] // peers
    proj = [] if later else [shape_of(2, nblocks, BLK)]
    proj_scratch = [pltpu.VMEM((2, nblocks, BLK), F32)] if later else []
    return call(
        functools.partial(operator_kernel, bool(later), peers, owners),
        "second_pass" if later else "first_pass",
        [
            shape_of(*mine.shape),
            shape_of(*mine.shape),
            shape_of(3, tiles, BLK),
            shape_of(2, peers // owners, stride, BLK),
            shape_of(8, BLK),
        ]
        + proj,
        (pos, jac, jp, oc, op, b_mat, bt, inv, mine, other) + later,
        [
            pltpu.VMEM((point_stage_rows(3) * GROUP, BLK), F32),
            pltpu.VMEM((cam_stage_rows(NP) * GROUP, BLK), F32),
            pltpu.VMEM((NP, nblocks, BLK), F32),
            pltpu.VMEM((tiles * point_stage_rows(3), BLK), F32),
            pltpu.VMEM((nblocks * cam_sum_rows(NP), BLK), F32),
        ]
        + proj_scratch,
        smem=(0,),
    )


def message_sum(got, peers):
    stride = got.shape[0] // peers
    total = got[0:stride, :]
    for d in range(1, peers):
        total = total + got[d * stride : (d + 1) * stride, :]
    return total


def send_all(msg, values, scalar, peers):
    stride = values.shape[0]
    data = stride - EXTRA
    row = lax.broadcasted_iota(jnp.int32, values.shape, 0)
    lanes = jnp.sum(jnp.where(row < data, scalar, 0.0), axis=0, keepdims=True)
    out = jnp.where(row < data, values, jnp.where(row == data, lanes, 0.0))
    for d in range(peers):
        msg[d * stride : (d + 1) * stride, :] = out


def start_kernel(peers, quarter, pos, got, grad, damp, msg, state, rows):
    data = NP * quarter
    rows[...] = jnp.ones(rows.shape, F32)
    for i in range(quarter):
        lanes = pl.ds(pl.multiple_of((pos[1] * quarter + i) * BLK, BLK), BLK)
        rows[0, pl.ds(i, NP, stride=quarter), :] = grad[:, lanes]
        rows[1, pl.ds(i, NP, stride=quarter), :] = damp[:, lanes]
    total = message_sum(got, peers)
    ones = jnp.ones((EXTRA, BLK), F32)
    rhs = rows[0] - jnp.concatenate([total[:data], ones], axis=0)
    precond = rows[1] + jnp.concatenate([total[data:], ones], axis=0)
    direction = rhs / precond
    state[0] = rhs
    state[1] = precond
    state[2] = rows[1]
    state[3] = direction
    send_all(msg, direction, rhs * direction, peers)


def image_kernel(peers, got, state, msg, image):
    direction = state[3]
    value = state[2] * direction + message_sum(got, peers)
    image[...] = value
    send_all(msg, value / state[1], direction * value, peers)


def last_kernel(peers, got, state, image, norm_in, curv_in, resid_out, scal_out):
    norm = norm_in[0:1, 0:1]
    curv = curv_in[0:1, 0:1]
    step0 = norm / curv
    total = message_sum(got, peers)
    stride = total.shape[0]
    sums = jnp.sum(total[stride - EXTRA :], axis=1, keepdims=True)
    zz, zd, norm1 = (sums[i : i + 1] for i in range(3))
    beta = norm1 / norm
    curv1 = zz + 2.0 * beta * zd + beta * beta * curv
    step1 = norm1 / curv1
    resid = state[0] - step0 * image[...]
    z = resid / state[1]
    image1 = (state[2] * z + total) + beta * image[...]
    resid_out[...] = resid - step1 * image1
    for i, s in enumerate((step0, step1, beta)):
        scal_out[i * 8 : (i + 1) * 8, :] = jnp.broadcast_to(s, (8, BLK))


def step_kernel(pos, scal, held0, held1, pg, sol0, sol1, cam_out, pt_out, pts_rows, cams_rows):
    step0, step1, beta = (scal[i * 8 : i * 8 + 1, 0:1] for i in range(3))
    tiles = pg.shape[1]
    for j in range(3):
        first = sol0[j]
        pts_rows[j * tiles : (j + 1) * tiles, :] = (
            pg[j] - step0 * first - step1 * (sol1[j] + beta * first)
        )
    for t in range(tiles):
        pt_out[:, t * BLK : (t + 1) * BLK] = pts_rows[pl.ds(t, 3, stride=tiles), :]
    quarters, stride = held0.shape[1], held0.shape[2]
    quarter = (stride - EXTRA) // NP
    for h in range(2):
        for x in range(quarters):
            d0 = held0[h, x]
            z = d0 - step0 * held1[h, x]
            cams_rows[...] = step0 * d0 + step1 * (z + beta * d0)
            put_cams(cam_out, cams_rows, pos[0] ^ h, x, quarters, quarter)


def put_cams(out, rows, core, x, quarters, quarter):
    for i in range(quarter):
        block = (core * quarters + x) * quarter + i
        lanes = pl.ds(pl.multiple_of(block * BLK, BLK), BLK)
        out[:, lanes] = rows[pl.ds(i, NP, stride=quarter), :]


def resid_kernel(pos, pieces, out, rows):
    quarters, stride = pieces.shape[1], pieces.shape[2]
    quarter = (stride - EXTRA) // NP
    for h in range(2):
        for s in range(quarters):
            x = (pos[3] + quarters - s) % quarters
            rows[...] = pieces[h, s]
            put_cams(out, rows, pos[0] ^ h, x, quarters, quarter)


def local(jac, jp, oc, op, entry, cov, cam_grad, cam_damp, pt_grad, pt_damp):
    quarters = lax.axis_size("x")
    owners = lax.axis_size("z") * lax.axis_size("y")
    peers = quarters * owners
    core = lax.axis_index("core")
    x = lax.axis_index("x")
    owner_here = lax.axis_index(("z", "y"))
    pos = jnp.stack([core, core * quarters + x, owner_here, x]).astype(jnp.int32)
    per_owner = cov.shape[1]
    shard = cam_grad.shape[1]
    quarter = shard // BLK // 2 // quarters
    half = peers * quarter

    slots = jnp.arange(cov.size, dtype=jnp.int32)
    local_block = jnp.sum(
        jnp.where(entry[:, None] == slots[None, :], cov.reshape(-1)[None, :], 0), axis=1
    )
    core_of = local_block // (quarters * quarter)
    x_of = local_block // quarter % quarters
    place = (
        (core_of ^ core) * half
        + (local_block % quarter) * peers
        + x_of * owners
        + entry // per_owner
    )
    places = jnp.arange(2 * half, dtype=jnp.int32)
    b_mat = (place[:, None] == places[None, :]).astype(BF16)
    bt = (places[:, None] == place[None, :]).astype(BF16)

    def exchange(v):
        return lax.ppermute(v, "core", [(0, 1), (1, 0)])

    def to_peers(v):
        shaped = v.reshape(peers, -1, BLK)
        return lax.all_to_all(shaped, ("x", "z", "y"), 0, 0, tiled=False).reshape(-1, BLK)

    stride = NP * quarter + EXTRA
    msg = shape_of(peers * stride, BLK)
    mine, other, inv, pg = setup_call(jac, jp, oc, op, bt, pt_grad, pt_damp, peers)
    got = to_peers(mine + exchange(other))
    msg_out, state = call(
        functools.partial(start_kernel, peers, quarter),
        "start_step",
        [msg, shape_of(4, stride, BLK)],
        (pos, got, cam_grad, cam_damp),
        [pltpu.VMEM((2, stride, BLK), F32)],
        smem=(0,),
    )
    mine = to_peers(msg_out)
    other = exchange(mine)
    mine, other, sol0, held0, norm, proj0 = operator_call(
        pos, jac, jp, oc, op, b_mat, bt, inv, mine, other, peers, owners
    )
    got = to_peers(mine + exchange(other))
    msg_out, image = call(
        functools.partial(image_kernel, peers), "image_step", [msg, shape_of(stride, BLK)], (got, state)
    )
    mine = to_peers(msg_out)
    other = exchange(mine)
    mine, other, sol1, held1, curv = operator_call(
        pos, jac, jp, oc, op, b_mat, bt, inv, mine, other, peers, owners, (proj0, state, image, norm)
    )
    got = to_peers(mine + exchange(other))
    resid, scal = call(
        functools.partial(last_kernel, peers),
        "last_step",
        [shape_of(stride, BLK), shape_of(24, BLK)],
        (got, state, image, norm, curv),
    )
    pieces = [resid] + [
        lax.ppermute(resid, "x", [(i, (i + s) % quarters) for i in range(quarters)])
        for s in range(1, quarters)
    ]
    cam_step, pt_step = call(
        step_kernel,
        "result_step",
        [shape_of(NP, shard), shape_of(3, pt_grad.shape[1])],
        (pos, scal, held0, held1, pg, sol0, sol1),
        [pltpu.VMEM((3 * pg.shape[1], BLK), F32), pltpu.VMEM((stride, BLK), F32)],
        smem=(0,),
    )
    row = jnp.stack(pieces)
    cam_resid = call(
        resid_kernel,
        "result_resid",
        shape_of(NP, shard),
        (pos, jnp.stack([row, exchange(row)])),
        [pltpu.VMEM((stride, BLK), F32)],
        smem=(0,),
    )
    return cam_step, cam_resid, pt_step


def solution(mesh):
    fine = Mesh(mesh.devices.reshape(4, 2, 4, 4), ("x", "core", "z", "y"))
    pts, cam = ("x", "core"), ("z", "y")
    every = pts + cam
    in_specs = (
        P(None, every, None),
        P(None, every, None),
        P(every, None),
        P(every, None),
        P(every),
        P(every, None),
        P(None, cam),
        P(None, cam),
        P(None, every),
        P(None, every),
    )
    out_specs = (P(None, cam), P(None, cam), P(None, every))
    return jax.shard_map(local, mesh=fine, in_specs=in_specs, out_specs=out_specs, check_vma=False)
```

```python
import functools

import jax
import jax.numpy as jnp
from jax import lax
from jax.experimental import pallas as pl
from jax.experimental.pallas import tpu as pltpu
from jax.sharding import Mesh, PartitionSpec as P

BLK = 128
BPT = 8
NP = 9
EXTRA = 8
F32 = jnp.float32
BF16 = jnp.bfloat16
GROUP = 64
VMEM_LIMIT = 24 * 1024 * 1024


def split3(x):
    hi = x.astype(BF16).astype(F32)
    rest = x - hi
    mid = rest.astype(BF16).astype(F32)
    return hi, mid, rest - mid


def apply_three(inverse, values):
    first = inverse[0] * values[0] + inverse[1] * values[1] + inverse[2] * values[2]
    second = inverse[1] * values[0] + inverse[3] * values[1] + inverse[4] * values[2]
    third = inverse[2] * values[0] + inverse[4] * values[1] + inverse[5] * values[2]
    return [first, second, third]


def lane_pick(table, idx):
    return jnp.take_along_axis(table, idx, axis=1, mode="promise_in_bounds")


def onehot_rows(idx_row):
    rows = lax.broadcasted_iota(jnp.int32, (BLK, BLK), 0)
    return jnp.where(rows == idx_row, 1.0, 0.0).astype(BF16)


NT = (((1,), (1,)), ((), ()))


def point_stage_rows(count):
    return -(-3 * count // 16) * 16


def cam_stage_rows(count):
    whole = count // 8 * 8
    return -(-(3 * whole + 8) // 16) * 16


def cam_sum_rows(count):
    return count // 8 * 8 + 8


def point_scatter(stage, vals, idx_ref, t, col):
    count = len(vals)
    group = vals[0].shape[0]
    high = point_stage_rows(count)
    for j, val in enumerate(vals):
        for s, piece in enumerate(split3(val)):
            row = s * count + j
            stage[row * group : (row + 1) * group, :] = piece
    tiles = group // BPT
    for u in range(0, tiles, 2):
        lhs, rhs = [], []
        for b in range(BPT):
            pair = [(u + v) * BPT + b for v in range(2)]
            lhs.append(
                jnp.concatenate([stage[pl.ds(c, high, stride=group), :] for c in pair], axis=0).astype(BF16)
            )
            rhs.append(
                jnp.concatenate([onehot_rows(idx_ref[pl.ds(t * group + c, 1), :]) for c in pair], axis=0)
            )
        res = lax.dot_general(
            jnp.concatenate(lhs, axis=1), jnp.concatenate(rhs, axis=1), NT, preferred_element_type=F32
        )
        for v in range(2):
            start = pl.multiple_of((t * tiles + u + v) * high, 16)
            col[pl.ds(start, high), :] = res[v * high : (v + 1) * high, v * BLK : (v + 1) * BLK]


def point_sums(col, count, tiles):
    high = point_stage_rows(count)
    out = []
    for j in range(count):
        pieces = [col[pl.ds(s * count + j, tiles, stride=high), :] for s in range(3)]
        out.append(pieces[0] + (pieces[1] + pieces[2]))
    return out


def cam_scatter(stage, vals, idx_ref, t, pblk):
    count = len(vals)
    whole = count // 8 * 8
    rest = count - whole
    group = vals[0].shape[0]
    high = cam_stage_rows(count)
    keep = cam_sum_rows(count)
    for k, val in enumerate(vals):
        for s, piece in enumerate(split3(val)):
            row = s * whole + k if k < whole else 3 * whole + s * rest + k - whole
            stage[row * group : (row + 1) * group, :] = piece
    for b in range(0, group, 2):
        lhs = jnp.concatenate(
            [stage[pl.ds(b + v, high, stride=group), :] for v in range(2)], axis=0
        ).astype(BF16)
        rhs = jnp.concatenate(
            [onehot_rows(idx_ref[pl.ds(t * group + b + v, 1), :]) for v in range(2)], axis=0
        )
        both = lax.dot_general(lhs, rhs, NT, preferred_element_type=F32)
        for v in range(2):
            res = both[v * high : (v + 1) * high, v * BLK : (v + 1) * BLK]
            start = pl.multiple_of((t * group + b + v) * keep, 8)
            pblk[pl.ds(start, whole), :] = (
                res[0:whole] + res[whole : 2 * whole] + res[2 * whole : 3 * whole]
            )
            pblk[pl.ds(start + whole, 8), :] = res[3 * whole : 3 * whole + 8]


def blocks_to_dense(pblk, bt_ref, count, mine_ref, other_ref, peers, stride):
    nblocks = bt_ref.shape[1]
    half = bt_ref.shape[0] // 2
    quarter = half // peers
    whole = count // 8 * 8
    rest = count - whole
    keep = cam_sum_rows(count)
    for k in range(count):
        if k < whole:
            x = pblk[pl.ds(k, nblocks, stride=keep), :]
        else:
            p = [pblk[pl.ds(k + s * rest, nblocks, stride=keep), :] for s in range(3)]
            x = p[0] + (p[1] + p[2])
        rhs = jnp.concatenate(split3(x), axis=1).astype(BF16)
        res = jnp.dot(bt_ref[...], rhs, preferred_element_type=F32)
        res = res[:, :BLK] + res[:, BLK : 2 * BLK] + res[:, 2 * BLK :]
        for i in range(quarter):
            rows = pl.ds(k * quarter + i, peers, stride=stride)
            mine_ref[rows, :] = res[i * peers : (i + 1) * peers]
            other_ref[rows, :] = res[half + i * peers : half + (i + 1) * peers]


def fill_extra(mine_ref, other_ref, rows, peers, stride):
    first = stride - EXTRA
    for i in range(EXTRA):
        row = rows[i] if i < len(rows) else jnp.zeros((1, BLK), F32)
        full = jnp.broadcast_to(row, (peers, BLK))
        mine_ref[pl.ds(first + i, peers, stride=stride), :] = full
        other_ref[pl.ds(first + i, peers, stride=stride), :] = full


def extra_sum(refs, index, peers, stride):
    first = stride - EXTRA
    rows = [jnp.sum(r[pl.ds(first + index, peers, stride=stride), :], axis=0, keepdims=True) for r in refs]
    return jnp.sum(functools.reduce(jnp.add, rows), axis=1, keepdims=True)


def spread_points(ref, t, group, pidx):
    tiles = group // BPT
    out = []
    for j in range(3):
        table = [
            jnp.broadcast_to(ref[j, pl.ds(t * tiles + u, 1), :], (BPT, BLK)) for u in range(tiles)
        ]
        out.append(lane_pick(jnp.concatenate(table, axis=0), pidx))
    return out


def place_rows(entry_ref, cov_ref, pos, table, owners, held):
    per_owner = cov_ref.shape[1]
    table[...] = jnp.zeros(table.shape, jnp.int32)
    table[0:owners, 0:per_owner] = cov_ref[...]
    entry = entry_ref[...]
    owner = entry // per_owner
    slot = entry % per_owner
    block = jnp.zeros(entry.shape, jnp.int32)
    for o in range(owners):
        row = jnp.broadcast_to(table[o : o + 1, :], entry.shape)
        block = jnp.where(owner == o, lane_pick(row, slot), block)
    other = (block // held) ^ pos[0]
    return (other * held + block % held) * owners + owner


def setup_kernel(
    owners, pos, entry, cov, jac_hbm, jp_hbm, oc_hbm, op_hbm, pt_grad, pt_damp,
    mine, other, inv_out, pg_out, b_mat, bt,
    jac, jp, oc, op, sems, stage, stage2, col, pblk, grad_rows, damp_rows, table, place, hot
):
    peers = owners
    copies = [
        pltpu.make_async_copy(src, dst, sems.at[i])
        for i, (src, dst) in enumerate([(op_hbm, op), (jp_hbm, jp), (oc_hbm, oc), (jac_hbm, jac)])
    ]
    for copy in copies:
        copy.start()
    nblocks = jac.shape[1]
    tiles = nblocks // BPT
    places = bt.shape[0]
    place[...] = place_rows(entry, cov, pos, table, owners, places // 2 // owners)
    for r in range(nblocks // BLK):
        lanes = slice(r * BLK, (r + 1) * BLK)
        row = lax.broadcasted_iota(jnp.int32, (places, BLK), 0)
        hot[:, lanes] = jnp.where(row == place[r : r + 1, :], 1.0, 0.0)
    bt[...] = hot[...].astype(BF16)
    b_mat[...] = hot[...].T.astype(BF16)
    for t in range(tiles):
        lanes = slice(t * BLK, (t + 1) * BLK)
        grad_rows[pl.ds(t, 3, stride=tiles), :] = pt_grad[:, lanes]
        damp_rows[pl.ds(t, 3, stride=tiles), :] = pt_damp[:, lanes]
    copies[0].wait()
    copies[1].wait()
    grad = [grad_rows[j * tiles : (j + 1) * tiles, :] for j in range(3)]
    damp = [damp_rows[j * tiles : (j + 1) * tiles, :] for j in range(3)]

    def terms(t, carry):
        rows = pl.ds(pl.multiple_of(t * GROUP, GROUP), GROUP)
        a = [jp[j, rows, :] for j in range(6)]
        vals = [
            a[p] * a[q] + a[3 + p] * a[3 + q]
            for p, q in [(0, 0), (0, 1), (0, 2), (1, 1), (1, 2), (2, 2)]
        ]
        point_scatter(stage, vals, op, t, col)
        return carry

    lax.fori_loop(0, nblocks // GROUP, terms, 0)
    entry = point_sums(col, 6, tiles)
    c00 = entry[0] + damp[0]
    c01 = entry[1]
    c02 = entry[2]
    c11 = entry[3] + damp[1]
    c12 = entry[4]
    c22 = entry[5] + damp[2]
    a00 = c11 * c22 - c12 * c12
    a01 = c02 * c12 - c01 * c22
    a02 = c01 * c12 - c02 * c11
    a11 = c00 * c22 - c02 * c02
    a12 = c01 * c02 - c00 * c12
    a22 = c00 * c11 - c01 * c01
    recip = 1.0 / (c00 * a00 + c01 * a01 + c02 * a02)
    inv = [a * recip for a in (a00, a01, a02, a11, a12, a22)]
    for j in range(6):
        inv_out[j] = inv[j]
    pg = apply_three(inv, grad)
    for j in range(3):
        pg_out[j] = pg[j]

    copies[2].wait()
    copies[3].wait()

    def rhs_terms(t, carry):
        rows = pl.ds(pl.multiple_of(t * GROUP, GROUP), GROUP)
        g = spread_points(pg_out, t, GROUP, op[rows, :])
        c0 = jp[0, rows, :] * g[0] + jp[1, rows, :] * g[1] + jp[2, rows, :] * g[2]
        c1 = jp[3, rows, :] * g[0] + jp[4, rows, :] * g[1] + jp[5, rows, :] * g[2]
        vals = []
        diag = []
        for k in range(NP):
            j0 = jac[k, rows, :]
            j1 = jac[NP + k, rows, :]
            vals.append(j0 * c0 + j1 * c1)
            diag.append(j0 * j0 + j1 * j1)
        cam_scatter(stage2, vals + diag, oc, t, pblk)
        return carry

    lax.fori_loop(0, nblocks // GROUP, rhs_terms, 0)
    blocks_to_dense(pblk, bt, 2 * NP, mine, other, peers, mine.shape[0] // peers)


def call(kernel, name, out_shape, operands, scratch=(), smem=(), stay=()):
    def space(i):
        return pltpu.SMEM if i in smem else pl.ANY if i in stay else pltpu.VMEM

    return pl.pallas_call(
        kernel,
        in_specs=[pl.BlockSpec(memory_space=space(i)) for i in range(len(operands))],
        out_shape=out_shape,
        scratch_shapes=scratch,
        compiler_params=pltpu.CompilerParams(vmem_limit_bytes=VMEM_LIMIT),
        name=name,
    )(*operands)


def shape_of(*dims):
    return jax.ShapeDtypeStruct(dims, F32)


def setup_call(pos, entry, cov, jac, jp, oc, op, pt_grad, pt_damp, owners, places):
    nblocks = jac.shape[1]
    tiles = nblocks // BPT
    msg = shape_of(NP * places, BLK)
    return call(
        functools.partial(setup_kernel, owners),
        "setup_pass",
        [
            msg,
            msg,
            shape_of(6, tiles, BLK),
            shape_of(3, tiles, BLK),
            jax.ShapeDtypeStruct((nblocks, places), BF16),
            jax.ShapeDtypeStruct((places, nblocks), BF16),
        ],
        (pos, entry.reshape(nblocks // BLK, BLK), cov, jac, jp, oc, op, pt_grad, pt_damp),
        [
            pltpu.VMEM(jac.shape, F32),
            pltpu.VMEM(jp.shape, F32),
            pltpu.VMEM(oc.shape, jnp.int32),
            pltpu.VMEM(op.shape, jnp.int32),
            pltpu.SemaphoreType.DMA((4,)),
            pltpu.VMEM((point_stage_rows(6) * GROUP, BLK), F32),
            pltpu.VMEM((cam_stage_rows(2 * NP) * GROUP, BLK), F32),
            pltpu.VMEM((tiles * point_stage_rows(6), BLK), F32),
            pltpu.VMEM((nblocks * cam_sum_rows(2 * NP), BLK), F32),
            pltpu.VMEM((3 * tiles, BLK), F32),
            pltpu.VMEM((3 * tiles, BLK), F32),
            pltpu.VMEM((owners, BLK), jnp.int32),
            pltpu.VMEM((nblocks // BLK, BLK), jnp.int32),
            pltpu.VMEM((places, nblocks), F32),
        ],
        smem=(0,),
        stay=(3, 4, 5, 6),
    )


def operator_kernel(second, peers, share, *refs):
    if second:
        (pos, jac, jp, oc, op, b_mat, bt, inv, mine_in, other_in, proj_in, state, image, norm_in,
         mine, other, sol_out, held_out, scal_out, stage, stage2, pick, col, pblk, proj) = refs
    else:
        (pos, jac, jp, oc, op, b_mat, bt, inv, mine_in, other_in,
         mine, other, sol_out, held_out, scal_out, proj, stage, stage2, pick, col, pblk) = refs
    nblocks = jac.shape[1]
    tiles = nblocks // BPT
    stride = mine_in.shape[0] // peers
    quarter = (stride - EXTRA) // NP
    for k in range(NP):
        x = jnp.concatenate(
            [
                ref[pl.ds(k * quarter + i, peers, stride=stride), :]
                for ref in (mine_in, other_in)
                for i in range(quarter)
            ],
            axis=0,
        )
        rhs = jnp.concatenate(split3(x), axis=1).astype(BF16)
        res = jnp.dot(b_mat[...], rhs, preferred_element_type=F32)
        pick[k] = res[:, :BLK] + res[:, BLK : 2 * BLK] + res[:, 2 * BLK :]
    for h, ref in enumerate((mine_in, other_in)):
        held_out[h] = ref[pl.ds(pl.multiple_of(pos[1] * stride, 8), stride), :]
    total = extra_sum((mine_in, other_in), 0, peers, stride)
    if second:
        norm = norm_in[0:1, 0:1]
        step_len = norm / total
        scal_out[...] = jnp.broadcast_to(total, (8, BLK))
        rhs, precond, damp, direction = (state[i] for i in range(4))
        resid = rhs - step_len * image[...]
        z = resid / precond
        keep = lax.broadcasted_iota(jnp.int32, (stride, BLK), 0) < stride - EXTRA

        def lanes(v):
            return share * jnp.sum(jnp.where(keep, v, 0.0), axis=0, keepdims=True)

        owner_sums = [lanes(damp * z * z), lanes(damp * z * direction), lanes(resid * z)]
    else:
        scal_out[...] = jnp.broadcast_to(total, (8, BLK))

    def project(t, carry):
        rows = pl.ds(pl.multiple_of(t * GROUP, GROUP), GROUP)
        cidx = oc[rows, :]
        p0 = jnp.zeros((GROUP, BLK), F32)
        p1 = jnp.zeros((GROUP, BLK), F32)
        for k in range(NP):
            v = lane_pick(pick[k, rows, :], cidx)
            p0 += jac[k, rows, :] * v
            p1 += jac[NP + k, rows, :] * v
        if second:
            p0 = proj_in[0, rows, :] - step_len * p0
            p1 = proj_in[1, rows, :] - step_len * p1
        proj[0, rows, :] = p0
        proj[1, rows, :] = p1
        vals = [jp[j, rows, :] * p0 + jp[3 + j, rows, :] * p1 for j in range(3)]
        point_scatter(stage, vals, op, t, col)
        return carry

    lax.fori_loop(0, nblocks // GROUP, project, 0)
    sol = apply_three([inv[j] for j in range(6)], point_sums(col, 3, tiles))
    for j in range(3):
        sol_out[j] = sol[j]

    def correct(t, carry):
        rows = pl.ds(pl.multiple_of(t * GROUP, GROUP), GROUP)
        g = spread_points(sol_out, t, GROUP, op[rows, :])
        p0 = proj[0, rows, :]
        p1 = proj[1, rows, :]
        c0 = p0 - (jp[0, rows, :] * g[0] + jp[1, rows, :] * g[1] + jp[2, rows, :] * g[2])
        c1 = p1 - (jp[3, rows, :] * g[0] + jp[4, rows, :] * g[1] + jp[5, rows, :] * g[2])
        if second:
            zz, zd = carry
            zz = zz + (p0 * c0 + p1 * c1)
            zd = zd + (proj_in[0, rows, :] * c0 + proj_in[1, rows, :] * c1)
            carry = (zz, zd)
        vals = [jac[k, rows, :] * c0 + jac[NP + k, rows, :] * c1 for k in range(NP)]
        cam_scatter(stage2, vals, oc, t, pblk)
        return carry

    zero = jnp.zeros((GROUP, BLK), F32)
    sums = lax.fori_loop(0, nblocks // GROUP, correct, (zero, zero) if second else 0)
    blocks_to_dense(pblk, bt, NP, mine, other, peers, stride)
    rows = []
    if second:
        rows = [
            jnp.sum(sums[0], axis=0, keepdims=True) + owner_sums[0],
            jnp.sum(sums[1], axis=0, keepdims=True) + owner_sums[1],
            owner_sums[2],
        ]
    fill_extra(mine, other, rows, peers, stride)


def operator_call(pos, jac, jp, oc, op, b_mat, bt, inv, mine, other, peers, share, later=()):
    nblocks = jac.shape[1]
    tiles = nblocks // BPT
    stride = mine.shape[0] // peers
    proj = [] if later else [shape_of(2, nblocks, BLK)]
    proj_scratch = [pltpu.VMEM((2, nblocks, BLK), F32)] if later else []
    return call(
        functools.partial(operator_kernel, bool(later), peers, share),
        "second_pass" if later else "first_pass",
        [
            shape_of(*mine.shape),
            shape_of(*mine.shape),
            shape_of(3, tiles, BLK),
            shape_of(2, stride, BLK),
            shape_of(8, BLK),
        ]
        + proj,
        (pos, jac, jp, oc, op, b_mat, bt, inv, mine, other) + later,
        [
            pltpu.VMEM((point_stage_rows(3) * GROUP, BLK), F32),
            pltpu.VMEM((cam_stage_rows(NP) * GROUP, BLK), F32),
            pltpu.VMEM((NP, nblocks, BLK), F32),
            pltpu.VMEM((tiles * point_stage_rows(3), BLK), F32),
            pltpu.VMEM((nblocks * cam_sum_rows(NP), BLK), F32),
        ]
        + proj_scratch,
        smem=(0,),
    )


def sum_kernel(peers, got, out):
    stride = got.shape[0] // peers
    total = got[0:stride, :]
    for d in range(1, peers):
        total = total + got[d * stride : (d + 1) * stride, :]
    out[...] = total


def sum_parts(parts):
    return (parts[0][...] + parts[1][...]) + (parts[2][...] + parts[3][...])


def send_all(msg, values, scalar, peers):
    stride = values.shape[0]
    data = stride - EXTRA
    row = lax.broadcasted_iota(jnp.int32, values.shape, 0)
    lanes = jnp.sum(jnp.where(row < data, scalar, 0.0), axis=0, keepdims=True)
    out = jnp.where(row < data, values, jnp.where(row == data, lanes, 0.0))
    for d in range(peers):
        msg[d * stride : (d + 1) * stride, :] = out


def start_kernel(peers, quarter, pos, p0, p1, p2, p3, grad, damp, msg, state, rows):
    data = NP * quarter
    rows[...] = jnp.ones(rows.shape, F32)
    for i in range(quarter):
        lanes = pl.ds(pl.multiple_of((pos[0] * quarter + i) * BLK, BLK), BLK)
        rows[0, pl.ds(i, NP, stride=quarter), :] = grad[:, lanes]
        rows[1, pl.ds(i, NP, stride=quarter), :] = damp[:, lanes]
    total = sum_parts((p0, p1, p2, p3))
    ones = jnp.ones((EXTRA, BLK), F32)
    rhs = rows[0] - jnp.concatenate([total[:data], ones], axis=0)
    precond = rows[1] + jnp.concatenate([total[data:], ones], axis=0)
    direction = rhs / precond
    state[0] = rhs
    state[1] = precond
    state[2] = rows[1]
    state[3] = direction
    send_all(msg, direction, rhs * direction, peers)


def image_kernel(peers, p0, p1, p2, p3, state, msg, image):
    direction = state[3]
    value = state[2] * direction + sum_parts((p0, p1, p2, p3))
    image[...] = value
    send_all(msg, value / state[1], direction * value, peers)


def last_kernel(p0, p1, p2, p3, state, image, norm_in, curv_in, resid_out, scal_out):
    norm = norm_in[0:1, 0:1]
    curv = curv_in[0:1, 0:1]
    step0 = norm / curv
    total = sum_parts((p0, p1, p2, p3))
    stride = total.shape[0]
    sums = jnp.sum(total[stride - EXTRA :], axis=1, keepdims=True)
    zz, zd, norm1 = (sums[i : i + 1] for i in range(3))
    beta = norm1 / norm
    curv1 = zz + 2.0 * beta * zd + beta * beta * curv
    step1 = norm1 / curv1
    resid = state[0] - step0 * image[...]
    z = resid / state[1]
    image1 = (state[2] * z + total) + beta * image[...]
    resid_out[...] = resid - step1 * image1
    for i, s in enumerate((step0, step1, beta)):
        scal_out[i * 8 : (i + 1) * 8, :] = jnp.broadcast_to(s, (8, BLK))


def step_kernel(pos, scal, held0, held1, pg, sol0, sol1, cam_out, pt_out, pts_rows, cams_rows):
    step0, step1, beta = (scal[i * 8 : i * 8 + 1, 0:1] for i in range(3))
    tiles = pg.shape[1]
    for j in range(3):
        first = sol0[j]
        pts_rows[j * tiles : (j + 1) * tiles, :] = (
            pg[j] - step0 * first - step1 * (sol1[j] + beta * first)
        )
    for t in range(tiles):
        pt_out[:, t * BLK : (t + 1) * BLK] = pts_rows[pl.ds(t, 3, stride=tiles), :]
    for h in range(2):
        d0 = held0[h]
        z = d0 - step0 * held1[h]
        cams_rows[...] = step0 * d0 + step1 * (z + beta * d0)
        put_cams(cam_out, cams_rows, pos[0] ^ h)


def put_cams(out, rows, core):
    held = (rows.shape[0] - EXTRA) // NP
    for i in range(held):
        lanes = pl.ds(pl.multiple_of((core * held + i) * BLK, BLK), BLK)
        out[:, lanes] = rows[pl.ds(i, NP, stride=held), :]


def resid_kernel(pos, own, theirs, out):
    put_cams(out, own, pos[0])
    put_cams(out, theirs, pos[0] ^ 1)


def local(jac, jp, oc, op, entry, cov, cam_grad, cam_damp, pt_grad, pt_damp):
    ways = lax.axis_size("x")
    peers = lax.axis_size("z") * lax.axis_size("y")
    pos = jnp.stack([lax.axis_index("core"), lax.axis_index(("z", "y"))]).astype(jnp.int32)
    shard = cam_grad.shape[1]
    held = shard // BLK // 2
    stride = NP * held + EXTRA
    msg = shape_of(peers * stride, BLK)

    def exchange(v):
        return lax.ppermute(v, "core", [(0, 1), (1, 0)])

    def to_peers(v):
        shaped = v.reshape(peers, -1, BLK)
        return lax.all_to_all(shaped, ("z", "y"), 0, 0, tiled=False).reshape(-1, BLK)

    def reduce_parts(mine, other):
        got = to_peers(mine + exchange(other))
        part = call(
            functools.partial(sum_kernel, peers), "sum_step", shape_of(got.shape[0] // peers, BLK), (got,)
        )
        return (part,) + tuple(
            lax.ppermute(part, "x", [(i, (i + s) % ways) for i in range(ways)])
            for s in range(1, ways)
        )

    mine, other, inv, pg, b_mat, bt = setup_call(
        pos, entry, cov, jac, jp, oc, op, pt_grad, pt_damp, peers, 2 * held * peers
    )
    msg_out, state = call(
        functools.partial(start_kernel, peers, held),
        "start_step",
        [msg, shape_of(4, stride, BLK)],
        (pos,) + reduce_parts(mine, other) + (cam_grad, cam_damp),
        [pltpu.VMEM((2, stride, BLK), F32)],
        smem=(0,),
    )
    mine = to_peers(msg_out)
    other = exchange(mine)
    share = 1.0 / ways
    mine, other, sol0, held0, norm, proj0 = operator_call(
        pos, jac, jp, oc, op, b_mat, bt, inv, mine, other, peers, share
    )
    msg_out, image = call(
        functools.partial(image_kernel, peers),
        "image_step",
        [msg, shape_of(stride, BLK)],
        reduce_parts(mine, other) + (state,),
    )
    mine = to_peers(msg_out)
    other = exchange(mine)
    mine, other, sol1, held1, curv = operator_call(
        pos, jac, jp, oc, op, b_mat, bt, inv, mine, other, peers, share, (proj0, state, image, norm)
    )
    resid, scal = call(
        last_kernel,
        "last_step",
        [shape_of(stride, BLK), shape_of(24, BLK)],
        reduce_parts(mine, other) + (state, image, norm, curv),
    )
    theirs = exchange(resid)
    cam_step, pt_step = call(
        step_kernel,
        "result_step",
        [shape_of(NP, shard), shape_of(3, pt_grad.shape[1])],
        (pos, scal, held0, held1, pg, sol0, sol1),
        [pltpu.VMEM((3 * pg.shape[1], BLK), F32), pltpu.VMEM((stride, BLK), F32)],
        smem=(0,),
    )
    cam_resid = call(
        resid_kernel, "result_resid", shape_of(NP, shard), (pos, resid, theirs), smem=(0,)
    )
    return cam_step, cam_resid, pt_step


def solution(mesh):
    fine = Mesh(mesh.devices.reshape(4, 2, 4, 4), ("x", "core", "z", "y"))
    pts, cam = ("x", "core"), ("z", "y")
    every = pts + cam
    in_specs = (
        P(None, every, None),
        P(None, every, None),
        P(every, None),
        P(every, None),
        P(every),
        P(every, None),
        P(None, cam),
        P(None, cam),
        P(None, every),
        P(None, every),
    )
    out_specs = (P(None, cam), P(None, cam), P(None, every))
    return jax.shard_map(local, mesh=fine, in_specs=in_specs, out_specs=out_specs, check_vma=False)
```

```python
import functools

import jax
import jax.numpy as jnp
from jax import lax
from jax.experimental import pallas as pl
from jax.experimental.pallas import tpu as pltpu
from jax.sharding import Mesh, PartitionSpec as P

BLK = 128
BPT = 8
NP = 9
EXTRA = 4
F32 = jnp.float32
BF16 = jnp.bfloat16
GROUP = 128
VMEM_LIMIT = 24 * 1024 * 1024


def split3(x):
    hi = x.astype(BF16).astype(F32)
    rest = x - hi
    mid = rest.astype(BF16).astype(F32)
    return hi, mid, rest - mid


def apply_three(inverse, values):
    first = inverse[0] * values[0] + inverse[1] * values[1] + inverse[2] * values[2]
    second = inverse[1] * values[0] + inverse[3] * values[1] + inverse[4] * values[2]
    third = inverse[2] * values[0] + inverse[4] * values[1] + inverse[5] * values[2]
    return [first, second, third]


def lane_pick(table, idx):
    return jnp.take_along_axis(table, idx, axis=1, mode="promise_in_bounds")


def onehot_rows(idx_row):
    rows = lax.broadcasted_iota(jnp.int32, (BLK, BLK), 0)
    return jnp.where(rows == idx_row, 1.0, 0.0).astype(BF16)


NT = (((1,), (1,)), ((), ()))


def point_stage_rows(count):
    return -(-3 * count // 16) * 16


def cam_stage_rows(count):
    whole = count // 8 * 8
    return -(-(3 * whole + 8) // 16) * 16


def cam_sum_rows(count):
    return count // 8 * 8 + 8


def point_scatter(stage, vals, idx_ref, t, col):
    count = len(vals)
    group = vals[0].shape[0]
    high = point_stage_rows(count)
    for j, val in enumerate(vals):
        for s, piece in enumerate(split3(val)):
            row = s * count + j
            stage[row * group : (row + 1) * group, :] = piece
    tiles = group // BPT
    for u in range(0, tiles, 2):
        lhs, rhs = [], []
        for b in range(BPT):
            pair = [(u + v) * BPT + b for v in range(2)]
            lhs.append(
                jnp.concatenate([stage[pl.ds(c, high, stride=group), :] for c in pair], axis=0).astype(BF16)
            )
            rhs.append(
                jnp.concatenate([onehot_rows(idx_ref[pl.ds(t * group + c, 1), :]) for c in pair], axis=0)
            )
        res = lax.dot_general(
            jnp.concatenate(lhs, axis=1), jnp.concatenate(rhs, axis=1), NT, preferred_element_type=F32
        )
        for v in range(2):
            start = pl.multiple_of((t * tiles + u + v) * high, 16)
            col[pl.ds(start, high), :] = res[v * high : (v + 1) * high, v * BLK : (v + 1) * BLK]


def point_sums(col, count, tiles):
    high = point_stage_rows(count)
    out = []
    for j in range(count):
        pieces = [col[pl.ds(s * count + j, tiles, stride=high), :] for s in range(3)]
        out.append(pieces[0] + (pieces[1] + pieces[2]))
    return out


def cam_scatter(stage, vals, idx_ref, t, pblk):
    count = len(vals)
    whole = count // 8 * 8
    rest = count - whole
    group = vals[0].shape[0]
    high = cam_stage_rows(count)
    keep = cam_sum_rows(count)
    for k, val in enumerate(vals):
        for s, piece in enumerate(split3(val)):
            row = s * whole + k if k < whole else 3 * whole + s * rest + k - whole
            stage[row * group : (row + 1) * group, :] = piece
    for b in range(0, group, 2):
        lhs = jnp.concatenate(
            [stage[pl.ds(b + v, high, stride=group), :] for v in range(2)], axis=0
        ).astype(BF16)
        rhs = jnp.concatenate(
            [onehot_rows(idx_ref[pl.ds(t * group + b + v, 1), :]) for v in range(2)], axis=0
        )
        both = lax.dot_general(lhs, rhs, NT, preferred_element_type=F32)
        for v in range(2):
            res = both[v * high : (v + 1) * high, v * BLK : (v + 1) * BLK]
            start = pl.multiple_of((t * group + b + v) * keep, 8)
            pblk[pl.ds(start, whole), :] = (
                res[0:whole] + res[whole : 2 * whole] + res[2 * whole : 3 * whole]
            )
            pblk[pl.ds(start + whole, 8), :] = res[3 * whole : 3 * whole + 8]


def pieces_wide(arrays):
    return jnp.concatenate([p for x in arrays for p in split3(x)], axis=1).astype(BF16)


def pieces_sum(res, i):
    res = res[:, 3 * i * BLK : 3 * (i + 1) * BLK]
    return res[:, :BLK] + res[:, BLK : 2 * BLK] + res[:, 2 * BLK :]


def blocks_to_dense(pblk, bt_ref, h, count, out_ref, peers):
    nblocks = bt_ref.shape[1]
    half = bt_ref.shape[0] // 2
    quarter = half // peers
    stride = out_ref.shape[0] // peers
    whole = count // 8 * 8
    rest = count - whole
    keep = cam_sum_rows(count)
    for k0 in range(0, count, 2):
        ks = range(k0, min(k0 + 2, count))
        arrays = []
        for k in ks:
            if k < whole:
                arrays.append(pblk[pl.ds(k, nblocks, stride=keep), :])
            else:
                p = [pblk[pl.ds(k + s * rest, nblocks, stride=keep), :] for s in range(3)]
                arrays.append(p[0] + (p[1] + p[2]))
        both = jnp.dot(
            bt_ref[h * half : (h + 1) * half, :], pieces_wide(arrays), preferred_element_type=F32
        )
        for n, k in enumerate(ks):
            res = pieces_sum(both, n)
            for i in range(quarter):
                out_ref[pl.ds(k * quarter + i, peers, stride=stride), :] = res[i * peers : (i + 1) * peers]


def half_kernel(peers, count, pblk, bt, extra, mine):
    blocks_to_dense(pblk, bt, 0, count, mine, peers)
    if extra is not None:
        fill_extra(mine, [extra[i : i + 1, :] for i in range(EXTRA)], peers)


def half_call(pblk, bt, peers, count, stride, extra=None):
    kernel = functools.partial(half_kernel, peers, count)
    operands = (pblk, bt)
    if extra is None:
        kernel = lambda pblk, bt, mine: half_kernel(peers, count, pblk, bt, None, mine)
    else:
        operands += (extra,)
    return call(
        kernel,
        "own_half",
        shape_of(peers * stride, BLK),
        operands,
        cost=pl.CostEstimate(flops=10**9, bytes_accessed=4 * 10**6, transcendentals=0),
    )


def pick_half(b_ref, h, msg_ref, peers, k0, count):
    half = b_ref.shape[1] // 2
    quarter = half // peers
    stride = msg_ref.shape[0] // peers
    arrays = [
        jnp.concatenate(
            [msg_ref[pl.ds(k * quarter + i, peers, stride=stride), :] for i in range(quarter)], axis=0
        )
        for k in range(k0, k0 + count)
    ]
    both = jnp.dot(
        b_ref[:, h * half : (h + 1) * half], pieces_wide(arrays), preferred_element_type=F32
    )
    return [pieces_sum(both, n) for n in range(count)]


def pick_kernel(peers, b_mat, mine, pick):
    for k0 in range(0, NP, 2):
        count = min(2, NP - k0)
        for n, value in enumerate(pick_half(b_mat, 0, mine, peers, k0, count)):
            pick[k0 + n] = value


def pick_call(b_mat, mine, peers):
    return call(
        functools.partial(pick_kernel, peers),
        "pick_own_half",
        shape_of(NP, b_mat.shape[0], BLK),
        (b_mat, mine),
        cost=pl.CostEstimate(flops=10**9, bytes_accessed=4 * 10**6, transcendentals=0),
    )


def fill_extra(msg_ref, rows, peers):
    stride = msg_ref.shape[0] // peers
    for i, row in enumerate(rows):
        msg_ref[pl.ds(stride - EXTRA + i, peers, stride=stride), :] = jnp.broadcast_to(row, (peers, BLK))


def extra_sum(refs, index, peers, stride):
    first = stride - EXTRA
    rows = [jnp.sum(r[pl.ds(first + index, peers, stride=stride), :], axis=0, keepdims=True) for r in refs]
    return jnp.sum(functools.reduce(jnp.add, rows), axis=1, keepdims=True)


def spread_points(ref, t, group, pidx):
    tiles = group // BPT
    out = []
    for j in range(3):
        table = [
            jnp.broadcast_to(ref[j, pl.ds(t * tiles + u, 1), :], (BPT, BLK)) for u in range(tiles)
        ]
        out.append(lane_pick(jnp.concatenate(table, axis=0), pidx))
    return out


def terms_kernel(pos, jp, op, col, stage):
    nblocks = op.shape[0]

    def terms(t, carry):
        rows = pl.ds(pl.multiple_of(t * GROUP, GROUP), GROUP)
        a = [jp[j, rows, :] for j in range(6)]
        vals = [
            a[p] * a[q] + a[3 + p] * a[3 + q]
            for p, q in [(0, 0), (0, 1), (0, 2), (1, 1), (1, 2), (2, 2)]
        ]
        point_scatter(stage, vals, op, t, col)
        return carry

    lax.fori_loop(0, nblocks // GROUP, terms, 0)


def setup_kernel(
    peers, col, jac, jp, oc, op, pt_grad, pt_damp, bt,
    other, pblk, inv_out, pg_out, stage2, grad_rows, damp_rows
):
    nblocks = jac.shape[1]
    tiles = nblocks // BPT
    for t in range(tiles):
        lanes = slice(t * BLK, (t + 1) * BLK)
        grad_rows[pl.ds(t, 3, stride=tiles), :] = pt_grad[:, lanes]
        damp_rows[pl.ds(t, 3, stride=tiles), :] = pt_damp[:, lanes]
    grad = [grad_rows[j * tiles : (j + 1) * tiles, :] for j in range(3)]
    damp = [damp_rows[j * tiles : (j + 1) * tiles, :] for j in range(3)]

    entry = point_sums(col, 6, tiles)
    c00 = entry[0] + damp[0]
    c01 = entry[1]
    c02 = entry[2]
    c11 = entry[3] + damp[1]
    c12 = entry[4]
    c22 = entry[5] + damp[2]
    a00 = c11 * c22 - c12 * c12
    a01 = c02 * c12 - c01 * c22
    a02 = c01 * c12 - c02 * c11
    a11 = c00 * c22 - c02 * c02
    a12 = c01 * c02 - c00 * c12
    a22 = c00 * c11 - c01 * c01
    recip = 1.0 / (c00 * a00 + c01 * a01 + c02 * a02)
    inv = [a * recip for a in (a00, a01, a02, a11, a12, a22)]
    for j in range(6):
        inv_out[j] = inv[j]
    pg = apply_three(inv, grad)
    for j in range(3):
        pg_out[j] = pg[j]

    def rhs_terms(t, carry):
        rows = pl.ds(pl.multiple_of(t * GROUP, GROUP), GROUP)
        g = spread_points(pg_out, t, GROUP, op[rows, :])
        c0 = jp[0, rows, :] * g[0] + jp[1, rows, :] * g[1] + jp[2, rows, :] * g[2]
        c1 = jp[3, rows, :] * g[0] + jp[4, rows, :] * g[1] + jp[5, rows, :] * g[2]
        vals = []
        diag = []
        for k in range(NP):
            j0 = jac[k, rows, :]
            j1 = jac[NP + k, rows, :]
            vals.append(j0 * c0 + j1 * c1)
            diag.append(j0 * j0 + j1 * j1)
        cam_scatter(stage2, vals + diag, oc, t, pblk)
        return carry

    lax.fori_loop(0, nblocks // GROUP, rhs_terms, 0)
    blocks_to_dense(pblk, bt, 1, 2 * NP, other, peers)


def call(kernel, name, out_shape, operands, scratch=(), smem=(), cost=None):
    return pl.pallas_call(
        kernel,
        in_specs=[
            pl.BlockSpec(memory_space=pltpu.SMEM if i in smem else pltpu.VMEM)
            for i in range(len(operands))
        ],
        out_shape=out_shape,
        scratch_shapes=scratch,
        compiler_params=pltpu.CompilerParams(vmem_limit_bytes=VMEM_LIMIT),
        cost_estimate=cost,
        name=name,
    )(*operands)


def shape_of(*dims):
    return jax.ShapeDtypeStruct(dims, F32)


def setup_call(pos, jac, jp, oc, op, pt_grad, pt_damp, bt, peers):
    nblocks = jac.shape[1]
    tiles = nblocks // BPT
    col = call(
        terms_kernel,
        "point_terms",
        shape_of(tiles * point_stage_rows(6), BLK),
        (pos, jp, op),
        [pltpu.VMEM((point_stage_rows(6) * GROUP, BLK), F32)],
        smem=(0,),
        cost=pl.CostEstimate(flops=4 * 10**9, bytes_accessed=10**7, transcendentals=0),
    )
    return call(
        functools.partial(setup_kernel, peers),
        "setup_pass",
        [
            shape_of(NP * bt.shape[0], BLK),
            shape_of(nblocks * cam_sum_rows(2 * NP), BLK),
            shape_of(6, tiles, BLK),
            shape_of(3, tiles, BLK),
        ],
        (col, jac, jp, oc, op, pt_grad, pt_damp, bt),
        [
            pltpu.VMEM((cam_stage_rows(2 * NP) * GROUP, BLK), F32),
            pltpu.VMEM((3 * tiles, BLK), F32),
            pltpu.VMEM((3 * tiles, BLK), F32),
        ],
    )


def operator_kernel(second, peers, side, *refs):
    if second:
        (pos, jac, jp, oc, op, b_mat, bt, inv, pick_in, mine_in, other_in, proj_in, state, image, norm_in,
         other, pblk, sol_out, held_out, scal_out, extra, stage, stage2, pick, col, proj) = refs
    else:
        (pos, jac, jp, oc, op, b_mat, bt, inv, pick_in, mine_in, other_in,
         other, pblk, sol_out, held_out, scal_out, extra, proj, stage, stage2, pick, col) = refs
    nblocks = jac.shape[1]
    tiles = nblocks // BPT
    stride = mine_in.shape[0] // peers
    for k0 in range(0, NP, 2):
        count = min(2, NP - k0)
        for n, value in enumerate(pick_half(b_mat, 1, other_in, peers, k0, count)):
            pick[k0 + n] = pick_in[k0 + n] + value
    for h, ref in enumerate((mine_in, other_in)):
        for x in range(peers // side**2):
            start = pl.multiple_of((x * side + pos[2 + h]) * stride, 8)
            held_out[h, x] = ref[pl.ds(start, stride), :]
    total = extra_sum((mine_in, other_in), 0, peers, stride)
    if second:
        norm = norm_in[0:1, 0:1]
        step_len = norm / total
        scal_out[...] = jnp.broadcast_to(total, (8, BLK))
        rhs, precond, damp, direction = (state[i] for i in range(4))
        resid = rhs - step_len * image[...]
        z = resid / precond
        keep = lax.broadcasted_iota(jnp.int32, (stride, BLK), 0) < stride - EXTRA

        def lanes(v):
            return jnp.sum(jnp.where(keep, v, 0.0), axis=0, keepdims=True)

        owner_sums = [lanes(damp * z * z), lanes(damp * z * direction), lanes(resid * z)]
    else:
        scal_out[...] = jnp.broadcast_to(total, (8, BLK))

    def project(t, carry):
        rows = pl.ds(pl.multiple_of(t * GROUP, GROUP), GROUP)
        cidx = oc[rows, :]
        p0 = jnp.zeros((GROUP, BLK), F32)
        p1 = jnp.zeros((GROUP, BLK), F32)
        for k in range(NP):
            v = lane_pick(pick[k, rows, :], cidx)
            p0 += jac[k, rows, :] * v
            p1 += jac[NP + k, rows, :] * v
        if second:
            p0 = proj_in[0, rows, :] - step_len * p0
            p1 = proj_in[1, rows, :] - step_len * p1
        proj[0, rows, :] = p0
        proj[1, rows, :] = p1
        vals = [jp[j, rows, :] * p0 + jp[3 + j, rows, :] * p1 for j in range(3)]
        point_scatter(stage, vals, op, t, col)
        return carry

    lax.fori_loop(0, nblocks // GROUP, project, 0)
    sol = apply_three([inv[j] for j in range(6)], point_sums(col, 3, tiles))
    for j in range(3):
        sol_out[j] = sol[j]

    def correct(t, carry):
        rows = pl.ds(pl.multiple_of(t * GROUP, GROUP), GROUP)
        g = spread_points(sol_out, t, GROUP, op[rows, :])
        p0 = proj[0, rows, :]
        p1 = proj[1, rows, :]
        c0 = p0 - (jp[0, rows, :] * g[0] + jp[1, rows, :] * g[1] + jp[2, rows, :] * g[2])
        c1 = p1 - (jp[3, rows, :] * g[0] + jp[4, rows, :] * g[1] + jp[5, rows, :] * g[2])
        if second:
            zz, zd = carry
            zz = zz + (p0 * c0 + p1 * c1)
            zd = zd + (proj_in[0, rows, :] * c0 + proj_in[1, rows, :] * c1)
            carry = (zz, zd)
        vals = [jac[k, rows, :] * c0 + jac[NP + k, rows, :] * c1 for k in range(NP)]
        cam_scatter(stage2, vals, oc, t, pblk)
        return carry

    zero = jnp.zeros((GROUP, BLK), F32)
    sums = lax.fori_loop(0, nblocks // GROUP, correct, (zero, zero) if second else 0)
    blocks_to_dense(pblk, bt, 1, NP, other, peers)
    rows = []
    if second:
        rows = [
            jnp.sum(sums[0], axis=0, keepdims=True) + owner_sums[0],
            jnp.sum(sums[1], axis=0, keepdims=True) + owner_sums[1],
            owner_sums[2],
        ]
    rows += [jnp.zeros((1, BLK), F32)] * (EXTRA - len(rows))
    fill_extra(other, rows, peers)
    extra[...] = jnp.concatenate(rows, axis=0)


def operator_call(pos, jac, jp, oc, op, b_mat, bt, inv, pick, mine, other, peers, side, later=()):
    nblocks = jac.shape[1]
    tiles = nblocks // BPT
    stride = mine.shape[0] // peers
    proj = [] if later else [shape_of(2, nblocks, BLK)]
    proj_scratch = [pltpu.VMEM((2, nblocks, BLK), F32)] if later else []
    return call(
        functools.partial(operator_kernel, bool(later), peers, side),
        "second_pass" if later else "first_pass",
        [
            shape_of(*mine.shape),
            shape_of(nblocks * cam_sum_rows(NP), BLK),
            shape_of(3, tiles, BLK),
            shape_of(2, peers // side**2, stride, BLK),
            shape_of(8, BLK),
            shape_of(EXTRA, BLK),
        ]
        + proj,
        (pos, jac, jp, oc, op, b_mat, bt, inv, pick, mine, other) + later,
        [
            pltpu.VMEM((point_stage_rows(3) * GROUP, BLK), F32),
            pltpu.VMEM((cam_stage_rows(NP) * GROUP, BLK), F32),
            pltpu.VMEM((NP, nblocks, BLK), F32),
            pltpu.VMEM((tiles * point_stage_rows(3), BLK), F32),
        ]
        + proj_scratch,
        smem=(0,),
    )


def message_sum(got, peers):
    stride = got.shape[0] // peers
    total = got[0:stride, :]
    for d in range(1, peers):
        total = total + got[d * stride : (d + 1) * stride, :]
    return total


def sum_kernel(parts, got, out):
    rows = got.shape[0] // parts
    total = got[0:rows, :]
    for d in range(1, parts):
        total = total + got[d * rows : (d + 1) * rows, :]
    out[...] = total


def send_all(msg, values, scalar, peers):
    stride = values.shape[0]
    data = stride - EXTRA
    row = lax.broadcasted_iota(jnp.int32, values.shape, 0)
    lanes = jnp.sum(jnp.where(row < data, scalar, 0.0), axis=0, keepdims=True)
    out = jnp.where(row < data, values, jnp.where(row == data, lanes, 0.0))
    for d in range(peers):
        msg[d * stride : (d + 1) * stride, :] = out


def start_kernel(peers, senders, quarter, pos, got, grad, damp, msg, state, rows):
    data = NP * quarter
    rows[...] = jnp.ones(rows.shape, F32)
    for i in range(quarter):
        lanes = pl.ds(pl.multiple_of((pos[1] * quarter + i) * BLK, BLK), BLK)
        rows[0, pl.ds(i, NP, stride=quarter), :] = grad[:, lanes]
        rows[1, pl.ds(i, NP, stride=quarter), :] = damp[:, lanes]
    total = message_sum(got, senders)
    ones = jnp.ones((EXTRA, BLK), F32)
    rhs = rows[0] - jnp.concatenate([total[:data], ones], axis=0)
    precond = rows[1] + jnp.concatenate([total[data:], ones], axis=0)
    direction = rhs / precond
    state[0] = rhs
    state[1] = precond
    state[2] = rows[1]
    state[3] = direction
    send_all(msg, direction, rhs * direction, peers)


def image_kernel(peers, got, state, msg, image):
    direction = state[3]
    value = state[2] * direction + message_sum(got, peers)
    image[...] = value
    send_all(msg, value / state[1], direction * value, peers)


def last_kernel(peers, got, state, image, norm_in, curv_in, resid_out, scal_out):
    norm = norm_in[0:1, 0:1]
    curv = curv_in[0:1, 0:1]
    step0 = norm / curv
    total = message_sum(got, peers)
    stride = total.shape[0]
    sums = jnp.sum(total[stride - EXTRA :], axis=1, keepdims=True)
    zz, zd, norm1 = (sums[i : i + 1] for i in range(3))
    beta = norm1 / norm
    curv1 = zz + 2.0 * beta * zd + beta * beta * curv
    step1 = norm1 / curv1
    resid = state[0] - step0 * image[...]
    z = resid / state[1]
    image1 = (state[2] * z + total) + beta * image[...]
    resid_out[...] = resid - step1 * image1
    for i, s in enumerate((step0, step1, beta)):
        scal_out[i * 8 : (i + 1) * 8, :] = jnp.broadcast_to(s, (8, BLK))


def step_kernel(pos, scal, held0, held1, pg, sol0, sol1, cam_out, pt_out, pts_rows, cams_rows):
    step0, step1, beta = (scal[i * 8 : i * 8 + 1, 0:1] for i in range(3))
    tiles = pg.shape[1]
    for j in range(3):
        first = sol0[j]
        pts_rows[j * tiles : (j + 1) * tiles, :] = (
            pg[j] - step0 * first - step1 * (sol1[j] + beta * first)
        )
    for t in range(tiles):
        pt_out[:, t * BLK : (t + 1) * BLK] = pts_rows[pl.ds(t, 3, stride=tiles), :]
    quarters, stride = held0.shape[1], held0.shape[2]
    quarter = (stride - EXTRA) // NP
    for h in range(2):
        for x in range(quarters):
            d0 = held0[h, x]
            z = d0 - step0 * held1[h, x]
            cams_rows[...] = step0 * d0 + step1 * (z + beta * d0)
            put_cams(cam_out, cams_rows, pos[0] ^ h, x, quarters, quarter)


def put_cams(out, rows, core, x, quarters, quarter):
    for i in range(quarter):
        block = (core * quarters + x) * quarter + i
        lanes = pl.ds(pl.multiple_of(block * BLK, BLK), BLK)
        out[:, lanes] = rows[pl.ds(i, NP, stride=quarter), :]


def resid_kernel(pos, pieces, out, rows):
    quarters, stride = pieces.shape[1], pieces.shape[2]
    quarter = (stride - EXTRA) // NP
    for h in range(2):
        for s in range(quarters):
            x = (pos[4] + quarters - s) % quarters
            rows[...] = pieces[h, s]
            put_cams(out, rows, pos[0] ^ h, x, quarters, quarter)


def local(jac, jp, oc, op, entry, cov, cam_grad, cam_damp, pt_grad, pt_damp):
    quarters = lax.axis_size("x")
    owners = lax.axis_size("z") * lax.axis_size("y")
    peers = quarters * owners
    core = lax.axis_index("core")
    x = lax.axis_index("x")
    side = lax.axis_size("z")
    z, y = lax.axis_index("z"), lax.axis_index("y")

    def peer_base(of_core, z, y):
        return jnp.where(of_core == 0, z, y) * (quarters * side) + jnp.where(of_core == 0, y, z)

    pos = jnp.stack(
        [core, core * quarters + x, peer_base(core, z, y), peer_base(1 - core, z, y), x]
    ).astype(jnp.int32)
    per_owner = cov.shape[1]
    shard = cam_grad.shape[1]
    quarter = shard // BLK // 2 // quarters
    half = peers * quarter

    entry_owner = entry // per_owner
    hit = (entry_owner[:, None, None] == jnp.arange(owners, dtype=jnp.int32)[None, :, None]) & (
        (entry % per_owner)[:, None, None] == jnp.arange(per_owner, dtype=jnp.int32)[None, None, :]
    )
    local_block = jnp.sum(jnp.where(hit, cov[None], 0), axis=(1, 2))
    core_of = local_block // (quarters * quarter)
    x_of = local_block // quarter % quarters
    place = (
        (core_of ^ core) * half
        + (local_block % quarter) * peers
        + peer_base(core_of, entry_owner // side, entry_owner % side)
        + x_of * side
    )
    places = jnp.arange(2 * half, dtype=jnp.int32)
    b_mat = (place[:, None] == places[None, :]).astype(BF16)
    bt = (places[:, None] == place[None, :]).astype(BF16)

    def exchange(v):
        return lax.ppermute(v, "core", [(0, 1), (1, 0)])

    def rank(x, c, z, y):
        return ((x * 2 + c) * side + z) * side + y

    xs, ss = range(quarters), range(side)
    all_peers = [[rank(x, 0, z, y) for z in ss for x in xs for y in ss]]
    all_peers += [[rank(x, 1, z, y) for y in ss for x in xs for z in ss]]
    first_axis = [[rank(x, 0, z, y) for z in ss] for x in xs for y in ss]
    first_axis += [[rank(x, 1, z, y) for y in ss] for x in xs for z in ss]
    last_axes = [[rank(x, 0, z, y) for x in xs for y in ss] for z in ss]
    last_axes += [[rank(x, 1, z, y) for x in xs for z in ss] for y in ss]

    def send(v, groups):
        shaped = v.reshape(len(groups[0]), -1, BLK)
        got = lax.all_to_all(
            shaped, ("x", "core", "z", "y"), 0, 0, axis_index_groups=groups, tiled=False
        )
        return got.reshape(-1, BLK)

    def to_peers(v):
        return send(v, all_peers)

    stride = NP * quarter + EXTRA
    msg = shape_of(peers * stride, BLK)
    def reduce_parts(other, pblk, count, rows, extra=None):
        theirs = exchange(other)
        return half_call(pblk, bt, peers, count, rows, extra) + theirs

    def fetch(msg_out):
        mine = to_peers(msg_out)
        other = exchange(mine)
        return pick_call(b_mat, mine, peers), mine, other

    other, pblk, inv, pg = setup_call(pos, jac, jp, oc, op, pt_grad, pt_damp, bt, peers)
    part = send(reduce_parts(other, pblk, 2 * NP, 2 * NP * quarter), first_axis)
    part = call(
        functools.partial(sum_kernel, side), "sum_step", shape_of(part.shape[0] // side, BLK), (part,)
    )
    got = send(part, last_axes)
    msg_out, state = call(
        functools.partial(start_kernel, peers, peers // side, quarter),
        "start_step",
        [msg, shape_of(4, stride, BLK)],
        (pos, got, cam_grad, cam_damp),
        [pltpu.VMEM((2, stride, BLK), F32)],
        smem=(0,),
    )
    pick, mine, other = fetch(msg_out)
    other, pblk, sol0, held0, norm, extra, proj0 = operator_call(
        pos, jac, jp, oc, op, b_mat, bt, inv, pick, mine, other, peers, side
    )
    got = to_peers(reduce_parts(other, pblk, NP, stride, extra))
    msg_out, image = call(
        functools.partial(image_kernel, peers), "image_step", [msg, shape_of(stride, BLK)], (got, state)
    )
    pick, mine, other = fetch(msg_out)
    other, pblk, sol1, held1, curv, extra = operator_call(
        pos, jac, jp, oc, op, b_mat, bt, inv, pick, mine, other, peers, side, (proj0, state, image, norm)
    )
    got = to_peers(reduce_parts(other, pblk, NP, stride, extra))
    resid, scal = call(
        functools.partial(last_kernel, peers),
        "last_step",
        [shape_of(stride, BLK), shape_of(24, BLK)],
        (got, state, image, norm, curv),
    )
    pieces = [resid] + [
        lax.ppermute(resid, "x", [(i, (i + s) % quarters) for i in range(quarters)])
        for s in range(1, quarters)
    ]
    cam_step, pt_step = call(
        step_kernel,
        "result_step",
        [shape_of(NP, shard), shape_of(3, pt_grad.shape[1])],
        (pos, scal, held0, held1, pg, sol0, sol1),
        [pltpu.VMEM((3 * pg.shape[1], BLK), F32), pltpu.VMEM((stride, BLK), F32)],
        smem=(0,),
        cost=pl.CostEstimate(flops=10**9, bytes_accessed=4 * 10**6, transcendentals=0),
    )
    row = jnp.stack(pieces)
    cam_resid = call(
        resid_kernel,
        "result_resid",
        shape_of(NP, shard),
        (pos, jnp.stack([row, exchange(row)])),
        [pltpu.VMEM((stride, BLK), F32)],
        smem=(0,),
    )
    return cam_step, cam_resid, pt_step


def solution(mesh):
    fine = Mesh(mesh.devices.reshape(4, 2, 4, 4), ("x", "core", "z", "y"))
    pts, cam = ("x", "core"), ("z", "y")
    every = pts + cam
    in_specs = (
        P(None, every, None),
        P(None, every, None),
        P(every, None),
        P(every, None),
        P(every),
        P(every, None),
        P(None, cam),
        P(None, cam),
        P(None, every),
        P(None, every),
    )
    out_specs = (P(None, cam), P(None, cam), P(None, every))
    return jax.shard_map(local, mesh=fine, in_specs=in_specs, out_specs=out_specs, check_vma=False)
```

```python
import functools

import jax
import jax.numpy as jnp
from jax import lax
from jax.experimental import pallas as pl
from jax.experimental.pallas import tpu as pltpu
from jax.sharding import Mesh, PartitionSpec as P

BLK = 128
BPT = 8
NP = 9
CHUNK_PEERS = 16
EXTRA = 4
F32 = jnp.float32
BF16 = jnp.bfloat16
GROUP = 128
VMEM_LIMIT = 24 * 1024 * 1024


def split3(x):
    hi = x.astype(BF16).astype(F32)
    rest = x - hi
    mid = rest.astype(BF16).astype(F32)
    return hi, mid, rest - mid


def apply_three(inverse, values):
    first = inverse[0] * values[0] + inverse[1] * values[1] + inverse[2] * values[2]
    second = inverse[1] * values[0] + inverse[3] * values[1] + inverse[4] * values[2]
    third = inverse[2] * values[0] + inverse[4] * values[1] + inverse[5] * values[2]
    return [first, second, third]


def lane_pick(table, idx):
    return jnp.take_along_axis(table, idx, axis=1, mode="promise_in_bounds")


def onehot_rows(idx_row):
    rows = lax.broadcasted_iota(jnp.int32, (BLK, BLK), 0)
    return jnp.where(rows == idx_row, 1.0, 0.0).astype(BF16)


NT = (((1,), (1,)), ((), ()))


def point_stage_rows(count):
    return -(-3 * count // 16) * 16


def cam_stage_rows(count):
    whole = count // 8 * 8
    return -(-(3 * whole + 8) // 16) * 16


def cam_sum_rows(count):
    return count // 8 * 8 + 8


def point_scatter(stage, vals, idx_ref, t, col):
    count = len(vals)
    group = vals[0].shape[0]
    high = point_stage_rows(count)
    for j, val in enumerate(vals):
        for s, piece in enumerate(split3(val)):
            row = s * count + j
            stage[row * group : (row + 1) * group, :] = piece
    tiles = group // BPT
    for u in range(0, tiles, 2):
        lhs, rhs = [], []
        for b in range(BPT):
            pair = [(u + v) * BPT + b for v in range(2)]
            lhs.append(
                jnp.concatenate([stage[pl.ds(c, high, stride=group), :] for c in pair], axis=0).astype(BF16)
            )
            rhs.append(
                jnp.concatenate([onehot_rows(idx_ref[pl.ds(t * group + c, 1), :]) for c in pair], axis=0)
            )
        res = lax.dot_general(
            jnp.concatenate(lhs, axis=1), jnp.concatenate(rhs, axis=1), NT, preferred_element_type=F32
        )
        for v in range(2):
            start = pl.multiple_of((t * tiles + u + v) * high, 16)
            col[pl.ds(start, high), :] = res[v * high : (v + 1) * high, v * BLK : (v + 1) * BLK]


def point_sums(col, count, tiles):
    high = point_stage_rows(count)
    out = []
    for j in range(count):
        pieces = [col[pl.ds(s * count + j, tiles, stride=high), :] for s in range(3)]
        out.append(pieces[0] + (pieces[1] + pieces[2]))
    return out


def cam_scatter(stage, vals, idx_ref, t, pblk):
    count = len(vals)
    whole = count // 8 * 8
    rest = count - whole
    group = vals[0].shape[0]
    high = cam_stage_rows(count)
    keep = cam_sum_rows(count)
    for k, val in enumerate(vals):
        for s, piece in enumerate(split3(val)):
            row = s * whole + k if k < whole else 3 * whole + s * rest + k - whole
            stage[row * group : (row + 1) * group, :] = piece
    for b in range(0, group, 2):
        lhs = jnp.concatenate(
            [stage[pl.ds(b + v, high, stride=group), :] for v in range(2)], axis=0
        ).astype(BF16)
        rhs = jnp.concatenate(
            [onehot_rows(idx_ref[pl.ds(t * group + b + v, 1), :]) for v in range(2)], axis=0
        )
        both = lax.dot_general(lhs, rhs, NT, preferred_element_type=F32)
        for v in range(2):
            res = both[v * high : (v + 1) * high, v * BLK : (v + 1) * BLK]
            start = pl.multiple_of((t * group + b + v) * keep, 8)
            pblk[pl.ds(start, whole), :] = (
                res[0:whole] + res[whole : 2 * whole] + res[2 * whole : 3 * whole]
            )
            pblk[pl.ds(start + whole, 8), :] = res[3 * whole : 3 * whole + 8]


def pieces_wide(arrays):
    return jnp.concatenate([p for x in arrays for p in split3(x)], axis=1).astype(BF16)


def pieces_sum(res, i):
    res = res[:, 3 * i * BLK : 3 * (i + 1) * BLK]
    return res[:, :BLK] + res[:, BLK : 2 * BLK] + res[:, 2 * BLK :]


def blocks_to_dense(pblk, bt_ref, h, count, outs):
    nblocks = bt_ref.shape[1]
    half = bt_ref.shape[0] // 2
    sub = CHUNK_PEERS
    peers = len(outs) * sub
    quarter = half // peers
    stride = outs[0].shape[0] // sub
    whole = count // 8 * 8
    rest = count - whole
    keep = cam_sum_rows(count)
    for k0 in range(0, count, 2):
        ks = range(k0, min(k0 + 2, count))
        arrays = []
        for k in ks:
            if k < whole:
                arrays.append(pblk[pl.ds(k, nblocks, stride=keep), :])
            else:
                p = [pblk[pl.ds(k + s * rest, nblocks, stride=keep), :] for s in range(3)]
                arrays.append(p[0] + (p[1] + p[2]))
        both = jnp.dot(
            bt_ref[h * half : (h + 1) * half, :], pieces_wide(arrays), preferred_element_type=F32
        )
        for n, k in enumerate(ks):
            res = pieces_sum(both, n)
            for i in range(quarter):
                for s, out in enumerate(outs):
                    first = i * peers + s * sub
                    out[pl.ds(k * quarter + i, sub, stride=stride), :] = res[first : first + sub]


def half_kernel(count, chunks, *refs):
    pblk, bt = refs[:2]
    outs = refs[-chunks:]
    blocks_to_dense(pblk, bt, 0, count, outs)
    if len(refs) > chunks + 2:
        fill_extra(outs, [refs[2][i : i + 1, :] for i in range(EXTRA)])


def half_call(pblk, bt, chunks, count, stride, extra=()):
    return call(
        functools.partial(half_kernel, count, chunks),
        "own_half",
        [shape_of(CHUNK_PEERS * stride, BLK)] * chunks,
        (pblk, bt) + extra,
        cost=pl.CostEstimate(flops=10**9, bytes_accessed=4 * 10**6, transcendentals=0),
    )


def pick_half(b_ref, h, msgs, k0, count):
    sub = CHUNK_PEERS
    half = b_ref.shape[1] // 2
    quarter = half // (sub * len(msgs))
    stride = msgs[0].shape[0] // sub
    arrays = [
        jnp.concatenate(
            [msg[pl.ds(k * quarter + i, sub, stride=stride), :] for i in range(quarter) for msg in msgs],
            axis=0,
        )
        for k in range(k0, k0 + count)
    ]
    both = jnp.dot(
        b_ref[:, h * half : (h + 1) * half], pieces_wide(arrays), preferred_element_type=F32
    )
    return [pieces_sum(both, n) for n in range(count)]


def pick_kernel(b_mat, *refs):
    pick = refs[-1]
    for k0 in range(0, NP, 2):
        count = min(2, NP - k0)
        for n, value in enumerate(pick_half(b_mat, 0, refs[:-1], k0, count)):
            pick[k0 + n] = value


def pick_call(b_mat, mine):
    return call(
        pick_kernel,
        "pick_own_half",
        shape_of(NP, b_mat.shape[0], BLK),
        (b_mat,) + mine,
        cost=pl.CostEstimate(flops=10**9, bytes_accessed=4 * 10**6, transcendentals=0),
    )


def fill_extra(msgs, rows):
    for msg in msgs:
        stride = msg.shape[0] // CHUNK_PEERS
        for i, row in enumerate(rows):
            msg[pl.ds(stride - EXTRA + i, CHUNK_PEERS, stride=stride), :] = jnp.broadcast_to(
                row, (CHUNK_PEERS, BLK)
            )


def extra_sum(msgs, index):
    stride = msgs[0].shape[0] // CHUNK_PEERS
    rows = [msg[pl.ds(stride - EXTRA + index, CHUNK_PEERS, stride=stride), :] for msg in msgs]
    total = jnp.sum(functools.reduce(jnp.add, rows), axis=0, keepdims=True)
    return jnp.sum(total, axis=1, keepdims=True)


def spread_points(ref, t, group, pidx):
    tiles = group // BPT
    out = []
    for j in range(3):
        table = [
            jnp.broadcast_to(ref[j, pl.ds(t * tiles + u, 1), :], (BPT, BLK)) for u in range(tiles)
        ]
        out.append(lane_pick(jnp.concatenate(table, axis=0), pidx))
    return out


def terms_kernel(pos, jp, op, col, stage):
    nblocks = op.shape[0]

    def terms(t, carry):
        rows = pl.ds(pl.multiple_of(t * GROUP, GROUP), GROUP)
        a = [jp[j, rows, :] for j in range(6)]
        vals = [
            a[p] * a[q] + a[3 + p] * a[3 + q]
            for p, q in [(0, 0), (0, 1), (0, 2), (1, 1), (1, 2), (2, 2)]
        ]
        point_scatter(stage, vals, op, t, col)
        return carry

    lax.fori_loop(0, nblocks // GROUP, terms, 0)


def setup_kernel(
    chunks, col, jac, jp, oc, op, pt_grad, pt_damp, bt, *refs
):
    others = refs[:chunks]
    pblk, inv_out, pg_out, stage2, grad_rows, damp_rows = refs[chunks:]
    nblocks = jac.shape[1]
    tiles = nblocks // BPT
    for t in range(tiles):
        lanes = slice(t * BLK, (t + 1) * BLK)
        grad_rows[pl.ds(t, 3, stride=tiles), :] = pt_grad[:, lanes]
        damp_rows[pl.ds(t, 3, stride=tiles), :] = pt_damp[:, lanes]
    grad = [grad_rows[j * tiles : (j + 1) * tiles, :] for j in range(3)]
    damp = [damp_rows[j * tiles : (j + 1) * tiles, :] for j in range(3)]

    entry = point_sums(col, 6, tiles)
    c00 = entry[0] + damp[0]
    c01 = entry[1]
    c02 = entry[2]
    c11 = entry[3] + damp[1]
    c12 = entry[4]
    c22 = entry[5] + damp[2]
    a00 = c11 * c22 - c12 * c12
    a01 = c02 * c12 - c01 * c22
    a02 = c01 * c12 - c02 * c11
    a11 = c00 * c22 - c02 * c02
    a12 = c01 * c02 - c00 * c12
    a22 = c00 * c11 - c01 * c01
    recip = 1.0 / (c00 * a00 + c01 * a01 + c02 * a02)
    inv = [a * recip for a in (a00, a01, a02, a11, a12, a22)]
    for j in range(6):
        inv_out[j] = inv[j]
    pg = apply_three(inv, grad)
    for j in range(3):
        pg_out[j] = pg[j]

    def rhs_terms(t, carry):
        rows = pl.ds(pl.multiple_of(t * GROUP, GROUP), GROUP)
        g = spread_points(pg_out, t, GROUP, op[rows, :])
        c0 = jp[0, rows, :] * g[0] + jp[1, rows, :] * g[1] + jp[2, rows, :] * g[2]
        c1 = jp[3, rows, :] * g[0] + jp[4, rows, :] * g[1] + jp[5, rows, :] * g[2]
        vals = []
        diag = []
        for k in range(NP):
            j0 = jac[k, rows, :]
            j1 = jac[NP + k, rows, :]
            vals.append(j0 * c0 + j1 * c1)
            diag.append(j0 * j0 + j1 * j1)
        cam_scatter(stage2, vals + diag, oc, t, pblk)
        return carry

    lax.fori_loop(0, nblocks // GROUP, rhs_terms, 0)
    blocks_to_dense(pblk, bt, 1, 2 * NP, others)


def call(kernel, name, out_shape, operands, scratch=(), smem=(), cost=None):
    return pl.pallas_call(
        kernel,
        in_specs=[
            pl.BlockSpec(memory_space=pltpu.SMEM if i in smem else pltpu.VMEM)
            for i in range(len(operands))
        ],
        out_shape=out_shape,
        scratch_shapes=scratch,
        compiler_params=pltpu.CompilerParams(vmem_limit_bytes=VMEM_LIMIT),
        cost_estimate=cost,
        name=name,
    )(*operands)


def shape_of(*dims):
    return jax.ShapeDtypeStruct(dims, F32)


def setup_call(pos, jac, jp, oc, op, pt_grad, pt_damp, bt, chunks):
    nblocks = jac.shape[1]
    tiles = nblocks // BPT
    col = call(
        terms_kernel,
        "point_terms",
        shape_of(tiles * point_stage_rows(6), BLK),
        (pos, jp, op),
        [pltpu.VMEM((point_stage_rows(6) * GROUP, BLK), F32)],
        smem=(0,),
        cost=pl.CostEstimate(flops=4 * 10**9, bytes_accessed=10**7, transcendentals=0),
    )
    return call(
        functools.partial(setup_kernel, chunks),
        "setup_pass",
        [
            *[shape_of(NP * bt.shape[0] // chunks, BLK)] * chunks,
            shape_of(nblocks * cam_sum_rows(2 * NP), BLK),
            shape_of(6, tiles, BLK),
            shape_of(3, tiles, BLK),
        ],
        (col, jac, jp, oc, op, pt_grad, pt_damp, bt),
        [
            pltpu.VMEM((cam_stage_rows(2 * NP) * GROUP, BLK), F32),
            pltpu.VMEM((3 * tiles, BLK), F32),
            pltpu.VMEM((3 * tiles, BLK), F32),
        ],
    )


def operator_kernel(second, chunks, *refs):
    pos, jac, jp, oc, op, b_mat, bt, inv, pick_in = refs[:9]
    mine_in, other_in = refs[9 : 9 + chunks], refs[9 + chunks : 9 + 2 * chunks]
    refs = refs[9 + 2 * chunks :]
    if second:
        proj_in, state, image, norm_in = refs[:4]
        refs = refs[4:]
    others = refs[:chunks]
    pblk, sol_out, held_out, scal_out, extra = refs[chunks : chunks + 5]
    refs = refs[chunks + 5 :]
    if second:
        stage, stage2, pick, col, proj = refs
    else:
        proj, stage, stage2, pick, col = refs
    nblocks = jac.shape[1]
    tiles = nblocks // BPT
    stride = mine_in[0].shape[0] // CHUNK_PEERS
    for k0 in range(0, NP, 2):
        count = min(2, NP - k0)
        for n, value in enumerate(pick_half(b_mat, 1, other_in, k0, count)):
            pick[k0 + n] = pick_in[k0 + n] + value
    for h, msgs in enumerate((mine_in, other_in)):
        for x in range(CHUNK_PEERS // chunks):
            start = pl.multiple_of((x * chunks + pos[2 + h]) * stride, 8)
            held_out[h, x] = msgs[0][pl.ds(start, stride), :]
    total = extra_sum(mine_in + other_in, 0)
    if second:
        norm = norm_in[0:1, 0:1]
        step_len = norm / total
        scal_out[...] = jnp.broadcast_to(total, (8, BLK))
        rhs, precond, damp, direction = (state[i] for i in range(4))
        resid = rhs - step_len * image[...]
        z = resid / precond
        keep = lax.broadcasted_iota(jnp.int32, (stride, BLK), 0) < stride - EXTRA

        def lanes(v):
            return jnp.sum(jnp.where(keep, v, 0.0), axis=0, keepdims=True)

        owner_sums = [lanes(damp * z * z), lanes(damp * z * direction), lanes(resid * z)]
    else:
        scal_out[...] = jnp.broadcast_to(total, (8, BLK))

    def project(t, carry):
        rows = pl.ds(pl.multiple_of(t * GROUP, GROUP), GROUP)
        cidx = oc[rows, :]
        p0 = jnp.zeros((GROUP, BLK), F32)
        p1 = jnp.zeros((GROUP, BLK), F32)
        for k in range(NP):
            v = lane_pick(pick[k, rows, :], cidx)
            p0 += jac[k, rows, :] * v
            p1 += jac[NP + k, rows, :] * v
        if second:
            p0 = proj_in[0, rows, :] - step_len * p0
            p1 = proj_in[1, rows, :] - step_len * p1
        proj[0, rows, :] = p0
        proj[1, rows, :] = p1
        vals = [jp[j, rows, :] * p0 + jp[3 + j, rows, :] * p1 for j in range(3)]
        point_scatter(stage, vals, op, t, col)
        return carry

    lax.fori_loop(0, nblocks // GROUP, project, 0)
    sol = apply_three([inv[j] for j in range(6)], point_sums(col, 3, tiles))
    for j in range(3):
        sol_out[j] = sol[j]

    def correct(t, carry):
        rows = pl.ds(pl.multiple_of(t * GROUP, GROUP), GROUP)
        g = spread_points(sol_out, t, GROUP, op[rows, :])
        p0 = proj[0, rows, :]
        p1 = proj[1, rows, :]
        c0 = p0 - (jp[0, rows, :] * g[0] + jp[1, rows, :] * g[1] + jp[2, rows, :] * g[2])
        c1 = p1 - (jp[3, rows, :] * g[0] + jp[4, rows, :] * g[1] + jp[5, rows, :] * g[2])
        if second:
            zz, zd = carry
            zz = zz + (p0 * c0 + p1 * c1)
            zd = zd + (proj_in[0, rows, :] * c0 + proj_in[1, rows, :] * c1)
            carry = (zz, zd)
        vals = [jac[k, rows, :] * c0 + jac[NP + k, rows, :] * c1 for k in range(NP)]
        cam_scatter(stage2, vals, oc, t, pblk)
        return carry

    zero = jnp.zeros((GROUP, BLK), F32)
    sums = lax.fori_loop(0, nblocks // GROUP, correct, (zero, zero) if second else 0)
    blocks_to_dense(pblk, bt, 1, NP, others)
    rows = []
    if second:
        rows = [
            jnp.sum(sums[0], axis=0, keepdims=True) + owner_sums[0],
            jnp.sum(sums[1], axis=0, keepdims=True) + owner_sums[1],
            owner_sums[2],
        ]
    rows += [jnp.zeros((1, BLK), F32)] * (EXTRA - len(rows))
    fill_extra(others, rows)
    extra[...] = jnp.concatenate(rows, axis=0)


def operator_call(pos, jac, jp, oc, op, b_mat, bt, inv, pick, mine, other, later=()):
    nblocks = jac.shape[1]
    tiles = nblocks // BPT
    chunks = len(mine)
    stride = mine[0].shape[0] // CHUNK_PEERS
    proj = [] if later else [shape_of(2, nblocks, BLK)]
    proj_scratch = [pltpu.VMEM((2, nblocks, BLK), F32)] if later else []
    return call(
        functools.partial(operator_kernel, bool(later), chunks),
        "second_pass" if later else "first_pass",
        [
            *[shape_of(*mine[0].shape)] * chunks,
            shape_of(nblocks * cam_sum_rows(NP), BLK),
            shape_of(3, tiles, BLK),
            shape_of(2, CHUNK_PEERS // chunks, stride, BLK),
            shape_of(8, BLK),
            shape_of(EXTRA, BLK),
        ]
        + proj,
        (pos, jac, jp, oc, op, b_mat, bt, inv, pick) + mine + other + later,
        [
            pltpu.VMEM((point_stage_rows(3) * GROUP, BLK), F32),
            pltpu.VMEM((cam_stage_rows(NP) * GROUP, BLK), F32),
            pltpu.VMEM((NP, nblocks, BLK), F32),
            pltpu.VMEM((tiles * point_stage_rows(3), BLK), F32),
        ]
        + proj_scratch,
        smem=(0,),
    )


def message_sum(got):
    rows = got.shape[0] // CHUNK_PEERS
    total = got[0:rows, :]
    for d in range(1, CHUNK_PEERS):
        total = total + got[d * rows : (d + 1) * rows, :]
    return total


def send_all(msg, values, scalar):
    stride = values.shape[0]
    data = stride - EXTRA
    row = lax.broadcasted_iota(jnp.int32, values.shape, 0)
    lanes = jnp.sum(jnp.where(row < data, scalar, 0.0), axis=0, keepdims=True)
    out = jnp.where(row < data, values, jnp.where(row == data, lanes, 0.0))
    for d in range(CHUNK_PEERS):
        msg[d * stride : (d + 1) * stride, :] = out


def start_kernel(quarter, pos, got, grad, damp, msg, state, rows):
    data = NP * quarter
    rows[...] = jnp.ones(rows.shape, F32)
    for i in range(quarter):
        lanes = pl.ds(pl.multiple_of((pos[1] * quarter + i) * BLK, BLK), BLK)
        rows[0, pl.ds(i, NP, stride=quarter), :] = grad[:, lanes]
        rows[1, pl.ds(i, NP, stride=quarter), :] = damp[:, lanes]
    total = message_sum(got)
    ones = jnp.ones((EXTRA, BLK), F32)
    rhs = rows[0] - jnp.concatenate([total[:data], ones], axis=0)
    precond = rows[1] + jnp.concatenate([total[data:], ones], axis=0)
    direction = rhs / precond
    state[0] = rhs
    state[1] = precond
    state[2] = rows[1]
    state[3] = direction
    send_all(msg, direction, rhs * direction)


def image_kernel(got, state, msg, image):
    direction = state[3]
    value = state[2] * direction + message_sum(got)
    image[...] = value
    send_all(msg, value / state[1], direction * value)


def last_kernel(got, state, image, norm_in, curv_in, resid_out, scal_out):
    norm = norm_in[0:1, 0:1]
    curv = curv_in[0:1, 0:1]
    step0 = norm / curv
    total = message_sum(got)
    stride = total.shape[0]
    sums = jnp.sum(total[stride - EXTRA :], axis=1, keepdims=True)
    zz, zd, norm1 = (sums[i : i + 1] for i in range(3))
    beta = norm1 / norm
    curv1 = zz + 2.0 * beta * zd + beta * beta * curv
    step1 = norm1 / curv1
    resid = state[0] - step0 * image[...]
    z = resid / state[1]
    image1 = (state[2] * z + total) + beta * image[...]
    resid_out[...] = resid - step1 * image1
    for i, s in enumerate((step0, step1, beta)):
        scal_out[i * 8 : (i + 1) * 8, :] = jnp.broadcast_to(s, (8, BLK))


def step_kernel(pos, scal, held0, held1, pg, sol0, sol1, cam_out, pt_out, pts_rows, cams_rows):
    step0, step1, beta = (scal[i * 8 : i * 8 + 1, 0:1] for i in range(3))
    tiles = pg.shape[1]
    for j in range(3):
        first = sol0[j]
        pts_rows[j * tiles : (j + 1) * tiles, :] = (
            pg[j] - step0 * first - step1 * (sol1[j] + beta * first)
        )
    for t in range(tiles):
        pt_out[:, t * BLK : (t + 1) * BLK] = pts_rows[pl.ds(t, 3, stride=tiles), :]
    quarters, stride = held0.shape[1], held0.shape[2]
    quarter = (stride - EXTRA) // NP
    for h in range(2):
        for x in range(quarters):
            d0 = held0[h, x]
            z = d0 - step0 * held1[h, x]
            cams_rows[...] = step0 * d0 + step1 * (z + beta * d0)
            put_cams(cam_out, cams_rows, pos[0] ^ h, x, quarters, quarter)


def put_cams(out, rows, core, x, quarters, quarter):
    for i in range(quarter):
        block = (core * quarters + x) * quarter + i
        lanes = pl.ds(pl.multiple_of(block * BLK, BLK), BLK)
        out[:, lanes] = rows[pl.ds(i, NP, stride=quarter), :]


def resid_kernel(pos, pieces, out, rows):
    quarters, stride = pieces.shape[1], pieces.shape[2]
    quarter = (stride - EXTRA) // NP
    for h in range(2):
        for s in range(quarters):
            x = (pos[4] + quarters - s) % quarters
            rows[...] = pieces[h, s]
            put_cams(out, rows, pos[0] ^ h, x, quarters, quarter)


def local(jac, jp, oc, op, entry, cov, cam_grad, cam_damp, pt_grad, pt_damp):
    quarters = lax.axis_size("x")
    owners = lax.axis_size("z") * lax.axis_size("y")
    peers = quarters * owners
    core = lax.axis_index("core")
    x = lax.axis_index("x")
    side = lax.axis_size("z")
    z, y = lax.axis_index("z"), lax.axis_index("y")

    def peer_base(of_core, owner_z, owner_y):
        chunk = jnp.where(of_core == 0, z - owner_z, y - owner_y) % side
        return chunk * CHUNK_PEERS + jnp.where(of_core == 0, owner_y, owner_z)

    pos = jnp.stack(
        [
            core,
            core * quarters + x,
            jnp.where(core == 0, y, z),
            jnp.where(core == 0, z, y),
            x,
        ]
    ).astype(jnp.int32)
    per_owner = cov.shape[1]
    shard = cam_grad.shape[1]
    quarter = shard // BLK // 2 // quarters
    half = peers * quarter

    entry_owner = entry // per_owner
    hit = (entry_owner[:, None, None] == jnp.arange(owners, dtype=jnp.int32)[None, :, None]) & (
        (entry % per_owner)[:, None, None] == jnp.arange(per_owner, dtype=jnp.int32)[None, None, :]
    )
    local_block = jnp.sum(jnp.where(hit, cov[None], 0), axis=(1, 2))
    core_of = local_block // (quarters * quarter)
    x_of = local_block // quarter % quarters
    place = (
        (core_of ^ core) * half
        + (local_block % quarter) * peers
        + peer_base(core_of, entry_owner // side, entry_owner % side)
        + x_of * side
    )
    places = jnp.arange(2 * half, dtype=jnp.int32)
    b_mat = (place[:, None] == places[None, :]).astype(BF16)
    bt = (places[:, None] == place[None, :]).astype(BF16)

    def exchange(v):
        return lax.ppermute(v, "core", [(0, 1), (1, 0)])

    def rank(x, c, z, y):
        return ((x * 2 + c) * side + z) * side + y

    xs, ss = range(quarters), range(side)
    every = ("x", "core", "z", "y")
    last_axes = [[rank(x, 0, z, y) for x in xs for y in ss] for z in ss]
    last_axes += [[rank(x, 1, z, y) for x in xs for z in ss] for y in ss]

    def shift(v, s):
        pairs = []
        for x in xs:
            for z in ss:
                for y in ss:
                    pairs.append((rank(x, 0, z, y), rank(x, 0, (z + s) % side, y)))
                    pairs.append((rank(x, 1, z, y), rank(x, 1, z, (y + s) % side)))
        return lax.ppermute(v, every, pairs)

    def over_last(v):
        shaped = v.reshape(CHUNK_PEERS, -1, BLK)
        got = lax.all_to_all(shaped, every, 0, 0, axis_index_groups=last_axes, tiled=False)
        return got.reshape(-1, BLK)

    stride = NP * quarter + EXTRA
    msg = shape_of(CHUNK_PEERS * stride, BLK)
    chunk_order = [*range(1, side), 0]

    def reduce_parts(others, pblk, count, rows, *extra):
        theirs = {s: exchange(others[s]) for s in chunk_order}
        own = half_call(pblk, bt, side, count, rows, extra)
        moved = [shift(own[s] + theirs[s], -s) for s in chunk_order[:-1]]
        total = own[0] + theirs[0]
        for part in moved:
            total = total + part
        return over_last(total)

    def fetch(msg_out):
        first = over_last(msg_out)
        mine = (first,) + tuple(shift(first, s) for s in range(1, side))
        other = tuple(exchange(part) for part in mine)
        return pick_call(b_mat, mine), mine, other

    *others, pblk, inv, pg = setup_call(pos, jac, jp, oc, op, pt_grad, pt_damp, bt, side)
    got = reduce_parts(others, pblk, 2 * NP, 2 * NP * quarter)
    msg_out, state = call(
        functools.partial(start_kernel, quarter),
        "start_step",
        [msg, shape_of(4, stride, BLK)],
        (pos, got, cam_grad, cam_damp),
        [pltpu.VMEM((2, stride, BLK), F32)],
        smem=(0,),
    )
    pick, mine, other = fetch(msg_out)
    *others, pblk, sol0, held0, norm, extra, proj0 = operator_call(
        pos, jac, jp, oc, op, b_mat, bt, inv, pick, mine, other
    )
    got = reduce_parts(others, pblk, NP, stride, extra)
    msg_out, image = call(
        image_kernel, "image_step", [msg, shape_of(stride, BLK)], (got, state)
    )
    pick, mine, other = fetch(msg_out)
    *others, pblk, sol1, held1, curv, extra = operator_call(
        pos, jac, jp, oc, op, b_mat, bt, inv, pick, mine, other, (proj0, state, image, norm)
    )
    got = reduce_parts(others, pblk, NP, stride, extra)
    resid, scal = call(
        last_kernel,
        "last_step",
        [shape_of(stride, BLK), shape_of(24, BLK)],
        (got, state, image, norm, curv),
    )
    pieces = [resid] + [
        lax.ppermute(resid, "x", [(i, (i + s) % quarters) for i in range(quarters)])
        for s in range(1, quarters)
    ]
    cam_step, pt_step = call(
        step_kernel,
        "result_step",
        [shape_of(NP, shard), shape_of(3, pt_grad.shape[1])],
        (pos, scal, held0, held1, pg, sol0, sol1),
        [pltpu.VMEM((3 * pg.shape[1], BLK), F32), pltpu.VMEM((stride, BLK), F32)],
        smem=(0,),
        cost=pl.CostEstimate(flops=10**9, bytes_accessed=4 * 10**6, transcendentals=0),
    )
    row = jnp.stack(pieces)
    cam_resid = call(
        resid_kernel,
        "result_resid",
        shape_of(NP, shard),
        (pos, jnp.stack([row, exchange(row)])),
        [pltpu.VMEM((stride, BLK), F32)],
        smem=(0,),
    )
    return cam_step, cam_resid, pt_step


def solution(mesh):
    fine = Mesh(mesh.devices.reshape(4, 2, 4, 4), ("x", "core", "z", "y"))
    pts, cam = ("x", "core"), ("z", "y")
    every = pts + cam
    in_specs = (
        P(None, every, None),
        P(None, every, None),
        P(every, None),
        P(every, None),
        P(every),
        P(every, None),
        P(None, cam),
        P(None, cam),
        P(None, every),
        P(None, every),
    )
    out_specs = (P(None, cam), P(None, cam), P(None, every))
    return jax.shard_map(local, mesh=fine, in_specs=in_specs, out_specs=out_specs, check_vma=False)
```

```python
import functools

import jax
import jax.numpy as jnp
from jax import lax
from jax.experimental import pallas as pl
from jax.experimental.pallas import tpu as pltpu
from jax.sharding import Mesh, PartitionSpec as P

BLK = 128
BPT = 8
NP = 9
CHUNK_PEERS = 16
EXTRA = 4
F32 = jnp.float32
BF16 = jnp.bfloat16
GROUP = 128
VMEM_LIMIT = 24 * 1024 * 1024


def split3(x):
    hi = x.astype(BF16).astype(F32)
    rest = x - hi
    mid = rest.astype(BF16).astype(F32)
    return hi, mid, rest - mid


def apply_three(inverse, values):
    first = inverse[0] * values[0] + inverse[1] * values[1] + inverse[2] * values[2]
    second = inverse[1] * values[0] + inverse[3] * values[1] + inverse[4] * values[2]
    third = inverse[2] * values[0] + inverse[4] * values[1] + inverse[5] * values[2]
    return [first, second, third]


def lane_pick(table, idx):
    return jnp.take_along_axis(table, idx, axis=1, mode="promise_in_bounds")


def onehot_rows(idx_row):
    rows = lax.broadcasted_iota(jnp.int32, (BLK, BLK), 0)
    return jnp.where(rows == idx_row, 1.0, 0.0).astype(BF16)


NT = (((1,), (1,)), ((), ()))


def aligned(index, multiple):
    return index if isinstance(index, int) else pl.multiple_of(index, multiple)


def steps(count, body, carry):
    for t in range(count):
        carry = body(t, carry)
    return carry


def point_stage_rows(count):
    return -(-3 * count // 16) * 16


def cam_stage_rows(count):
    whole = count // 8 * 8
    return -(-(3 * whole + 8) // 16) * 16


def cam_sum_rows(count):
    return count // 8 * 8 + 8


def point_scatter(stage, vals, idx_ref, t, col):
    count = len(vals)
    group = vals[0].shape[0]
    high = point_stage_rows(count)
    for j, val in enumerate(vals):
        for s, piece in enumerate(split3(val)):
            row = s * count + j
            stage[row * group : (row + 1) * group, :] = piece
    tiles = group // BPT
    for u in range(0, tiles, 2):
        lhs, rhs = [], []
        for b in range(BPT):
            pair = [(u + v) * BPT + b for v in range(2)]
            lhs.append(
                jnp.concatenate([stage[pl.ds(c, high, stride=group), :] for c in pair], axis=0).astype(BF16)
            )
            rhs.append(
                jnp.concatenate([onehot_rows(idx_ref[pl.ds(t * group + c, 1), :]) for c in pair], axis=0)
            )
        res = lax.dot_general(
            jnp.concatenate(lhs, axis=1), jnp.concatenate(rhs, axis=1), NT, preferred_element_type=F32
        )
        for v in range(2):
            start = aligned((t * tiles + u + v) * high, 16)
            col[pl.ds(start, high), :] = res[v * high : (v + 1) * high, v * BLK : (v + 1) * BLK]


def point_sums(col, count, tiles):
    high = point_stage_rows(count)
    out = []
    for j in range(count):
        pieces = [col[pl.ds(s * count + j, tiles, stride=high), :] for s in range(3)]
        out.append(pieces[0] + (pieces[1] + pieces[2]))
    return out


def cam_scatter(stage, vals, idx_ref, t, pblk):
    count = len(vals)
    whole = count // 8 * 8
    rest = count - whole
    group = vals[0].shape[0]
    high = cam_stage_rows(count)
    keep = cam_sum_rows(count)
    for k, val in enumerate(vals):
        for s, piece in enumerate(split3(val)):
            row = s * whole + k if k < whole else 3 * whole + s * rest + k - whole
            stage[row * group : (row + 1) * group, :] = piece
    for b in range(0, group, 2):
        lhs = jnp.concatenate(
            [stage[pl.ds(b + v, high, stride=group), :] for v in range(2)], axis=0
        ).astype(BF16)
        rhs = jnp.concatenate(
            [onehot_rows(idx_ref[pl.ds(t * group + b + v, 1), :]) for v in range(2)], axis=0
        )
        both = lax.dot_general(lhs, rhs, NT, preferred_element_type=F32)
        for v in range(2):
            res = both[v * high : (v + 1) * high, v * BLK : (v + 1) * BLK]
            start = aligned((t * group + b + v) * keep, 8)
            pblk[pl.ds(start, whole), :] = (
                res[0:whole] + res[whole : 2 * whole] + res[2 * whole : 3 * whole]
            )
            pblk[pl.ds(start + whole, 8), :] = res[3 * whole : 3 * whole + 8]


def pieces_wide(arrays):
    return jnp.concatenate([p for x in arrays for p in split3(x)], axis=1).astype(BF16)


def pieces_sum(res, i):
    res = res[:, 3 * i * BLK : 3 * (i + 1) * BLK]
    return res[:, :BLK] + res[:, BLK : 2 * BLK] + res[:, 2 * BLK :]


def blocks_to_dense(pblk, bt_ref, h, count, outs):
    nblocks = bt_ref.shape[1]
    half = bt_ref.shape[0] // 2
    sub = CHUNK_PEERS
    peers = len(outs) * sub
    quarter = half // peers
    stride = outs[0].shape[0] // sub
    whole = count // 8 * 8
    rest = count - whole
    keep = cam_sum_rows(count)
    for k0 in range(0, count, 2):
        ks = range(k0, min(k0 + 2, count))
        arrays = []
        for k in ks:
            if k < whole:
                arrays.append(pblk[pl.ds(k, nblocks, stride=keep), :])
            else:
                p = [pblk[pl.ds(k + s * rest, nblocks, stride=keep), :] for s in range(3)]
                arrays.append(p[0] + (p[1] + p[2]))
        both = jnp.dot(
            bt_ref[h * half : (h + 1) * half, :], pieces_wide(arrays), preferred_element_type=F32
        )
        for n, k in enumerate(ks):
            res = pieces_sum(both, n)
            for i in range(quarter):
                for s, out in enumerate(outs):
                    first = i * peers + s * sub
                    out[pl.ds(k * quarter + i, sub, stride=stride), :] = res[first : first + sub]


def half_kernel(count, chunks, *refs):
    pblk, bt = refs[:2]
    outs = refs[-chunks:]
    blocks_to_dense(pblk, bt, 0, count, outs)
    if len(refs) > chunks + 2:
        fill_extra(outs, [refs[2][i : i + 1, :] for i in range(EXTRA)])


def half_call(pblk, bt, chunks, count, stride, extra=()):
    return call(
        functools.partial(half_kernel, count, chunks),
        "own_half",
        [shape_of(CHUNK_PEERS * stride, BLK)] * chunks,
        (pblk, bt) + extra,
        cost=pl.CostEstimate(flops=10**9, bytes_accessed=4 * 10**6, transcendentals=0),
    )


def pick_half(b_ref, h, msgs, k0, count):
    sub = CHUNK_PEERS
    half = b_ref.shape[1] // 2
    quarter = half // (sub * len(msgs))
    stride = msgs[0].shape[0] // sub
    arrays = [
        jnp.concatenate(
            [msg[pl.ds(k * quarter + i, sub, stride=stride), :] for i in range(quarter) for msg in msgs],
            axis=0,
        )
        for k in range(k0, k0 + count)
    ]
    both = jnp.dot(
        b_ref[:, h * half : (h + 1) * half], pieces_wide(arrays), preferred_element_type=F32
    )
    return [pieces_sum(both, n) for n in range(count)]


def pick_kernel(b_mat, *refs):
    pick = refs[-1]
    for k0 in range(0, NP, 2):
        count = min(2, NP - k0)
        for n, value in enumerate(pick_half(b_mat, 0, refs[:-1], k0, count)):
            pick[k0 + n] = value


def pick_call(b_mat, mine):
    return call(
        pick_kernel,
        "pick_own_half",
        shape_of(NP, b_mat.shape[0], BLK),
        (b_mat,) + mine,
        cost=pl.CostEstimate(flops=10**9, bytes_accessed=4 * 10**6, transcendentals=0),
    )


def fill_extra(msgs, rows):
    for msg in msgs:
        stride = msg.shape[0] // CHUNK_PEERS
        for i, row in enumerate(rows):
            msg[pl.ds(stride - EXTRA + i, CHUNK_PEERS, stride=stride), :] = jnp.broadcast_to(
                row, (CHUNK_PEERS, BLK)
            )


def extra_sum(msgs, index):
    stride = msgs[0].shape[0] // CHUNK_PEERS
    rows = [msg[pl.ds(stride - EXTRA + index, CHUNK_PEERS, stride=stride), :] for msg in msgs]
    total = jnp.sum(functools.reduce(jnp.add, rows), axis=0, keepdims=True)
    return jnp.sum(total, axis=1, keepdims=True)


def spread_points(ref, t, group, pidx):
    tiles = group // BPT
    out = []
    for j in range(3):
        table = [
            jnp.broadcast_to(ref[j, pl.ds(t * tiles + u, 1), :], (BPT, BLK)) for u in range(tiles)
        ]
        out.append(lane_pick(jnp.concatenate(table, axis=0), pidx))
    return out


def terms_kernel(pos, jp, op, col, stage):
    nblocks = op.shape[0]

    def terms(t, carry):
        rows = pl.ds(pl.multiple_of(t * GROUP, GROUP), GROUP)
        a = [jp[j, rows, :] for j in range(6)]
        vals = [
            a[p] * a[q] + a[3 + p] * a[3 + q]
            for p, q in [(0, 0), (0, 1), (0, 2), (1, 1), (1, 2), (2, 2)]
        ]
        point_scatter(stage, vals, op, t, col)
        return carry

    lax.fori_loop(0, nblocks // GROUP, terms, 0)


def place_rows(pos, entry_ref, cov_ref, table, quarters, side, half):
    owners, per_owner = cov_ref.shape
    peers = quarters * side * side
    quarter = half // peers
    table[...] = jnp.zeros(table.shape, jnp.int32)
    table[:, 0:per_owner] = cov_ref[...]
    entry = entry_ref[...]
    owner = entry // per_owner
    slot = entry % per_owner
    block = jnp.zeros(entry.shape, jnp.int32)
    for o in range(owners):
        row = jnp.broadcast_to(table[o : o + 1, :], entry.shape)
        block = jnp.where(owner == o, lane_pick(row, slot), block)
    core_of = block // (quarters * quarter)
    x_of = block // quarter % quarters
    owner_z, owner_y = owner // side, owner % side
    chunk = jnp.where(core_of == 0, pos[5] - owner_z, pos[6] - owner_y) + side
    last = jnp.where(core_of == 0, owner_y, owner_z)
    return (
        (core_of ^ pos[0]) * half
        + (block % quarter) * peers
        + chunk % side * CHUNK_PEERS
        + x_of * side
        + last
    )


def setup_kernel(
    chunks, quarters, pos, entry, cov, col, jac, jp, oc, op, pt_grad, pt_damp, *refs
):
    others = refs[:chunks]
    pblk, inv_out, pg_out, place, bt, stage2, grad_rows, damp_rows, table = refs[chunks:]
    places = bt.shape[0]
    place[...] = place_rows(pos, entry, cov, table, quarters, chunks, places // 2)
    for r in range(place.shape[0]):
        row = lax.broadcasted_iota(jnp.int32, (places, BLK), 0)
        hit = row == place[r : r + 1, :]
        bt[:, r * BLK : (r + 1) * BLK] = jnp.where(hit, 1.0, 0.0).astype(BF16)
    nblocks = jac.shape[1]
    tiles = nblocks // BPT
    for t in range(tiles):
        lanes = slice(t * BLK, (t + 1) * BLK)
        grad_rows[pl.ds(t, 3, stride=tiles), :] = pt_grad[:, lanes]
        damp_rows[pl.ds(t, 3, stride=tiles), :] = pt_damp[:, lanes]
    grad = [grad_rows[j * tiles : (j + 1) * tiles, :] for j in range(3)]
    damp = [damp_rows[j * tiles : (j + 1) * tiles, :] for j in range(3)]

    entry = point_sums(col, 6, tiles)
    c00 = entry[0] + damp[0]
    c01 = entry[1]
    c02 = entry[2]
    c11 = entry[3] + damp[1]
    c12 = entry[4]
    c22 = entry[5] + damp[2]
    a00 = c11 * c22 - c12 * c12
    a01 = c02 * c12 - c01 * c22
    a02 = c01 * c12 - c02 * c11
    a11 = c00 * c22 - c02 * c02
    a12 = c01 * c02 - c00 * c12
    a22 = c00 * c11 - c01 * c01
    recip = 1.0 / (c00 * a00 + c01 * a01 + c02 * a02)
    inv = [a * recip for a in (a00, a01, a02, a11, a12, a22)]
    for j in range(6):
        inv_out[j] = inv[j]
    pg = apply_three(inv, grad)
    for j in range(3):
        pg_out[j] = pg[j]

    def rhs_terms(t, carry):
        rows = pl.ds(pl.multiple_of(t * GROUP, GROUP), GROUP)
        g = spread_points(pg_out, t, GROUP, op[rows, :])
        c0 = jp[0, rows, :] * g[0] + jp[1, rows, :] * g[1] + jp[2, rows, :] * g[2]
        c1 = jp[3, rows, :] * g[0] + jp[4, rows, :] * g[1] + jp[5, rows, :] * g[2]
        vals = []
        diag = []
        for k in range(NP):
            j0 = jac[k, rows, :]
            j1 = jac[NP + k, rows, :]
            vals.append(j0 * c0 + j1 * c1)
            diag.append(j0 * j0 + j1 * j1)
        cam_scatter(stage2, vals + diag, oc, t, pblk)
        return carry

    lax.fori_loop(0, nblocks // GROUP, rhs_terms, 0)
    blocks_to_dense(pblk, bt, 1, 2 * NP, others)


def call(kernel, name, out_shape, operands, scratch=(), smem=(), cost=None):
    return pl.pallas_call(
        kernel,
        in_specs=[
            pl.BlockSpec(memory_space=pltpu.SMEM if i in smem else pltpu.VMEM)
            for i in range(len(operands))
        ],
        out_shape=out_shape,
        scratch_shapes=scratch,
        compiler_params=pltpu.CompilerParams(vmem_limit_bytes=VMEM_LIMIT),
        cost_estimate=cost,
        name=name,
    )(*operands)


def shape_of(*dims):
    return jax.ShapeDtypeStruct(dims, F32)


def setup_call(pos, entry, cov, jac, jp, oc, op, pt_grad, pt_damp, chunks, quarters, places):
    nblocks = jac.shape[1]
    tiles = nblocks // BPT
    col = call(
        terms_kernel,
        "point_terms",
        shape_of(tiles * point_stage_rows(6), BLK),
        (pos, jp, op),
        [pltpu.VMEM((point_stage_rows(6) * GROUP, BLK), F32)],
        smem=(0,),
        cost=pl.CostEstimate(flops=4 * 10**9, bytes_accessed=10**7, transcendentals=0),
    )
    return call(
        functools.partial(setup_kernel, chunks, quarters),
        "setup_pass",
        [
            *[shape_of(NP * places // chunks, BLK)] * chunks,
            shape_of(nblocks * cam_sum_rows(2 * NP), BLK),
            shape_of(6, tiles, BLK),
            shape_of(3, tiles, BLK),
            jax.ShapeDtypeStruct((nblocks // BLK, BLK), jnp.int32),
            jax.ShapeDtypeStruct((places, nblocks), BF16),
        ],
        (pos, entry.reshape(nblocks // BLK, BLK), cov, col, jac, jp, oc, op, pt_grad, pt_damp),
        [
            pltpu.VMEM((cam_stage_rows(2 * NP) * GROUP, BLK), F32),
            pltpu.VMEM((3 * tiles, BLK), F32),
            pltpu.VMEM((3 * tiles, BLK), F32),
            pltpu.VMEM((cov.shape[0], BLK), jnp.int32),
        ],
        smem=(0,),
    )


def operator_kernel(second, chunks, *refs):
    pos, jac, jp, oc, op, b_mat, bt, inv, pick_in = refs[:9]
    mine_in, other_in = refs[9 : 9 + chunks], refs[9 + chunks : 9 + 2 * chunks]
    refs = refs[9 + 2 * chunks :]
    if second:
        proj_in, state, image, norm_in = refs[:4]
        refs = refs[4:]
    others = refs[:chunks]
    pblk, sol_out, held_out, scal_out, extra = refs[chunks : chunks + 5]
    refs = refs[chunks + 5 :]
    if second:
        stage, stage2, pick, col, proj = refs
    else:
        proj, stage, stage2, pick, col = refs
    nblocks = jac.shape[1]
    tiles = nblocks // BPT
    stride = mine_in[0].shape[0] // CHUNK_PEERS
    for k0 in range(0, NP, 2):
        count = min(2, NP - k0)
        for n, value in enumerate(pick_half(b_mat, 1, other_in, k0, count)):
            pick[k0 + n] = pick_in[k0 + n] + value
    for h, msgs in enumerate((mine_in, other_in)):
        for x in range(CHUNK_PEERS // chunks):
            start = pl.multiple_of((x * chunks + pos[2 + h]) * stride, 8)
            held_out[h, x] = msgs[0][pl.ds(start, stride), :]
    total = extra_sum(mine_in + other_in, 0)
    if second:
        norm = norm_in[0:1, 0:1]
        step_len = norm / total
        scal_out[...] = jnp.broadcast_to(total, (8, BLK))
        rhs, precond, damp, direction = (state[i] for i in range(4))
        resid = rhs - step_len * image[...]
        z = resid / precond
        keep = lax.broadcasted_iota(jnp.int32, (stride, BLK), 0) < stride - EXTRA

        def lanes(v):
            return jnp.sum(jnp.where(keep, v, 0.0), axis=0, keepdims=True)

        owner_sums = [lanes(damp * z * z), lanes(damp * z * direction), lanes(resid * z)]
    else:
        scal_out[...] = jnp.broadcast_to(total, (8, BLK))

    def project(t, carry):
        rows = pl.ds(t * GROUP, GROUP)
        cidx = oc[rows, :]
        p0 = jnp.zeros((GROUP, BLK), F32)
        p1 = jnp.zeros((GROUP, BLK), F32)
        for k in range(NP):
            v = lane_pick(pick[k, rows, :], cidx)
            p0 += jac[k, rows, :] * v
            p1 += jac[NP + k, rows, :] * v
        if second:
            p0 = proj_in[0, rows, :] - step_len * p0
            p1 = proj_in[1, rows, :] - step_len * p1
        proj[0, rows, :] = p0
        proj[1, rows, :] = p1
        vals = [jp[j, rows, :] * p0 + jp[3 + j, rows, :] * p1 for j in range(3)]
        point_scatter(stage.at[t], vals, op, t, col)
        return carry

    steps(nblocks // GROUP, project, 0)
    sol = apply_three([inv[j] for j in range(6)], point_sums(col, 3, tiles))
    for j in range(3):
        sol_out[j] = sol[j]

    def correct(t, carry):
        rows = pl.ds(t * GROUP, GROUP)
        g = spread_points(sol_out, t, GROUP, op[rows, :])
        p0 = proj[0, rows, :]
        p1 = proj[1, rows, :]
        c0 = p0 - (jp[0, rows, :] * g[0] + jp[1, rows, :] * g[1] + jp[2, rows, :] * g[2])
        c1 = p1 - (jp[3, rows, :] * g[0] + jp[4, rows, :] * g[1] + jp[5, rows, :] * g[2])
        if second:
            zz, zd = carry
            zz = zz + (p0 * c0 + p1 * c1)
            zd = zd + (proj_in[0, rows, :] * c0 + proj_in[1, rows, :] * c1)
            carry = (zz, zd)
        vals = [jac[k, rows, :] * c0 + jac[NP + k, rows, :] * c1 for k in range(NP)]
        cam_scatter(stage2.at[t], vals, oc, t, pblk)
        return carry

    zero = jnp.zeros((GROUP, BLK), F32)
    sums = steps(nblocks // GROUP, correct, (zero, zero) if second else 0)
    blocks_to_dense(pblk, bt, 1, NP, others)
    rows = []
    if second:
        rows = [
            jnp.sum(sums[0], axis=0, keepdims=True) + owner_sums[0],
            jnp.sum(sums[1], axis=0, keepdims=True) + owner_sums[1],
            owner_sums[2],
        ]
    rows += [jnp.zeros((1, BLK), F32)] * (EXTRA - len(rows))
    fill_extra(others, rows)
    extra[...] = jnp.concatenate(rows, axis=0)


def operator_call(pos, jac, jp, oc, op, b_mat, bt, inv, pick, mine, other, later=()):
    nblocks = jac.shape[1]
    tiles = nblocks // BPT
    chunks = len(mine)
    stride = mine[0].shape[0] // CHUNK_PEERS
    proj = [] if later else [shape_of(2, nblocks, BLK)]
    proj_scratch = [pltpu.VMEM((2, nblocks, BLK), F32)] if later else []
    return call(
        functools.partial(operator_kernel, bool(later), chunks),
        "second_pass" if later else "first_pass",
        [
            *[shape_of(*mine[0].shape)] * chunks,
            shape_of(nblocks * cam_sum_rows(NP), BLK),
            shape_of(3, tiles, BLK),
            shape_of(2, CHUNK_PEERS // chunks, stride, BLK),
            shape_of(8, BLK),
            shape_of(EXTRA, BLK),
        ]
        + proj,
        (pos, jac, jp, oc, op, b_mat, bt, inv, pick) + mine + other + later,
        [
            pltpu.VMEM((nblocks // GROUP, point_stage_rows(3) * GROUP, BLK), F32),
            pltpu.VMEM((nblocks // GROUP, cam_stage_rows(NP) * GROUP, BLK), F32),
            pltpu.VMEM((NP, nblocks, BLK), F32),
            pltpu.VMEM((tiles * point_stage_rows(3), BLK), F32),
        ]
        + proj_scratch,
        smem=(0,),
    )


def message_sum(got):
    rows = got.shape[0] // CHUNK_PEERS
    total = got[0:rows, :]
    for d in range(1, CHUNK_PEERS):
        total = total + got[d * rows : (d + 1) * rows, :]
    return total


def send_all(msg, values, scalar):
    stride = values.shape[0]
    data = stride - EXTRA
    row = lax.broadcasted_iota(jnp.int32, values.shape, 0)
    lanes = jnp.sum(jnp.where(row < data, scalar, 0.0), axis=0, keepdims=True)
    out = jnp.where(row < data, values, jnp.where(row == data, lanes, 0.0))
    for d in range(CHUNK_PEERS):
        msg[d * stride : (d + 1) * stride, :] = out


def start_kernel(quarter, pos, got, grad, damp, msg, state, rows):
    data = NP * quarter
    rows[...] = jnp.ones(rows.shape, F32)
    for i in range(quarter):
        lanes = pl.ds(pl.multiple_of((pos[1] * quarter + i) * BLK, BLK), BLK)
        rows[0, pl.ds(i, NP, stride=quarter), :] = grad[:, lanes]
        rows[1, pl.ds(i, NP, stride=quarter), :] = damp[:, lanes]
    total = message_sum(got)
    ones = jnp.ones((EXTRA, BLK), F32)
    rhs = rows[0] - jnp.concatenate([total[:data], ones], axis=0)
    precond = rows[1] + jnp.concatenate([total[data:], ones], axis=0)
    direction = rhs / precond
    state[0] = rhs
    state[1] = precond
    state[2] = rows[1]
    state[3] = direction
    send_all(msg, direction, rhs * direction)


def image_kernel(got, state, msg, image):
    direction = state[3]
    value = state[2] * direction + message_sum(got)
    image[...] = value
    send_all(msg, value / state[1], direction * value)


def last_kernel(got, state, image, norm_in, curv_in, resid_out, scal_out):
    norm = norm_in[0:1, 0:1]
    curv = curv_in[0:1, 0:1]
    step0 = norm / curv
    total = message_sum(got)
    stride = total.shape[0]
    sums = jnp.sum(total[stride - EXTRA :], axis=1, keepdims=True)
    zz, zd, norm1 = (sums[i : i + 1] for i in range(3))
    beta = norm1 / norm
    curv1 = zz + 2.0 * beta * zd + beta * beta * curv
    step1 = norm1 / curv1
    resid = state[0] - step0 * image[...]
    z = resid / state[1]
    image1 = (state[2] * z + total) + beta * image[...]
    resid_out[...] = resid - step1 * image1
    for i, s in enumerate((step0, step1, beta)):
        scal_out[i * 8 : (i + 1) * 8, :] = jnp.broadcast_to(s, (8, BLK))


def step_kernel(pos, scal, held0, held1, pg, sol0, sol1, cam_out, pt_out, pts_rows, cams_rows):
    step0, step1, beta = (scal[i * 8 : i * 8 + 1, 0:1] for i in range(3))
    tiles = pg.shape[1]
    for j in range(3):
        first = sol0[j]
        pts_rows[j * tiles : (j + 1) * tiles, :] = (
            pg[j] - step0 * first - step1 * (sol1[j] + beta * first)
        )
    for t in range(tiles):
        pt_out[:, t * BLK : (t + 1) * BLK] = pts_rows[pl.ds(t, 3, stride=tiles), :]
    quarters, stride = held0.shape[1], held0.shape[2]
    quarter = (stride - EXTRA) // NP
    for h in range(2):
        for x in range(quarters):
            d0 = held0[h, x]
            z = d0 - step0 * held1[h, x]
            cams_rows[...] = step0 * d0 + step1 * (z + beta * d0)
            put_cams(cam_out, cams_rows, pos[0] ^ h, x, quarters, quarter)


def put_cams(out, rows, core, x, quarters, quarter):
    for i in range(quarter):
        block = (core * quarters + x) * quarter + i
        lanes = pl.ds(pl.multiple_of(block * BLK, BLK), BLK)
        out[:, lanes] = rows[pl.ds(i, NP, stride=quarter), :]


def resid_kernel(pos, pieces, out, rows):
    quarters, stride = pieces.shape[1], pieces.shape[2]
    quarter = (stride - EXTRA) // NP
    for h in range(2):
        for s in range(quarters):
            x = (pos[4] + quarters - s) % quarters
            rows[...] = pieces[h, s]
            put_cams(out, rows, pos[0] ^ h, x, quarters, quarter)


def local(jac, jp, oc, op, entry, cov, cam_grad, cam_damp, pt_grad, pt_damp):
    quarters = lax.axis_size("x")
    owners = lax.axis_size("z") * lax.axis_size("y")
    peers = quarters * owners
    core = lax.axis_index("core")
    x = lax.axis_index("x")
    side = lax.axis_size("z")
    z, y = lax.axis_index("z"), lax.axis_index("y")

    pos = jnp.stack(
        [
            core,
            core * quarters + x,
            jnp.where(core == 0, y, z),
            jnp.where(core == 0, z, y),
            x,
            z,
            y,
        ]
    ).astype(jnp.int32)
    shard = cam_grad.shape[1]
    quarter = shard // BLK // 2 // quarters
    half = peers * quarter

    def exchange(v):
        return lax.ppermute(v, "core", [(0, 1), (1, 0)])

    def rank(x, c, z, y):
        return ((x * 2 + c) * side + z) * side + y

    xs, ss = range(quarters), range(side)
    every = ("x", "core", "z", "y")
    last_axes = [[rank(x, 0, z, y) for x in xs for y in ss] for z in ss]
    last_axes += [[rank(x, 1, z, y) for x in xs for z in ss] for y in ss]

    def shift(v, s):
        pairs = []
        for x in xs:
            for z in ss:
                for y in ss:
                    pairs.append((rank(x, 0, z, y), rank(x, 0, (z + s) % side, y)))
                    pairs.append((rank(x, 1, z, y), rank(x, 1, z, (y + s) % side)))
        return lax.ppermute(v, every, pairs)

    def over_last(v):
        shaped = v.reshape(CHUNK_PEERS, -1, BLK)
        got = lax.all_to_all(shaped, every, 0, 0, axis_index_groups=last_axes, tiled=False)
        return got.reshape(-1, BLK)

    stride = NP * quarter + EXTRA
    msg = shape_of(CHUNK_PEERS * stride, BLK)
    chunk_order = [*range(1, side), 0]

    def reduce_parts(others, pblk, bt, count, rows, *extra):
        theirs = {s: exchange(others[s]) for s in chunk_order}
        own = half_call(pblk, bt, side, count, rows, extra)
        moved = [shift(own[s] + theirs[s], -s) for s in chunk_order[:-1]]
        total = own[0] + theirs[0]
        for part in moved:
            total = total + part
        return over_last(total)

    def fetch(msg_out, b_mat):
        first = over_last(msg_out)
        mine = (first,) + tuple(shift(first, s) for s in range(1, side))
        other = tuple(exchange(part) for part in mine)
        return pick_call(b_mat, mine), mine, other

    *others, pblk, inv, pg, place, bt = setup_call(
        pos, entry, cov, jac, jp, oc, op, pt_grad, pt_damp, side, quarters, 2 * half
    )
    places = jnp.arange(2 * half, dtype=jnp.int32)
    b_mat = (place.reshape(-1, 1) == places[None, :]).astype(BF16)
    got = reduce_parts(others, pblk, bt, 2 * NP, 2 * NP * quarter)
    msg_out, state = call(
        functools.partial(start_kernel, quarter),
        "start_step",
        [msg, shape_of(4, stride, BLK)],
        (pos, got, cam_grad, cam_damp),
        [pltpu.VMEM((2, stride, BLK), F32)],
        smem=(0,),
    )
    pick, mine, other = fetch(msg_out, b_mat)
    *others, pblk, sol0, held0, norm, extra, proj0 = operator_call(
        pos, jac, jp, oc, op, b_mat, bt, inv, pick, mine, other
    )
    got = reduce_parts(others, pblk, bt, NP, stride, extra)
    msg_out, image = call(
        image_kernel, "image_step", [msg, shape_of(stride, BLK)], (got, state)
    )
    pick, mine, other = fetch(msg_out, b_mat)
    *others, pblk, sol1, held1, curv, extra = operator_call(
        pos, jac, jp, oc, op, b_mat, bt, inv, pick, mine, other, (proj0, state, image, norm)
    )
    got = reduce_parts(others, pblk, bt, NP, stride, extra)
    resid, scal = call(
        last_kernel,
        "last_step",
        [shape_of(stride, BLK), shape_of(24, BLK)],
        (got, state, image, norm, curv),
    )
    pieces = [resid] + [
        lax.ppermute(resid, "x", [(i, (i + s) % quarters) for i in range(quarters)])
        for s in range(1, quarters)
    ]
    cam_step, pt_step = call(
        step_kernel,
        "result_step",
        [shape_of(NP, shard), shape_of(3, pt_grad.shape[1])],
        (pos, scal, held0, held1, pg, sol0, sol1),
        [pltpu.VMEM((3 * pg.shape[1], BLK), F32), pltpu.VMEM((stride, BLK), F32)],
        smem=(0,),
        cost=pl.CostEstimate(flops=10**9, bytes_accessed=4 * 10**6, transcendentals=0),
    )
    row = jnp.stack(pieces)
    cam_resid = call(
        resid_kernel,
        "result_resid",
        shape_of(NP, shard),
        (pos, jnp.stack([row, exchange(row)])),
        [pltpu.VMEM((stride, BLK), F32)],
        smem=(0,),
    )
    return cam_step, cam_resid, pt_step


def solution(mesh):
    fine = Mesh(mesh.devices.reshape(4, 2, 4, 4), ("x", "core", "z", "y"))
    pts, cam = ("x", "core"), ("z", "y")
    every = pts + cam
    in_specs = (
        P(None, every, None),
        P(None, every, None),
        P(every, None),
        P(every, None),
        P(every),
        P(every, None),
        P(None, cam),
        P(None, cam),
        P(None, every),
        P(None, every),
    )
    out_specs = (P(None, cam), P(None, cam), P(None, every))
    return jax.shard_map(local, mesh=fine, in_specs=in_specs, out_specs=out_specs, check_vma=False)
```

```python
import functools

import jax
import jax.numpy as jnp
from jax import lax
from jax.experimental import pallas as pl
from jax.experimental.pallas import tpu as pltpu
from jax.sharding import Mesh, PartitionSpec as P

BLK = 128
BPT = 8
NP = 9
CHUNK_PEERS = 16
EXTRA = 4
F32 = jnp.float32
BF16 = jnp.bfloat16
GROUP = 128
VMEM_LIMIT = 24 * 1024 * 1024


def split3(x):
    hi = x.astype(BF16).astype(F32)
    rest = x - hi
    mid = rest.astype(BF16).astype(F32)
    return hi, mid, rest - mid


def apply_three(inverse, values):
    first = inverse[0] * values[0] + inverse[1] * values[1] + inverse[2] * values[2]
    second = inverse[1] * values[0] + inverse[3] * values[1] + inverse[4] * values[2]
    third = inverse[2] * values[0] + inverse[4] * values[1] + inverse[5] * values[2]
    return [first, second, third]


def lane_pick(table, idx):
    return jnp.take_along_axis(table, idx, axis=1, mode="promise_in_bounds")


def onehot_rows(idx_row):
    rows = lax.broadcasted_iota(jnp.int32, (BLK, BLK), 0)
    return jnp.where(rows == idx_row, 1.0, 0.0).astype(BF16)


NT = (((1,), (1,)), ((), ()))


def point_stage_rows(count):
    return -(-3 * count // 16) * 16


def cam_stage_rows(count):
    whole = count // 8 * 8
    return -(-(3 * whole + 8) // 16) * 16


def cam_sum_rows(count):
    return count // 8 * 8 + 8


def point_scatter(stage, vals, idx_ref, t, col):
    count = len(vals)
    group = vals[0].shape[0]
    high = point_stage_rows(count)
    for j, val in enumerate(vals):
        for s, piece in enumerate(split3(val)):
            row = s * count + j
            stage[row * group : (row + 1) * group, :] = piece
    tiles = group // BPT
    for u in range(0, tiles, 2):
        lhs, rhs = [], []
        for b in range(BPT):
            pair = [(u + v) * BPT + b for v in range(2)]
            lhs.append(
                jnp.concatenate([stage[pl.ds(c, high, stride=group), :] for c in pair], axis=0).astype(BF16)
            )
            rhs.append(
                jnp.concatenate([onehot_rows(idx_ref[pl.ds(t * group + c, 1), :]) for c in pair], axis=0)
            )
        res = lax.dot_general(
            jnp.concatenate(lhs, axis=1), jnp.concatenate(rhs, axis=1), NT, preferred_element_type=F32
        )
        for v in range(2):
            start = pl.multiple_of((t * tiles + u + v) * high, 16)
            col[pl.ds(start, high), :] = res[v * high : (v + 1) * high, v * BLK : (v + 1) * BLK]


def point_sums(col, count, tiles):
    high = point_stage_rows(count)
    out = []
    for j in range(count):
        pieces = [col[pl.ds(s * count + j, tiles, stride=high), :] for s in range(3)]
        out.append(pieces[0] + (pieces[1] + pieces[2]))
    return out


def cam_scatter(stage, vals, idx_ref, t, pblk):
    count = len(vals)
    whole = count // 8 * 8
    rest = count - whole
    group = vals[0].shape[0]
    high = cam_stage_rows(count)
    keep = cam_sum_rows(count)
    for k, val in enumerate(vals):
        for s, piece in enumerate(split3(val)):
            row = s * whole + k if k < whole else 3 * whole + s * rest + k - whole
            stage[row * group : (row + 1) * group, :] = piece
    for b in range(0, group, 2):
        lhs = jnp.concatenate(
            [stage[pl.ds(b + v, high, stride=group), :] for v in range(2)], axis=0
        ).astype(BF16)
        rhs = jnp.concatenate(
            [onehot_rows(idx_ref[pl.ds(t * group + b + v, 1), :]) for v in range(2)], axis=0
        )
        both = lax.dot_general(lhs, rhs, NT, preferred_element_type=F32)
        for v in range(2):
            res = both[v * high : (v + 1) * high, v * BLK : (v + 1) * BLK]
            start = pl.multiple_of((t * group + b + v) * keep, 8)
            pblk[pl.ds(start, whole), :] = (
                res[0:whole] + res[whole : 2 * whole] + res[2 * whole : 3 * whole]
            )
            pblk[pl.ds(start + whole, 8), :] = res[3 * whole : 3 * whole + 8]


def pieces_wide(arrays):
    return jnp.concatenate([p for x in arrays for p in split3(x)], axis=1).astype(BF16)


def pieces_sum(res, i):
    res = res[:, 3 * i * BLK : 3 * (i + 1) * BLK]
    return res[:, :BLK] + res[:, BLK : 2 * BLK] + res[:, 2 * BLK :]


def blocks_to_dense(pblk, bt_ref, h, count, outs):
    nblocks = bt_ref.shape[1]
    half = bt_ref.shape[0] // 2
    sub = CHUNK_PEERS
    peers = len(outs) * sub
    quarter = half // peers
    stride = outs[0].shape[0] // sub
    whole = count // 8 * 8
    rest = count - whole
    keep = cam_sum_rows(count)
    for k0 in range(0, count, 2):
        ks = range(k0, min(k0 + 2, count))
        arrays = []
        for k in ks:
            if k < whole:
                arrays.append(pblk[pl.ds(k, nblocks, stride=keep), :])
            else:
                p = [pblk[pl.ds(k + s * rest, nblocks, stride=keep), :] for s in range(3)]
                arrays.append(p[0] + (p[1] + p[2]))
        both = jnp.dot(
            bt_ref[h * half : (h + 1) * half, :], pieces_wide(arrays), preferred_element_type=F32
        )
        for n, k in enumerate(ks):
            res = pieces_sum(both, n)
            for i in range(quarter):
                for s, out in enumerate(outs):
                    first = i * peers + s * sub
                    out[pl.ds(k * quarter + i, sub, stride=stride), :] = res[first : first + sub]


def half_kernel(count, chunks, *refs):
    pblk, bt = refs[:2]
    outs = refs[-chunks:]
    blocks_to_dense(pblk, bt, 0, count, outs)
    if len(refs) > chunks + 2:
        fill_extra(outs, [refs[2][i : i + 1, :] for i in range(EXTRA)])


def half_call(pblk, bt, chunks, count, stride, extra=()):
    return call(
        functools.partial(half_kernel, count, chunks),
        "own_half",
        [shape_of(CHUNK_PEERS * stride, BLK)] * chunks,
        (pblk, bt) + extra,
        cost=pl.CostEstimate(flops=10**9, bytes_accessed=4 * 10**6, transcendentals=0),
    )


def pick_half(b_ref, h, msgs, k0, count):
    sub = CHUNK_PEERS
    half = b_ref.shape[1] // 2
    quarter = half // (sub * len(msgs))
    stride = msgs[0].shape[0] // sub
    arrays = [
        jnp.concatenate(
            [msg[pl.ds(k * quarter + i, sub, stride=stride), :] for i in range(quarter) for msg in msgs],
            axis=0,
        )
        for k in range(k0, k0 + count)
    ]
    both = jnp.dot(
        b_ref[:, h * half : (h + 1) * half], pieces_wide(arrays), preferred_element_type=F32
    )
    return [pieces_sum(both, n) for n in range(count)]


def pick_kernel(b_mat, *refs):
    pick = refs[-1]
    for k0 in range(0, NP, 2):
        count = min(2, NP - k0)
        for n, value in enumerate(pick_half(b_mat, 0, refs[:-1], k0, count)):
            pick[k0 + n] = value


def pick_call(b_mat, mine):
    return call(
        pick_kernel,
        "pick_own_half",
        shape_of(NP, b_mat.shape[0], BLK),
        (b_mat,) + mine,
        cost=pl.CostEstimate(flops=10**9, bytes_accessed=4 * 10**6, transcendentals=0),
    )


def fill_extra(msgs, rows):
    for msg in msgs:
        stride = msg.shape[0] // CHUNK_PEERS
        for i, row in enumerate(rows):
            msg[pl.ds(stride - EXTRA + i, CHUNK_PEERS, stride=stride), :] = jnp.broadcast_to(
                row, (CHUNK_PEERS, BLK)
            )


def extra_sum(msgs, index):
    stride = msgs[0].shape[0] // CHUNK_PEERS
    rows = [msg[pl.ds(stride - EXTRA + index, CHUNK_PEERS, stride=stride), :] for msg in msgs]
    total = jnp.sum(functools.reduce(jnp.add, rows), axis=0, keepdims=True)
    return jnp.sum(total, axis=1, keepdims=True)


def spread_points(ref, t, group, pidx):
    tiles = group // BPT
    out = []
    for j in range(3):
        table = [
            jnp.broadcast_to(ref[j, pl.ds(t * tiles + u, 1), :], (BPT, BLK)) for u in range(tiles)
        ]
        out.append(lane_pick(jnp.concatenate(table, axis=0), pidx))
    return out


def terms_kernel(pos, jp, op, col, stage):
    nblocks = op.shape[0]

    def terms(t, carry):
        rows = pl.ds(pl.multiple_of(t * GROUP, GROUP), GROUP)
        a = [jp[j, rows, :] for j in range(6)]
        vals = [
            a[p] * a[q] + a[3 + p] * a[3 + q]
            for p, q in [(0, 0), (0, 1), (0, 2), (1, 1), (1, 2), (2, 2)]
        ]
        point_scatter(stage, vals, op, t, col)
        return carry

    lax.fori_loop(0, nblocks // GROUP, terms, 0)


def place_rows(pos, entry_ref, cov_ref, table, quarters, side, half):
    owners, per_owner = cov_ref.shape
    peers = quarters * side * side
    quarter = half // peers
    table[...] = jnp.zeros(table.shape, jnp.int32)
    table[:, 0:per_owner] = cov_ref[...]
    entry = entry_ref[...]
    owner = entry // per_owner
    slot = entry % per_owner
    block = jnp.zeros(entry.shape, jnp.int32)
    for o in range(owners):
        row = jnp.broadcast_to(table[o : o + 1, :], entry.shape)
        block = jnp.where(owner == o, lane_pick(row, slot), block)
    core_of = block // (quarters * quarter)
    x_of = block // quarter % quarters
    owner_z, owner_y = owner // side, owner % side
    chunk = (jnp.where(core_of == 0, pos[5] - owner_z, pos[6] - owner_y) + side) % side
    chunk = chunk ^ (chunk >> 1)
    last = jnp.where(core_of == 0, owner_y, owner_z)
    return (
        (core_of ^ pos[0]) * half
        + (block % quarter) * peers
        + chunk * CHUNK_PEERS
        + x_of * side
        + last
    )


def setup_kernel(
    chunks, quarters, pos, entry, cov, col, jac, jp, oc, op, pt_grad, pt_damp, *refs
):
    others = refs[:chunks]
    pblk, inv_out, pg_out, place, bt, stage2, grad_rows, damp_rows, table = refs[chunks:]
    places = bt.shape[0]
    place[...] = place_rows(pos, entry, cov, table, quarters, chunks, places // 2)
    for r in range(place.shape[0]):
        row = lax.broadcasted_iota(jnp.int32, (places, BLK), 0)
        hit = row == place[r : r + 1, :]
        bt[:, r * BLK : (r + 1) * BLK] = jnp.where(hit, 1.0, 0.0).astype(BF16)
    nblocks = jac.shape[1]
    tiles = nblocks // BPT
    for t in range(tiles):
        lanes = slice(t * BLK, (t + 1) * BLK)
        grad_rows[pl.ds(t, 3, stride=tiles), :] = pt_grad[:, lanes]
        damp_rows[pl.ds(t, 3, stride=tiles), :] = pt_damp[:, lanes]
    grad = [grad_rows[j * tiles : (j + 1) * tiles, :] for j in range(3)]
    damp = [damp_rows[j * tiles : (j + 1) * tiles, :] for j in range(3)]

    entry = point_sums(col, 6, tiles)
    c00 = entry[0] + damp[0]
    c01 = entry[1]
    c02 = entry[2]
    c11 = entry[3] + damp[1]
    c12 = entry[4]
    c22 = entry[5] + damp[2]
    a00 = c11 * c22 - c12 * c12
    a01 = c02 * c12 - c01 * c22
    a02 = c01 * c12 - c02 * c11
    a11 = c00 * c22 - c02 * c02
    a12 = c01 * c02 - c00 * c12
    a22 = c00 * c11 - c01 * c01
    recip = 1.0 / (c00 * a00 + c01 * a01 + c02 * a02)
    inv = [a * recip for a in (a00, a01, a02, a11, a12, a22)]
    for j in range(6):
        inv_out[j] = inv[j]
    pg = apply_three(inv, grad)
    for j in range(3):
        pg_out[j] = pg[j]

    def rhs_terms(t, carry):
        rows = pl.ds(pl.multiple_of(t * GROUP, GROUP), GROUP)
        g = spread_points(pg_out, t, GROUP, op[rows, :])
        c0 = jp[0, rows, :] * g[0] + jp[1, rows, :] * g[1] + jp[2, rows, :] * g[2]
        c1 = jp[3, rows, :] * g[0] + jp[4, rows, :] * g[1] + jp[5, rows, :] * g[2]
        vals = []
        diag = []
        for k in range(NP):
            j0 = jac[k, rows, :]
            j1 = jac[NP + k, rows, :]
            vals.append(j0 * c0 + j1 * c1)
            diag.append(j0 * j0 + j1 * j1)
        cam_scatter(stage2, vals + diag, oc, t, pblk)
        return carry

    lax.fori_loop(0, nblocks // GROUP, rhs_terms, 0)
    blocks_to_dense(pblk, bt, 1, 2 * NP, others)


def call(kernel, name, out_shape, operands, scratch=(), smem=(), cost=None):
    return pl.pallas_call(
        kernel,
        in_specs=[
            pl.BlockSpec(memory_space=pltpu.SMEM if i in smem else pltpu.VMEM)
            for i in range(len(operands))
        ],
        out_shape=out_shape,
        scratch_shapes=scratch,
        compiler_params=pltpu.CompilerParams(vmem_limit_bytes=VMEM_LIMIT),
        cost_estimate=cost,
        name=name,
    )(*operands)


def shape_of(*dims):
    return jax.ShapeDtypeStruct(dims, F32)


def setup_call(pos, entry, cov, jac, jp, oc, op, pt_grad, pt_damp, chunks, quarters, places):
    nblocks = jac.shape[1]
    tiles = nblocks // BPT
    col = call(
        terms_kernel,
        "point_terms",
        shape_of(tiles * point_stage_rows(6), BLK),
        (pos, jp, op),
        [pltpu.VMEM((point_stage_rows(6) * GROUP, BLK), F32)],
        smem=(0,),
        cost=pl.CostEstimate(flops=4 * 10**9, bytes_accessed=10**7, transcendentals=0),
    )
    return call(
        functools.partial(setup_kernel, chunks, quarters),
        "setup_pass",
        [
            *[shape_of(NP * places // chunks, BLK)] * chunks,
            shape_of(nblocks * cam_sum_rows(2 * NP), BLK),
            shape_of(6, tiles, BLK),
            shape_of(3, tiles, BLK),
            jax.ShapeDtypeStruct((nblocks // BLK, BLK), jnp.int32),
            jax.ShapeDtypeStruct((places, nblocks), BF16),
        ],
        (pos, entry.reshape(nblocks // BLK, BLK), cov, col, jac, jp, oc, op, pt_grad, pt_damp),
        [
            pltpu.VMEM((cam_stage_rows(2 * NP) * GROUP, BLK), F32),
            pltpu.VMEM((3 * tiles, BLK), F32),
            pltpu.VMEM((3 * tiles, BLK), F32),
            pltpu.VMEM((cov.shape[0], BLK), jnp.int32),
        ],
        smem=(0,),
    )


def operator_kernel(second, chunks, *refs):
    pos, jac, jp, oc, op, b_mat, bt, inv, pick_in = refs[:9]
    mine_in, other_in = refs[9 : 9 + chunks], refs[9 + chunks : 9 + 2 * chunks]
    refs = refs[9 + 2 * chunks :]
    if second:
        proj_in, state, image, norm_in = refs[:4]
        refs = refs[4:]
    others = refs[:chunks]
    pblk, sol_out, held_out, scal_out, extra = refs[chunks : chunks + 5]
    refs = refs[chunks + 5 :]
    if second:
        stage, stage2, pick, col, proj = refs
    else:
        proj, stage, stage2, pick, col = refs
    nblocks = jac.shape[1]
    tiles = nblocks // BPT
    stride = mine_in[0].shape[0] // CHUNK_PEERS
    for k0 in range(0, NP, 2):
        count = min(2, NP - k0)
        for n, value in enumerate(pick_half(b_mat, 1, other_in, k0, count)):
            pick[k0 + n] = pick_in[k0 + n] + value
    for h, msgs in enumerate((mine_in, other_in)):
        for x in range(CHUNK_PEERS // chunks):
            start = pl.multiple_of((x * chunks + pos[2 + h]) * stride, 8)
            held_out[h, x] = msgs[0][pl.ds(start, stride), :]
    total = extra_sum(mine_in + other_in, 0)
    if second:
        norm = norm_in[0:1, 0:1]
        step_len = norm / total
        scal_out[...] = jnp.broadcast_to(total, (8, BLK))
        rhs, precond, damp, direction = (state[i] for i in range(4))
        resid = rhs - step_len * image[...]
        z = resid / precond
        keep = lax.broadcasted_iota(jnp.int32, (stride, BLK), 0) < stride - EXTRA

        def lanes(v):
            return jnp.sum(jnp.where(keep, v, 0.0), axis=0, keepdims=True)

        owner_sums = [lanes(damp * z * z), lanes(damp * z * direction), lanes(resid * z)]
    else:
        scal_out[...] = jnp.broadcast_to(total, (8, BLK))

    def project(t, carry):
        rows = pl.ds(pl.multiple_of(t * GROUP, GROUP), GROUP)
        cidx = oc[rows, :]
        p0 = jnp.zeros((GROUP, BLK), F32)
        p1 = jnp.zeros((GROUP, BLK), F32)
        for k in range(NP):
            v = lane_pick(pick[k, rows, :], cidx)
            p0 += jac[k, rows, :] * v
            p1 += jac[NP + k, rows, :] * v
        if second:
            p0 = proj_in[0, rows, :] - step_len * p0
            p1 = proj_in[1, rows, :] - step_len * p1
        proj[0, rows, :] = p0
        proj[1, rows, :] = p1
        vals = [jp[j, rows, :] * p0 + jp[3 + j, rows, :] * p1 for j in range(3)]
        point_scatter(stage, vals, op, t, col)
        return carry

    lax.fori_loop(0, nblocks // GROUP, project, 0)
    sol = apply_three([inv[j] for j in range(6)], point_sums(col, 3, tiles))
    for j in range(3):
        sol_out[j] = sol[j]

    def correct(t, carry):
        rows = pl.ds(pl.multiple_of(t * GROUP, GROUP), GROUP)
        g = spread_points(sol_out, t, GROUP, op[rows, :])
        p0 = proj[0, rows, :]
        p1 = proj[1, rows, :]
        c0 = p0 - (jp[0, rows, :] * g[0] + jp[1, rows, :] * g[1] + jp[2, rows, :] * g[2])
        c1 = p1 - (jp[3, rows, :] * g[0] + jp[4, rows, :] * g[1] + jp[5, rows, :] * g[2])
        if second:
            zz, zd = carry
            zz = zz + (p0 * c0 + p1 * c1)
            zd = zd + (proj_in[0, rows, :] * c0 + proj_in[1, rows, :] * c1)
            carry = (zz, zd)
        vals = [jac[k, rows, :] * c0 + jac[NP + k, rows, :] * c1 for k in range(NP)]
        cam_scatter(stage2, vals, oc, t, pblk)
        return carry

    zero = jnp.zeros((GROUP, BLK), F32)
    sums = lax.fori_loop(0, nblocks // GROUP, correct, (zero, zero) if second else 0)
    blocks_to_dense(pblk, bt, 1, NP, others)
    rows = []
    if second:
        rows = [
            jnp.sum(sums[0], axis=0, keepdims=True) + owner_sums[0],
            jnp.sum(sums[1], axis=0, keepdims=True) + owner_sums[1],
            owner_sums[2],
        ]
    rows += [jnp.zeros((1, BLK), F32)] * (EXTRA - len(rows))
    fill_extra(others, rows)
    extra[...] = jnp.concatenate(rows, axis=0)


def operator_call(pos, jac, jp, oc, op, b_mat, bt, inv, pick, mine, other, later=()):
    nblocks = jac.shape[1]
    tiles = nblocks // BPT
    chunks = len(mine)
    stride = mine[0].shape[0] // CHUNK_PEERS
    proj = [] if later else [shape_of(2, nblocks, BLK)]
    proj_scratch = [pltpu.VMEM((2, nblocks, BLK), F32)] if later else []
    return call(
        functools.partial(operator_kernel, bool(later), chunks),
        "second_pass" if later else "first_pass",
        [
            *[shape_of(*mine[0].shape)] * chunks,
            shape_of(nblocks * cam_sum_rows(NP), BLK),
            shape_of(3, tiles, BLK),
            shape_of(2, CHUNK_PEERS // chunks, stride, BLK),
            shape_of(8, BLK),
            shape_of(EXTRA, BLK),
        ]
        + proj,
        (pos, jac, jp, oc, op, b_mat, bt, inv, pick) + mine + other + later,
        [
            pltpu.VMEM((point_stage_rows(3) * GROUP, BLK), F32),
            pltpu.VMEM((cam_stage_rows(NP) * GROUP, BLK), F32),
            pltpu.VMEM((NP, nblocks, BLK), F32),
            pltpu.VMEM((tiles * point_stage_rows(3), BLK), F32),
        ]
        + proj_scratch,
        smem=(0,),
    )


def message_sum(got):
    rows = got.shape[0] // CHUNK_PEERS
    total = got[0:rows, :]
    for d in range(1, CHUNK_PEERS):
        total = total + got[d * rows : (d + 1) * rows, :]
    return total


def send_all(msg, values, scalar):
    stride = values.shape[0]
    data = stride - EXTRA
    row = lax.broadcasted_iota(jnp.int32, values.shape, 0)
    lanes = jnp.sum(jnp.where(row < data, scalar, 0.0), axis=0, keepdims=True)
    out = jnp.where(row < data, values, jnp.where(row == data, lanes, 0.0))
    for d in range(CHUNK_PEERS):
        msg[d * stride : (d + 1) * stride, :] = out


def start_kernel(quarter, pos, got, grad, damp, msg, state, rows):
    data = NP * quarter
    rows[...] = jnp.ones(rows.shape, F32)
    for i in range(quarter):
        lanes = pl.ds(pl.multiple_of((pos[1] * quarter + i) * BLK, BLK), BLK)
        rows[0, pl.ds(i, NP, stride=quarter), :] = grad[:, lanes]
        rows[1, pl.ds(i, NP, stride=quarter), :] = damp[:, lanes]
    total = message_sum(got)
    ones = jnp.ones((EXTRA, BLK), F32)
    rhs = rows[0] - jnp.concatenate([total[:data], ones], axis=0)
    precond = rows[1] + jnp.concatenate([total[data:], ones], axis=0)
    direction = rhs / precond
    state[0] = rhs
    state[1] = precond
    state[2] = rows[1]
    state[3] = direction
    send_all(msg, direction, rhs * direction)


def image_kernel(got, state, msg, image):
    direction = state[3]
    value = state[2] * direction + message_sum(got)
    image[...] = value
    send_all(msg, value / state[1], direction * value)


def last_kernel(got, state, image, norm_in, curv_in, resid_out, scal_out):
    norm = norm_in[0:1, 0:1]
    curv = curv_in[0:1, 0:1]
    step0 = norm / curv
    total = message_sum(got)
    stride = total.shape[0]
    sums = jnp.sum(total[stride - EXTRA :], axis=1, keepdims=True)
    zz, zd, norm1 = (sums[i : i + 1] for i in range(3))
    beta = norm1 / norm
    curv1 = zz + 2.0 * beta * zd + beta * beta * curv
    step1 = norm1 / curv1
    resid = state[0] - step0 * image[...]
    z = resid / state[1]
    image1 = (state[2] * z + total) + beta * image[...]
    resid_out[...] = resid - step1 * image1
    for i, s in enumerate((step0, step1, beta)):
        scal_out[i * 8 : (i + 1) * 8, :] = jnp.broadcast_to(s, (8, BLK))


def step_kernel(pos, scal, held0, held1, pg, sol0, sol1, cam_out, pt_out, pts_rows, cams_rows):
    step0, step1, beta = (scal[i * 8 : i * 8 + 1, 0:1] for i in range(3))
    tiles = pg.shape[1]
    for j in range(3):
        first = sol0[j]
        pts_rows[j * tiles : (j + 1) * tiles, :] = (
            pg[j] - step0 * first - step1 * (sol1[j] + beta * first)
        )
    for t in range(tiles):
        pt_out[:, t * BLK : (t + 1) * BLK] = pts_rows[pl.ds(t, 3, stride=tiles), :]
    quarters, stride = held0.shape[1], held0.shape[2]
    quarter = (stride - EXTRA) // NP
    for h in range(2):
        for x in range(quarters):
            d0 = held0[h, x]
            z = d0 - step0 * held1[h, x]
            cams_rows[...] = step0 * d0 + step1 * (z + beta * d0)
            put_cams(cam_out, cams_rows, pos[0] ^ h, x, quarters, quarter)


def put_cams(out, rows, core, x, quarters, quarter):
    for i in range(quarter):
        block = (core * quarters + x) * quarter + i
        lanes = pl.ds(pl.multiple_of(block * BLK, BLK), BLK)
        out[:, lanes] = rows[pl.ds(i, NP, stride=quarter), :]


def resid_kernel(pos, pieces, out, rows):
    quarters, stride = pieces.shape[1], pieces.shape[2]
    quarter = (stride - EXTRA) // NP
    for h in range(2):
        for s in range(quarters):
            x = (pos[4] + quarters - s) % quarters
            rows[...] = pieces[h, s]
            put_cams(out, rows, pos[0] ^ h, x, quarters, quarter)


def local(jac, jp, oc, op, entry, cov, cam_grad, cam_damp, pt_grad, pt_damp):
    quarters = lax.axis_size("x")
    owners = lax.axis_size("z") * lax.axis_size("y")
    peers = quarters * owners
    core = lax.axis_index("core")
    x = lax.axis_index("x")
    side = lax.axis_size("z")
    z, y = lax.axis_index("z"), lax.axis_index("y")

    pos = jnp.stack(
        [
            core,
            core * quarters + x,
            jnp.where(core == 0, y, z),
            jnp.where(core == 0, z, y),
            x,
            z,
            y,
        ]
    ).astype(jnp.int32)
    shard = cam_grad.shape[1]
    quarter = shard // BLK // 2 // quarters
    half = peers * quarter

    def exchange(v):
        return lax.ppermute(v, "core", [(0, 1), (1, 0)])

    def rank(x, c, z, y):
        return ((x * 2 + c) * side + z) * side + y

    xs, ss = range(quarters), range(side)
    every = ("x", "core", "z", "y")
    last_axes = [[rank(x, 0, z, y) for x in xs for y in ss] for z in ss]
    last_axes += [[rank(x, 1, z, y) for x in xs for z in ss] for y in ss]

    def shift(v, s):
        pairs = []
        for x in xs:
            for z in ss:
                for y in ss:
                    pairs.append((rank(x, 0, z, y), rank(x, 0, (z + s) % side, y)))
                    pairs.append((rank(x, 1, z, y), rank(x, 1, z, (y + s) % side)))
        return lax.ppermute(v, every, pairs)

    def over_last(v):
        shaped = v.reshape(CHUNK_PEERS, -1, BLK)
        got = lax.all_to_all(shaped, every, 0, 0, axis_index_groups=last_axes, tiled=False)
        return got.reshape(-1, BLK)

    stride = NP * quarter + EXTRA
    msg = shape_of(CHUNK_PEERS * stride, BLK)
    distance = [s ^ (s >> 1) for s in range(side)]
    chunk_order = sorted(range(1, side), key=lambda c: abs(distance[c] - side // 2)) + [0]

    def reduce_parts(others, pblk, bt, count, rows, *extra):
        theirs = {s: exchange(others[s]) for s in chunk_order}
        own = half_call(pblk, bt, side, count, rows, extra)
        moved = [shift(own[s] + theirs[s], -distance[s]) for s in chunk_order[:-1]]
        total = own[0] + theirs[0]
        for part in moved:
            total = total + part
        return over_last(total)

    def fetch(msg_out, b_mat):
        first = over_last(msg_out)
        moved = {s: shift(first, distance[s]) for s in chunk_order[:-1]}
        mine = (first,) + tuple(moved[s] for s in range(1, side))
        other = tuple(exchange(part) for part in mine)
        return pick_call(b_mat, mine), mine, other

    *others, pblk, inv, pg, place, bt = setup_call(
        pos, entry, cov, jac, jp, oc, op, pt_grad, pt_damp, side, quarters, 2 * half
    )
    places = jnp.arange(2 * half, dtype=jnp.int32)
    b_mat = (place.reshape(-1, 1) == places[None, :]).astype(BF16)
    got = reduce_parts(others, pblk, bt, 2 * NP, 2 * NP * quarter)
    msg_out, state = call(
        functools.partial(start_kernel, quarter),
        "start_step",
        [msg, shape_of(4, stride, BLK)],
        (pos, got, cam_grad, cam_damp),
        [pltpu.VMEM((2, stride, BLK), F32)],
        smem=(0,),
    )
    pick, mine, other = fetch(msg_out, b_mat)
    *others, pblk, sol0, held0, norm, extra, proj0 = operator_call(
        pos, jac, jp, oc, op, b_mat, bt, inv, pick, mine, other
    )
    got = reduce_parts(others, pblk, bt, NP, stride, extra)
    msg_out, image = call(
        image_kernel, "image_step", [msg, shape_of(stride, BLK)], (got, state)
    )
    pick, mine, other = fetch(msg_out, b_mat)
    *others, pblk, sol1, held1, curv, extra = operator_call(
        pos, jac, jp, oc, op, b_mat, bt, inv, pick, mine, other, (proj0, state, image, norm)
    )
    got = reduce_parts(others, pblk, bt, NP, stride, extra)
    resid, scal = call(
        last_kernel,
        "last_step",
        [shape_of(stride, BLK), shape_of(24, BLK)],
        (got, state, image, norm, curv),
    )
    pieces = [resid] + [
        lax.ppermute(resid, "x", [(i, (i + s) % quarters) for i in range(quarters)])
        for s in range(1, quarters)
    ]
    cam_step, pt_step = call(
        step_kernel,
        "result_step",
        [shape_of(NP, shard), shape_of(3, pt_grad.shape[1])],
        (pos, scal, held0, held1, pg, sol0, sol1),
        [pltpu.VMEM((3 * pg.shape[1], BLK), F32), pltpu.VMEM((stride, BLK), F32)],
        smem=(0,),
        cost=pl.CostEstimate(flops=10**9, bytes_accessed=4 * 10**6, transcendentals=0),
    )
    row = jnp.stack(pieces)
    cam_resid = call(
        resid_kernel,
        "result_resid",
        shape_of(NP, shard),
        (pos, jnp.stack([row, exchange(row)])),
        [pltpu.VMEM((stride, BLK), F32)],
        smem=(0,),
    )
    return cam_step, cam_resid, pt_step


def solution(mesh):
    fine = Mesh(mesh.devices.reshape(4, 2, 4, 4), ("x", "core", "z", "y"))
    pts, cam = ("x", "core"), ("z", "y")
    every = pts + cam
    in_specs = (
        P(None, every, None),
        P(None, every, None),
        P(every, None),
        P(every, None),
        P(every),
        P(every, None),
        P(None, cam),
        P(None, cam),
        P(None, every),
        P(None, every),
    )
    out_specs = (P(None, cam), P(None, cam), P(None, every))
    return jax.shard_map(local, mesh=fine, in_specs=in_specs, out_specs=out_specs, check_vma=False)
```

```python
import functools

import jax
import jax.numpy as jnp
from jax import lax
from jax.experimental import pallas as pl
from jax.experimental.pallas import tpu as pltpu
from jax.sharding import Mesh, PartitionSpec as P

BLK = 128
BPT = 8
NP = 9
CHUNK_PEERS = 16
EXTRA = 4
F32 = jnp.float32
BF16 = jnp.bfloat16
GROUP = 128
VMEM_LIMIT = 24 * 1024 * 1024


def split3(x):
    hi = x.astype(BF16).astype(F32)
    rest = x - hi
    mid = rest.astype(BF16).astype(F32)
    return hi, mid, rest - mid


def apply_three(inverse, values):
    first = inverse[0] * values[0] + inverse[1] * values[1] + inverse[2] * values[2]
    second = inverse[1] * values[0] + inverse[3] * values[1] + inverse[4] * values[2]
    third = inverse[2] * values[0] + inverse[4] * values[1] + inverse[5] * values[2]
    return [first, second, third]


def lane_pick(table, idx):
    return jnp.take_along_axis(table, idx, axis=1, mode="promise_in_bounds")


def onehot_rows(idx_row):
    rows = lax.broadcasted_iota(jnp.int32, (BLK, BLK), 0)
    return jnp.where(rows == idx_row, 1.0, 0.0).astype(BF16)


NT = (((1,), (1,)), ((), ()))


def point_stage_rows(count):
    return -(-3 * count // 16) * 16


def cam_stage_rows(count):
    whole = count // 8 * 8
    return -(-(3 * whole + 8) // 16) * 16


def cam_sum_rows(count):
    return count // 8 * 8 + 8


def point_scatter(stage, vals, idx_ref, t, col):
    count = len(vals)
    group = vals[0].shape[0]
    high = point_stage_rows(count)
    for j, val in enumerate(vals):
        for s, piece in enumerate(split3(val)):
            row = s * count + j
            stage[row * group : (row + 1) * group, :] = piece
    tiles = group // BPT
    for u in range(0, tiles, 2):
        lhs, rhs = [], []
        for b in range(BPT):
            pair = [(u + v) * BPT + b for v in range(2)]
            lhs.append(
                jnp.concatenate([stage[pl.ds(c, high, stride=group), :] for c in pair], axis=0).astype(BF16)
            )
            rhs.append(
                jnp.concatenate([onehot_rows(idx_ref[pl.ds(t * group + c, 1), :]) for c in pair], axis=0)
            )
        res = lax.dot_general(
            jnp.concatenate(lhs, axis=1), jnp.concatenate(rhs, axis=1), NT, preferred_element_type=F32
        )
        for v in range(2):
            start = pl.multiple_of((t * tiles + u + v) * high, 16)
            col[pl.ds(start, high), :] = res[v * high : (v + 1) * high, v * BLK : (v + 1) * BLK]


def point_sums(col, count, tiles):
    high = point_stage_rows(count)
    out = []
    for j in range(count):
        pieces = [col[pl.ds(s * count + j, tiles, stride=high), :] for s in range(3)]
        out.append(pieces[0] + (pieces[1] + pieces[2]))
    return out


def cam_scatter(stage, vals, idx_ref, t, pblk):
    count = len(vals)
    whole = count // 8 * 8
    rest = count - whole
    group = vals[0].shape[0]
    high = cam_stage_rows(count)
    keep = cam_sum_rows(count)
    for k, val in enumerate(vals):
        for s, piece in enumerate(split3(val)):
            row = s * whole + k if k < whole else 3 * whole + s * rest + k - whole
            stage[row * group : (row + 1) * group, :] = piece
    for b in range(0, group, 2):
        lhs = jnp.concatenate(
            [stage[pl.ds(b + v, high, stride=group), :] for v in range(2)], axis=0
        ).astype(BF16)
        rhs = jnp.concatenate(
            [onehot_rows(idx_ref[pl.ds(t * group + b + v, 1), :]) for v in range(2)], axis=0
        )
        both = lax.dot_general(lhs, rhs, NT, preferred_element_type=F32)
        for v in range(2):
            res = both[v * high : (v + 1) * high, v * BLK : (v + 1) * BLK]
            start = pl.multiple_of((t * group + b + v) * keep, 8)
            pblk[pl.ds(start, whole), :] = (
                res[0:whole] + res[whole : 2 * whole] + res[2 * whole : 3 * whole]
            )
            pblk[pl.ds(start + whole, 8), :] = res[3 * whole : 3 * whole + 8]


def pieces_wide(arrays):
    return jnp.concatenate([p for x in arrays for p in split3(x)], axis=1).astype(BF16)


def pieces_sum(res, i):
    res = res[:, 3 * i * BLK : 3 * (i + 1) * BLK]
    return res[:, :BLK] + res[:, BLK : 2 * BLK] + res[:, 2 * BLK :]


def blocks_to_dense(pblk, bt_ref, h, count, outs):
    nblocks = bt_ref.shape[1]
    half = bt_ref.shape[0] // 2
    sub = CHUNK_PEERS
    peers = len(outs) * sub
    quarter = half // peers
    stride = outs[0].shape[0] // sub
    whole = count // 8 * 8
    rest = count - whole
    keep = cam_sum_rows(count)
    for k0 in range(0, count, 2):
        ks = range(k0, min(k0 + 2, count))
        arrays = []
        for k in ks:
            if k < whole:
                arrays.append(pblk[pl.ds(k, nblocks, stride=keep), :])
            else:
                p = [pblk[pl.ds(k + s * rest, nblocks, stride=keep), :] for s in range(3)]
                arrays.append(p[0] + (p[1] + p[2]))
        both = jnp.dot(
            bt_ref[h * half : (h + 1) * half, :], pieces_wide(arrays), preferred_element_type=F32
        )
        for n, k in enumerate(ks):
            res = pieces_sum(both, n)
            for i in range(quarter):
                for s, out in enumerate(outs):
                    first = i * peers + s * sub
                    out[pl.ds(k * quarter + i, sub, stride=stride), :] = res[first : first + sub]


def half_kernel(count, chunks, *refs):
    pblk, bt = refs[:2]
    outs = refs[-chunks:]
    blocks_to_dense(pblk, bt, 0, count, outs)
    if len(refs) > chunks + 2:
        fill_extra(outs, [refs[2][i : i + 1, :] for i in range(EXTRA)])


def half_call(pblk, bt, chunks, count, stride, extra=()):
    return call(
        functools.partial(half_kernel, count, chunks),
        "own_half",
        [shape_of(CHUNK_PEERS * stride, BLK)] * chunks,
        (pblk, bt) + extra,
        cost=pl.CostEstimate(flops=10**9, bytes_accessed=4 * 10**6, transcendentals=0),
    )


def pick_half(b_ref, h, msgs, k0, count):
    sub = CHUNK_PEERS
    half = b_ref.shape[1] // 2
    quarter = half // (sub * len(msgs))
    stride = msgs[0].shape[0] // sub
    arrays = [
        jnp.concatenate(
            [msg[pl.ds(k * quarter + i, sub, stride=stride), :] for i in range(quarter) for msg in msgs],
            axis=0,
        )
        for k in range(k0, k0 + count)
    ]
    both = jnp.dot(
        b_ref[:, h * half : (h + 1) * half], pieces_wide(arrays), preferred_element_type=F32
    )
    return [pieces_sum(both, n) for n in range(count)]


def pick_kernel(b_mat, *refs):
    pick = refs[-1]
    for k0 in range(0, NP, 2):
        count = min(2, NP - k0)
        for n, value in enumerate(pick_half(b_mat, 0, refs[:-1], k0, count)):
            pick[k0 + n] = value


def pick_call(b_mat, mine):
    return call(
        pick_kernel,
        "pick_own_half",
        shape_of(NP, b_mat.shape[0], BLK),
        (b_mat,) + mine,
        cost=pl.CostEstimate(flops=10**9, bytes_accessed=4 * 10**6, transcendentals=0),
    )


def fill_extra(msgs, rows):
    for msg in msgs:
        stride = msg.shape[0] // CHUNK_PEERS
        for i, row in enumerate(rows):
            msg[pl.ds(stride - EXTRA + i, CHUNK_PEERS, stride=stride), :] = jnp.broadcast_to(
                row, (CHUNK_PEERS, BLK)
            )


def extra_sum(msgs, index):
    stride = msgs[0].shape[0] // CHUNK_PEERS
    rows = [msg[pl.ds(stride - EXTRA + index, CHUNK_PEERS, stride=stride), :] for msg in msgs]
    total = jnp.sum(functools.reduce(jnp.add, rows), axis=0, keepdims=True)
    return jnp.sum(total, axis=1, keepdims=True)


def spread_points(ref, t, group, pidx):
    tiles = group // BPT
    out = []
    for j in range(3):
        table = [
            jnp.broadcast_to(ref[j, pl.ds(t * tiles + u, 1), :], (BPT, BLK)) for u in range(tiles)
        ]
        out.append(lane_pick(jnp.concatenate(table, axis=0), pidx))
    return out


def terms_kernel(pos, jp, op, col, stage):
    nblocks = op.shape[0]

    def terms(t, carry):
        rows = pl.ds(pl.multiple_of(t * GROUP, GROUP), GROUP)
        a = [jp[j, rows, :] for j in range(6)]
        vals = [
            a[p] * a[q] + a[3 + p] * a[3 + q]
            for p, q in [(0, 0), (0, 1), (0, 2), (1, 1), (1, 2), (2, 2)]
        ]
        point_scatter(stage, vals, op, t, col)
        return carry

    lax.fori_loop(0, nblocks // GROUP, terms, 0)


def place_rows(pos, entry_ref, cov_ref, table, quarters, side, half):
    owners, per_owner = cov_ref.shape
    peers = quarters * side * side
    quarter = half // peers
    table[...] = jnp.zeros(table.shape, jnp.int32)
    table[:, 0:per_owner] = cov_ref[...]
    entry = entry_ref[...]
    owner = entry // per_owner
    slot = entry % per_owner
    block = jnp.zeros(entry.shape, jnp.int32)
    for o in range(owners):
        row = jnp.broadcast_to(table[o : o + 1, :], entry.shape)
        block = jnp.where(owner == o, lane_pick(row, slot), block)
    core_of = block // (quarters * quarter)
    x_of = block // quarter % quarters
    owner_z, owner_y = owner // side, owner % side
    chunk = (jnp.where(core_of == 0, pos[5] - owner_z, pos[6] - owner_y) + side) % side
    chunk = chunk ^ (chunk >> 1)
    last = jnp.where(core_of == 0, owner_y, owner_z)
    return (
        (core_of ^ pos[0]) * half
        + (block % quarter) * peers
        + chunk * CHUNK_PEERS
        + x_of * side
        + last
    )


def setup_kernel(
    chunks, quarters, pos, entry, cov, col, jac, jp, oc, op, pt_grad, pt_damp, *refs
):
    others = refs[:chunks]
    pblk, inv_out, pg_out, place, bt, stage2, grad_rows, damp_rows, table = refs[chunks:]
    places = bt.shape[0]
    place[...] = place_rows(pos, entry, cov, table, quarters, chunks, places // 2)
    for r in range(place.shape[0]):
        row = lax.broadcasted_iota(jnp.int32, (places, BLK), 0)
        hit = row == place[r : r + 1, :]
        bt[:, r * BLK : (r + 1) * BLK] = jnp.where(hit, 1.0, 0.0).astype(BF16)
    nblocks = jac.shape[1]
    tiles = nblocks // BPT
    for t in range(tiles):
        lanes = slice(t * BLK, (t + 1) * BLK)
        grad_rows[pl.ds(t, 3, stride=tiles), :] = pt_grad[:, lanes]
        damp_rows[pl.ds(t, 3, stride=tiles), :] = pt_damp[:, lanes]
    grad = [grad_rows[j * tiles : (j + 1) * tiles, :] for j in range(3)]
    damp = [damp_rows[j * tiles : (j + 1) * tiles, :] for j in range(3)]

    entry = point_sums(col, 6, tiles)
    c00 = entry[0] + damp[0]
    c01 = entry[1]
    c02 = entry[2]
    c11 = entry[3] + damp[1]
    c12 = entry[4]
    c22 = entry[5] + damp[2]
    a00 = c11 * c22 - c12 * c12
    a01 = c02 * c12 - c01 * c22
    a02 = c01 * c12 - c02 * c11
    a11 = c00 * c22 - c02 * c02
    a12 = c01 * c02 - c00 * c12
    a22 = c00 * c11 - c01 * c01
    recip = 1.0 / (c00 * a00 + c01 * a01 + c02 * a02)
    inv = [a * recip for a in (a00, a01, a02, a11, a12, a22)]
    for j in range(6):
        inv_out[j] = inv[j]
    pg = apply_three(inv, grad)
    for j in range(3):
        pg_out[j] = pg[j]

    def rhs_terms(t, carry):
        rows = pl.ds(pl.multiple_of(t * GROUP, GROUP), GROUP)
        g = spread_points(pg_out, t, GROUP, op[rows, :])
        c0 = jp[0, rows, :] * g[0] + jp[1, rows, :] * g[1] + jp[2, rows, :] * g[2]
        c1 = jp[3, rows, :] * g[0] + jp[4, rows, :] * g[1] + jp[5, rows, :] * g[2]
        vals = []
        diag = []
        for k in range(NP):
            j0 = jac[k, rows, :]
            j1 = jac[NP + k, rows, :]
            vals.append(j0 * c0 + j1 * c1)
            diag.append(j0 * j0 + j1 * j1)
        cam_scatter(stage2, vals + diag, oc, t, pblk)
        return carry

    lax.fori_loop(0, nblocks // GROUP, rhs_terms, 0)
    blocks_to_dense(pblk, bt, 1, 2 * NP, others)


def call(kernel, name, out_shape, operands, scratch=(), smem=(), cost=None):
    return pl.pallas_call(
        kernel,
        in_specs=[
            pl.BlockSpec(memory_space=pltpu.SMEM if i in smem else pltpu.VMEM)
            for i in range(len(operands))
        ],
        out_shape=out_shape,
        scratch_shapes=scratch,
        compiler_params=pltpu.CompilerParams(vmem_limit_bytes=VMEM_LIMIT),
        cost_estimate=cost,
        name=name,
    )(*operands)


def shape_of(*dims):
    return jax.ShapeDtypeStruct(dims, F32)


def setup_call(pos, entry, cov, jac, jp, oc, op, pt_grad, pt_damp, chunks, quarters, places):
    nblocks = jac.shape[1]
    tiles = nblocks // BPT
    col = call(
        terms_kernel,
        "point_terms",
        shape_of(tiles * point_stage_rows(6), BLK),
        (pos, jp, op),
        [pltpu.VMEM((point_stage_rows(6) * GROUP, BLK), F32)],
        smem=(0,),
        cost=pl.CostEstimate(flops=4 * 10**9, bytes_accessed=10**7, transcendentals=0),
    )
    return call(
        functools.partial(setup_kernel, chunks, quarters),
        "setup_pass",
        [
            *[shape_of(NP * places // chunks, BLK)] * chunks,
            shape_of(nblocks * cam_sum_rows(2 * NP), BLK),
            shape_of(6, tiles, BLK),
            shape_of(3, tiles, BLK),
            jax.ShapeDtypeStruct((nblocks // BLK, BLK), jnp.int32),
            jax.ShapeDtypeStruct((places, nblocks), BF16),
        ],
        (pos, entry.reshape(nblocks // BLK, BLK), cov, col, jac, jp, oc, op, pt_grad, pt_damp),
        [
            pltpu.VMEM((cam_stage_rows(2 * NP) * GROUP, BLK), F32),
            pltpu.VMEM((3 * tiles, BLK), F32),
            pltpu.VMEM((3 * tiles, BLK), F32),
            pltpu.VMEM((cov.shape[0], BLK), jnp.int32),
        ],
        smem=(0,),
    )


def operator_kernel(second, chunks, *refs):
    pos, jac, jp, oc, op, b_mat, bt, inv, pick_in = refs[:9]
    mine_in, other_in = refs[9 : 9 + chunks], refs[9 + chunks : 9 + 2 * chunks]
    refs = refs[9 + 2 * chunks :]
    if second:
        proj_in, state, image, norm_in = refs[:4]
        refs = refs[4:]
    others = refs[:chunks]
    pblk, sol_out, held_out, scal_out, extra = refs[chunks : chunks + 5]
    refs = refs[chunks + 5 :]
    if second:
        stage, stage2, pick, col, proj = refs
    else:
        proj, stage, stage2, pick, col = refs
    nblocks = jac.shape[1]
    tiles = nblocks // BPT
    stride = mine_in[0].shape[0] // CHUNK_PEERS
    for k0 in range(0, NP, 2):
        count = min(2, NP - k0)
        for n, value in enumerate(pick_half(b_mat, 1, other_in, k0, count)):
            pick[k0 + n] = pick_in[k0 + n] + value
    for h, msgs in enumerate((mine_in, other_in)):
        for x in range(CHUNK_PEERS // chunks):
            start = pl.multiple_of((x * chunks + pos[2 + h]) * stride, 8)
            held_out[h, x] = msgs[0][pl.ds(start, stride), :]
    total = extra_sum(mine_in + other_in, 0)
    if second:
        norm = norm_in[0:1, 0:1]
        step_len = norm / total
        scal_out[...] = jnp.broadcast_to(total, (8, BLK))
        rhs, precond, damp, direction = (state[i] for i in range(4))
        resid = rhs - step_len * image[...]
        z = resid / precond
        keep = lax.broadcasted_iota(jnp.int32, (stride, BLK), 0) < stride - EXTRA

        def lanes(v):
            return jnp.sum(jnp.where(keep, v, 0.0), axis=0, keepdims=True)

        owner_sums = [lanes(damp * z * z), lanes(damp * z * direction), lanes(resid * z)]
    else:
        scal_out[...] = jnp.broadcast_to(total, (8, BLK))

    def project(t, carry):
        rows = pl.ds(pl.multiple_of(t * GROUP, GROUP), GROUP)
        cidx = oc[rows, :]
        p0 = jnp.zeros((GROUP, BLK), F32)
        p1 = jnp.zeros((GROUP, BLK), F32)
        for k in range(NP):
            v = lane_pick(pick[k, rows, :], cidx)
            p0 += jac[k, rows, :] * v
            p1 += jac[NP + k, rows, :] * v
        if second:
            p0 = proj_in[0, rows, :] - step_len * p0
            p1 = proj_in[1, rows, :] - step_len * p1
        proj[0, rows, :] = p0
        proj[1, rows, :] = p1
        vals = [jp[j, rows, :] * p0 + jp[3 + j, rows, :] * p1 for j in range(3)]
        point_scatter(stage, vals, op, t, col)
        return carry

    lax.fori_loop(0, nblocks // GROUP, project, 0)
    sol = apply_three([inv[j] for j in range(6)], point_sums(col, 3, tiles))
    for j in range(3):
        sol_out[j] = sol[j]

    def correct(t, carry):
        rows = pl.ds(pl.multiple_of(t * GROUP, GROUP), GROUP)
        g = spread_points(sol_out, t, GROUP, op[rows, :])
        p0 = proj[0, rows, :]
        p1 = proj[1, rows, :]
        c0 = p0 - (jp[0, rows, :] * g[0] + jp[1, rows, :] * g[1] + jp[2, rows, :] * g[2])
        c1 = p1 - (jp[3, rows, :] * g[0] + jp[4, rows, :] * g[1] + jp[5, rows, :] * g[2])
        if second:
            zz, zd = carry
            zz = zz + (p0 * c0 + p1 * c1)
            zd = zd + (proj_in[0, rows, :] * c0 + proj_in[1, rows, :] * c1)
            carry = (zz, zd)
        vals = [jac[k, rows, :] * c0 + jac[NP + k, rows, :] * c1 for k in range(NP)]
        cam_scatter(stage2, vals, oc, t, pblk)
        return carry

    zero = jnp.zeros((GROUP, BLK), F32)
    sums = lax.fori_loop(0, nblocks // GROUP, correct, (zero, zero) if second else 0)
    blocks_to_dense(pblk, bt, 1, NP, others)
    rows = []
    if second:
        rows = [
            jnp.sum(sums[0], axis=0, keepdims=True) + owner_sums[0],
            jnp.sum(sums[1], axis=0, keepdims=True) + owner_sums[1],
            owner_sums[2],
        ]
    rows += [jnp.zeros((1, BLK), F32)] * (EXTRA - len(rows))
    fill_extra(others, rows)
    extra[...] = jnp.concatenate(rows, axis=0)


def operator_call(pos, jac, jp, oc, op, b_mat, bt, inv, pick, mine, other, later=()):
    nblocks = jac.shape[1]
    tiles = nblocks // BPT
    chunks = len(mine)
    stride = mine[0].shape[0] // CHUNK_PEERS
    proj = [] if later else [shape_of(2, nblocks, BLK)]
    proj_scratch = [pltpu.VMEM((2, nblocks, BLK), F32)] if later else []
    return call(
        functools.partial(operator_kernel, bool(later), chunks),
        "second_pass" if later else "first_pass",
        [
            *[shape_of(*mine[0].shape)] * chunks,
            shape_of(nblocks * cam_sum_rows(NP), BLK),
            shape_of(3, tiles, BLK),
            shape_of(2, CHUNK_PEERS // chunks, stride, BLK),
            shape_of(8, BLK),
            shape_of(EXTRA, BLK),
        ]
        + proj,
        (pos, jac, jp, oc, op, b_mat, bt, inv, pick) + mine + other + later,
        [
            pltpu.VMEM((point_stage_rows(3) * GROUP, BLK), F32),
            pltpu.VMEM((cam_stage_rows(NP) * GROUP, BLK), F32),
            pltpu.VMEM((NP, nblocks, BLK), F32),
            pltpu.VMEM((tiles * point_stage_rows(3), BLK), F32),
        ]
        + proj_scratch,
        smem=(0,),
    )


def message_sum(got):
    rows = got.shape[0] // CHUNK_PEERS
    total = got[0:rows, :]
    for d in range(1, CHUNK_PEERS):
        total = total + got[d * rows : (d + 1) * rows, :]
    return total


def send_all(msg, values, scalar):
    stride = values.shape[0]
    data = stride - EXTRA
    row = lax.broadcasted_iota(jnp.int32, values.shape, 0)
    lanes = jnp.sum(jnp.where(row < data, scalar, 0.0), axis=0, keepdims=True)
    out = jnp.where(row < data, values, jnp.where(row == data, lanes, 0.0))
    for d in range(CHUNK_PEERS):
        msg[d * stride : (d + 1) * stride, :] = out


def start_kernel(quarter, pos, got, grad, damp, msg, state, rows):
    data = NP * quarter
    rows[...] = jnp.ones(rows.shape, F32)
    for i in range(quarter):
        lanes = pl.ds(pl.multiple_of((pos[1] * quarter + i) * BLK, BLK), BLK)
        rows[0, pl.ds(i, NP, stride=quarter), :] = grad[:, lanes]
        rows[1, pl.ds(i, NP, stride=quarter), :] = damp[:, lanes]
    total = message_sum(got)
    ones = jnp.ones((EXTRA, BLK), F32)
    rhs = rows[0] - jnp.concatenate([total[:data], ones], axis=0)
    precond = rows[1] + jnp.concatenate([total[data:], ones], axis=0)
    direction = rhs / precond
    state[0] = rhs
    state[1] = precond
    state[2] = rows[1]
    state[3] = direction
    send_all(msg, direction, rhs * direction)


def image_kernel(got, state, msg, image):
    direction = state[3]
    value = state[2] * direction + message_sum(got)
    image[...] = value
    send_all(msg, value / state[1], direction * value)


def last_kernel(got, state, image, norm_in, curv_in, resid_out, scal_out):
    norm = norm_in[0:1, 0:1]
    curv = curv_in[0:1, 0:1]
    step0 = norm / curv
    total = message_sum(got)
    stride = total.shape[0]
    sums = jnp.sum(total[stride - EXTRA :], axis=1, keepdims=True)
    zz, zd, norm1 = (sums[i : i + 1] for i in range(3))
    beta = norm1 / norm
    curv1 = zz + 2.0 * beta * zd + beta * beta * curv
    step1 = norm1 / curv1
    resid = state[0] - step0 * image[...]
    z = resid / state[1]
    image1 = (state[2] * z + total) + beta * image[...]
    resid_out[...] = resid - step1 * image1
    for i, s in enumerate((step0, step1, beta)):
        scal_out[i * 8 : (i + 1) * 8, :] = jnp.broadcast_to(s, (8, BLK))


def step_kernel(pos, scal, held0, held1, pg, sol0, sol1, cam_out, pt_out, pts_rows, cams_rows):
    step0, step1, beta = (scal[i * 8 : i * 8 + 1, 0:1] for i in range(3))
    tiles = pg.shape[1]
    for j in range(3):
        first = sol0[j]
        pts_rows[j * tiles : (j + 1) * tiles, :] = (
            pg[j] - step0 * first - step1 * (sol1[j] + beta * first)
        )
    for t in range(tiles):
        pt_out[:, t * BLK : (t + 1) * BLK] = pts_rows[pl.ds(t, 3, stride=tiles), :]
    quarters, stride = held0.shape[1], held0.shape[2]
    quarter = (stride - EXTRA) // NP
    for h in range(2):
        for x in range(quarters):
            d0 = held0[h, x]
            z = d0 - step0 * held1[h, x]
            cams_rows[...] = step0 * d0 + step1 * (z + beta * d0)
            put_cams(cam_out, cams_rows, pos[0] ^ h, x, quarters, quarter)


def put_cams(out, rows, core, x, quarters, quarter):
    for i in range(quarter):
        block = (core * quarters + x) * quarter + i
        lanes = pl.ds(pl.multiple_of(block * BLK, BLK), BLK)
        out[:, lanes] = rows[pl.ds(i, NP, stride=quarter), :]


def resid_kernel(pos, *refs):
    *pieces, out, rows = refs
    quarters, stride = len(pieces), pieces[0].shape[1]
    quarter = (stride - EXTRA) // NP
    for h in range(2):
        for s in range(quarters):
            x = (pos[4] + quarters - (s ^ (s >> 1))) % quarters
            rows[...] = pieces[s][h]
            put_cams(out, rows, pos[0] ^ h, x, quarters, quarter)


def local(jac, jp, oc, op, entry, cov, cam_grad, cam_damp, pt_grad, pt_damp):
    quarters = lax.axis_size("x")
    owners = lax.axis_size("z") * lax.axis_size("y")
    peers = quarters * owners
    core = lax.axis_index("core")
    x = lax.axis_index("x")
    side = lax.axis_size("z")
    z, y = lax.axis_index("z"), lax.axis_index("y")

    pos = jnp.stack(
        [
            core,
            core * quarters + x,
            jnp.where(core == 0, y, z),
            jnp.where(core == 0, z, y),
            x,
            z,
            y,
        ]
    ).astype(jnp.int32)
    shard = cam_grad.shape[1]
    quarter = shard // BLK // 2 // quarters
    half = peers * quarter

    def exchange(v):
        return lax.ppermute(v, "core", [(0, 1), (1, 0)])

    def rank(x, c, z, y):
        return ((x * 2 + c) * side + z) * side + y

    xs, ss = range(quarters), range(side)
    every = ("x", "core", "z", "y")
    last_axes = [[rank(x, 0, z, y) for x in xs for y in ss] for z in ss]
    last_axes += [[rank(x, 1, z, y) for x in xs for z in ss] for y in ss]

    def shift(v, s):
        pairs = []
        for x in xs:
            for z in ss:
                for y in ss:
                    pairs.append((rank(x, 0, z, y), rank(x, 0, (z + s) % side, y)))
                    pairs.append((rank(x, 1, z, y), rank(x, 1, z, (y + s) % side)))
        return lax.ppermute(v, every, pairs)

    def over_last(v):
        shaped = v.reshape(CHUNK_PEERS, -1, BLK)
        got = lax.all_to_all(shaped, every, 0, 0, axis_index_groups=last_axes, tiled=False)
        return got.reshape(-1, BLK)

    stride = NP * quarter + EXTRA
    msg = shape_of(CHUNK_PEERS * stride, BLK)
    distance = [s ^ (s >> 1) for s in range(side)]
    chunk_order = sorted(range(1, side), key=lambda c: abs(distance[c] - side // 2)) + [0]

    def reduce_parts(others, pblk, bt, count, rows, *extra):
        theirs = {s: exchange(others[s]) for s in chunk_order}
        own = half_call(pblk, bt, side, count, rows, extra)
        moved = [shift(own[s] + theirs[s], -distance[s]) for s in chunk_order[:-1]]
        total = own[0] + theirs[0]
        for part in moved:
            total = total + part
        return over_last(total)

    def fetch(msg_out, b_mat):
        first = over_last(msg_out)
        moved = {s: shift(first, distance[s]) for s in chunk_order[:-1]}
        mine = (first,) + tuple(moved[s] for s in range(1, side))
        other = tuple(exchange(part) for part in mine)
        return pick_call(b_mat, mine), mine, other

    *others, pblk, inv, pg, place, bt = setup_call(
        pos, entry, cov, jac, jp, oc, op, pt_grad, pt_damp, side, quarters, 2 * half
    )
    places = jnp.arange(2 * half, dtype=jnp.int32)
    b_mat = (place.reshape(-1, 1) == places[None, :]).astype(BF16)
    got = reduce_parts(others, pblk, bt, 2 * NP, 2 * NP * quarter)
    msg_out, state = call(
        functools.partial(start_kernel, quarter),
        "start_step",
        [msg, shape_of(4, stride, BLK)],
        (pos, got, cam_grad, cam_damp),
        [pltpu.VMEM((2, stride, BLK), F32)],
        smem=(0,),
    )
    pick, mine, other = fetch(msg_out, b_mat)
    *others, pblk, sol0, held0, norm, extra, proj0 = operator_call(
        pos, jac, jp, oc, op, b_mat, bt, inv, pick, mine, other
    )
    got = reduce_parts(others, pblk, bt, NP, stride, extra)
    msg_out, image = call(
        image_kernel, "image_step", [msg, shape_of(stride, BLK)], (got, state)
    )
    pick, mine, other = fetch(msg_out, b_mat)
    *others, pblk, sol1, held1, curv, extra = operator_call(
        pos, jac, jp, oc, op, b_mat, bt, inv, pick, mine, other, (proj0, state, image, norm)
    )
    got = reduce_parts(others, pblk, bt, NP, stride, extra)
    resid, scal = call(
        last_kernel,
        "last_step",
        [shape_of(stride, BLK), shape_of(24, BLK)],
        (got, state, image, norm, curv),
    )
    both = jnp.stack([resid, exchange(resid)])
    pieces = [both] + [
        lax.ppermute(both, "x", [(i, (i + (s ^ (s >> 1))) % quarters) for i in range(quarters)])
        for s in range(1, quarters)
    ]
    cam_step, pt_step = call(
        step_kernel,
        "result_step",
        [shape_of(NP, shard), shape_of(3, pt_grad.shape[1])],
        (pos, scal, held0, held1, pg, sol0, sol1),
        [pltpu.VMEM((3 * pg.shape[1], BLK), F32), pltpu.VMEM((stride, BLK), F32)],
        smem=(0,),
        cost=pl.CostEstimate(flops=10**9, bytes_accessed=4 * 10**6, transcendentals=0),
    )
    cam_resid = call(
        resid_kernel,
        "result_resid",
        shape_of(NP, shard),
        (pos, *pieces),
        [pltpu.VMEM((stride, BLK), F32)],
        smem=(0,),
    )
    return cam_step, cam_resid, pt_step


def solution(mesh):
    fine = Mesh(mesh.devices.reshape(4, 2, 4, 4), ("x", "core", "z", "y"))
    pts, cam = ("x", "core"), ("z", "y")
    every = pts + cam
    in_specs = (
        P(None, every, None),
        P(None, every, None),
        P(every, None),
        P(every, None),
        P(every),
        P(every, None),
        P(None, cam),
        P(None, cam),
        P(None, every),
        P(None, every),
    )
    out_specs = (P(None, cam), P(None, cam), P(None, every))
    return jax.shard_map(local, mesh=fine, in_specs=in_specs, out_specs=out_specs, check_vma=False)
```

```python
import functools

import jax
import jax.numpy as jnp
from jax import lax
from jax.experimental import pallas as pl
from jax.experimental.pallas import tpu as pltpu
from jax.sharding import Mesh, PartitionSpec as P

BLK = 128
BPT = 8
NP = 9
CHUNK_PEERS = 16
EXTRA = 4
F32 = jnp.float32
BF16 = jnp.bfloat16
GROUP = 128
VMEM_LIMIT = 24 * 1024 * 1024


def split3(x):
    hi = x.astype(BF16).astype(F32)
    rest = x - hi
    mid = rest.astype(BF16).astype(F32)
    return hi, mid, rest - mid


def apply_three(inverse, values):
    first = inverse[0] * values[0] + inverse[1] * values[1] + inverse[2] * values[2]
    second = inverse[1] * values[0] + inverse[3] * values[1] + inverse[4] * values[2]
    third = inverse[2] * values[0] + inverse[4] * values[1] + inverse[5] * values[2]
    return [first, second, third]


def lane_pick(table, idx):
    return jnp.take_along_axis(table, idx, axis=1, mode="promise_in_bounds")


def onehot_rows(idx_row):
    rows = lax.broadcasted_iota(jnp.int32, (BLK, BLK), 0)
    return jnp.where(rows == idx_row, 1.0, 0.0).astype(BF16)


NT = (((1,), (1,)), ((), ()))


def point_stage_rows(count):
    return -(-3 * count // 16) * 16


def cam_stage_rows(count):
    whole = count // 8 * 8
    return -(-(3 * whole + 8) // 16) * 16


def cam_sum_rows(count):
    return count // 8 * 8 + 8


def point_scatter(stage, vals, idx_ref, t, col):
    count = len(vals)
    group = vals[0].shape[0]
    high = point_stage_rows(count)
    for j, val in enumerate(vals):
        for s, piece in enumerate(split3(val)):
            row = s * count + j
            stage[row * group : (row + 1) * group, :] = piece
    tiles = group // BPT
    for u in range(0, tiles, 2):
        lhs, rhs = [], []
        for b in range(BPT):
            pair = [(u + v) * BPT + b for v in range(2)]
            lhs.append(
                jnp.concatenate([stage[pl.ds(c, high, stride=group), :] for c in pair], axis=0).astype(BF16)
            )
            rhs.append(
                jnp.concatenate([onehot_rows(idx_ref[pl.ds(t * group + c, 1), :]) for c in pair], axis=0)
            )
        res = lax.dot_general(
            jnp.concatenate(lhs, axis=1), jnp.concatenate(rhs, axis=1), NT, preferred_element_type=F32
        )
        for v in range(2):
            start = pl.multiple_of((t * tiles + u + v) * high, 16)
            col[pl.ds(start, high), :] = res[v * high : (v + 1) * high, v * BLK : (v + 1) * BLK]


def point_sums(col, count, tiles):
    high = point_stage_rows(count)
    out = []
    for j in range(count):
        pieces = [col[pl.ds(s * count + j, tiles, stride=high), :] for s in range(3)]
        out.append(pieces[0] + (pieces[1] + pieces[2]))
    return out


def cam_scatter(stage, vals, idx_ref, t, pblk):
    count = len(vals)
    whole = count // 8 * 8
    rest = count - whole
    group = vals[0].shape[0]
    high = cam_stage_rows(count)
    keep = cam_sum_rows(count)
    for k, val in enumerate(vals):
        for s, piece in enumerate(split3(val)):
            row = s * whole + k if k < whole else 3 * whole + s * rest + k - whole
            stage[row * group : (row + 1) * group, :] = piece
    for b in range(0, group, 2):
        lhs = jnp.concatenate(
            [stage[pl.ds(b + v, high, stride=group), :] for v in range(2)], axis=0
        ).astype(BF16)
        rhs = jnp.concatenate(
            [onehot_rows(idx_ref[pl.ds(t * group + b + v, 1), :]) for v in range(2)], axis=0
        )
        both = lax.dot_general(lhs, rhs, NT, preferred_element_type=F32)
        for v in range(2):
            res = both[v * high : (v + 1) * high, v * BLK : (v + 1) * BLK]
            start = pl.multiple_of((t * group + b + v) * keep, 8)
            pblk[pl.ds(start, whole), :] = (
                res[0:whole] + res[whole : 2 * whole] + res[2 * whole : 3 * whole]
            )
            pblk[pl.ds(start + whole, 8), :] = res[3 * whole : 3 * whole + 8]


def pieces_wide(arrays):
    return jnp.concatenate([p for x in arrays for p in split3(x)], axis=1).astype(BF16)


def pieces_sum(res, i):
    res = res[:, 3 * i * BLK : 3 * (i + 1) * BLK]
    return res[:, :BLK] + res[:, BLK : 2 * BLK] + res[:, 2 * BLK :]


def blocks_to_dense(pblk, bt_ref, h, count, outs):
    nblocks = bt_ref.shape[1]
    half = bt_ref.shape[0] // 2
    sub = CHUNK_PEERS
    peers = len(outs) * sub
    quarter = half // peers
    stride = outs[0].shape[0] // sub
    whole = count // 8 * 8
    rest = count - whole
    keep = cam_sum_rows(count)
    for k0 in range(0, count, 2):
        ks = range(k0, min(k0 + 2, count))
        arrays = []
        for k in ks:
            if k < whole:
                arrays.append(pblk[pl.ds(k, nblocks, stride=keep), :])
            else:
                p = [pblk[pl.ds(k + s * rest, nblocks, stride=keep), :] for s in range(3)]
                arrays.append(p[0] + (p[1] + p[2]))
        both = jnp.dot(
            bt_ref[h * half : (h + 1) * half, :], pieces_wide(arrays), preferred_element_type=F32
        )
        for n, k in enumerate(ks):
            res = pieces_sum(both, n)
            for i in range(quarter):
                for s, out in enumerate(outs):
                    first = i * peers + s * sub
                    out[pl.ds(k * quarter + i, sub, stride=stride), :] = res[first : first + sub]


def half_kernel(count, chunks, *refs):
    pblk, bt = refs[:2]
    outs = refs[-chunks:]
    blocks_to_dense(pblk, bt, 0, count, outs)
    if len(refs) > chunks + 2:
        fill_extra(outs, [refs[2][i : i + 1, :] for i in range(EXTRA)])


def half_call(pblk, bt, chunks, count, stride, extra=()):
    return call(
        functools.partial(half_kernel, count, chunks),
        "own_half",
        [shape_of(CHUNK_PEERS * stride, BLK)] * chunks,
        (pblk, bt) + extra,
        cost=pl.CostEstimate(flops=10**9, bytes_accessed=4 * 10**6, transcendentals=0),
    )


def pick_half(b_ref, h, msgs, k0, count):
    sub = CHUNK_PEERS
    half = b_ref.shape[1] // 2
    quarter = half // (sub * len(msgs))
    stride = msgs[0].shape[0] // sub
    arrays = [
        jnp.concatenate(
            [msg[pl.ds(k * quarter + i, sub, stride=stride), :] for i in range(quarter) for msg in msgs],
            axis=0,
        )
        for k in range(k0, k0 + count)
    ]
    both = jnp.dot(
        b_ref[:, h * half : (h + 1) * half], pieces_wide(arrays), preferred_element_type=F32
    )
    return [pieces_sum(both, n) for n in range(count)]


def pick_kernel(b_mat, *refs):
    pick = refs[-1]
    for k0 in range(0, NP, 2):
        count = min(2, NP - k0)
        for n, value in enumerate(pick_half(b_mat, 0, refs[:-1], k0, count)):
            pick[k0 + n] = value


def pick_call(b_mat, mine):
    return call(
        pick_kernel,
        "pick_own_half",
        shape_of(NP, b_mat.shape[0], BLK),
        (b_mat,) + mine,
        cost=pl.CostEstimate(flops=10**9, bytes_accessed=4 * 10**6, transcendentals=0),
    )


def fill_extra(msgs, rows):
    for msg in msgs:
        stride = msg.shape[0] // CHUNK_PEERS
        for i, row in enumerate(rows):
            msg[pl.ds(stride - EXTRA + i, CHUNK_PEERS, stride=stride), :] = jnp.broadcast_to(
                row, (CHUNK_PEERS, BLK)
            )


def extra_sum(msgs, index):
    stride = msgs[0].shape[0] // CHUNK_PEERS
    rows = [msg[pl.ds(stride - EXTRA + index, CHUNK_PEERS, stride=stride), :] for msg in msgs]
    total = jnp.sum(functools.reduce(jnp.add, rows), axis=0, keepdims=True)
    return jnp.sum(total, axis=1, keepdims=True)


def spread_points(ref, t, group, pidx):
    tiles = group // BPT
    out = []
    for j in range(3):
        table = [
            jnp.broadcast_to(ref[j, pl.ds(t * tiles + u, 1), :], (BPT, BLK)) for u in range(tiles)
        ]
        out.append(lane_pick(jnp.concatenate(table, axis=0), pidx))
    return out


def terms_kernel(pos, jp, op, col, stage):
    nblocks = op.shape[0]

    def terms(t, carry):
        rows = pl.ds(pl.multiple_of(t * GROUP, GROUP), GROUP)
        a = [jp[j, rows, :] for j in range(6)]
        vals = [
            a[p] * a[q] + a[3 + p] * a[3 + q]
            for p, q in [(0, 0), (0, 1), (0, 2), (1, 1), (1, 2), (2, 2)]
        ]
        point_scatter(stage, vals, op, t, col)
        return carry

    lax.fori_loop(0, nblocks // GROUP, terms, 0)


def place_rows(pos, entry_ref, cov_ref, table, quarters, side, half):
    owners, per_owner = cov_ref.shape
    peers = quarters * side * side
    quarter = half // peers
    table[...] = jnp.zeros(table.shape, jnp.int32)
    table[:, 0:per_owner] = cov_ref[...]
    entry = entry_ref[...]
    owner = entry // per_owner
    slot = entry % per_owner
    block = jnp.zeros(entry.shape, jnp.int32)
    for o in range(owners):
        row = jnp.broadcast_to(table[o : o + 1, :], entry.shape)
        block = jnp.where(owner == o, lane_pick(row, slot), block)
    core_of = block // (quarters * quarter)
    x_of = block // quarter % quarters
    owner_z, owner_y = owner // side, owner % side
    chunk = (jnp.where(core_of == 0, pos[5] - owner_z, pos[6] - owner_y) + side) % side
    chunk = chunk ^ (chunk >> 1)
    last = jnp.where(core_of == 0, owner_y, owner_z)
    return (
        (core_of ^ pos[0]) * half
        + (block % quarter) * peers
        + chunk * CHUNK_PEERS
        + x_of * side
        + last
    )


def setup_kernel(
    chunks, quarters, pos, entry, cov, col, jac, jp, oc, op, pt_grad, pt_damp, *refs
):
    others = refs[:chunks]
    pblk, inv_out, pg_out, place, bt, stage2, grad_rows, damp_rows, table = refs[chunks:]
    places = bt.shape[0]
    place[...] = place_rows(pos, entry, cov, table, quarters, chunks, places // 2)
    for r in range(place.shape[0]):
        row = lax.broadcasted_iota(jnp.int32, (places, BLK), 0)
        hit = row == place[r : r + 1, :]
        bt[:, r * BLK : (r + 1) * BLK] = jnp.where(hit, 1.0, 0.0).astype(BF16)
    nblocks = jac.shape[1]
    tiles = nblocks // BPT
    for t in range(tiles):
        lanes = slice(t * BLK, (t + 1) * BLK)
        grad_rows[pl.ds(t, 3, stride=tiles), :] = pt_grad[:, lanes]
        damp_rows[pl.ds(t, 3, stride=tiles), :] = pt_damp[:, lanes]
    grad = [grad_rows[j * tiles : (j + 1) * tiles, :] for j in range(3)]
    damp = [damp_rows[j * tiles : (j + 1) * tiles, :] for j in range(3)]

    entry = point_sums(col, 6, tiles)
    c00 = entry[0] + damp[0]
    c01 = entry[1]
    c02 = entry[2]
    c11 = entry[3] + damp[1]
    c12 = entry[4]
    c22 = entry[5] + damp[2]
    a00 = c11 * c22 - c12 * c12
    a01 = c02 * c12 - c01 * c22
    a02 = c01 * c12 - c02 * c11
    a11 = c00 * c22 - c02 * c02
    a12 = c01 * c02 - c00 * c12
    a22 = c00 * c11 - c01 * c01
    recip = 1.0 / (c00 * a00 + c01 * a01 + c02 * a02)
    inv = [a * recip for a in (a00, a01, a02, a11, a12, a22)]
    for j in range(6):
        inv_out[j] = inv[j]
    pg = apply_three(inv, grad)
    for j in range(3):
        pg_out[j] = pg[j]

    def rhs_terms(t, carry):
        rows = pl.ds(pl.multiple_of(t * GROUP, GROUP), GROUP)
        g = spread_points(pg_out, t, GROUP, op[rows, :])
        c0 = jp[0, rows, :] * g[0] + jp[1, rows, :] * g[1] + jp[2, rows, :] * g[2]
        c1 = jp[3, rows, :] * g[0] + jp[4, rows, :] * g[1] + jp[5, rows, :] * g[2]
        vals = []
        diag = []
        for k in range(NP):
            j0 = jac[k, rows, :]
            j1 = jac[NP + k, rows, :]
            vals.append(j0 * c0 + j1 * c1)
            diag.append(j0 * j0 + j1 * j1)
        cam_scatter(stage2, vals + diag, oc, t, pblk)
        return carry

    lax.fori_loop(0, nblocks // GROUP, rhs_terms, 0)
    blocks_to_dense(pblk, bt, 1, 2 * NP, others)


def call(kernel, name, out_shape, operands, scratch=(), smem=(), cost=None):
    return pl.pallas_call(
        kernel,
        in_specs=[
            pl.BlockSpec(memory_space=pltpu.SMEM if i in smem else pltpu.VMEM)
            for i in range(len(operands))
        ],
        out_shape=out_shape,
        scratch_shapes=scratch,
        compiler_params=pltpu.CompilerParams(vmem_limit_bytes=VMEM_LIMIT),
        cost_estimate=cost,
        name=name,
    )(*operands)


def shape_of(*dims):
    return jax.ShapeDtypeStruct(dims, F32)


def setup_call(pos, entry, cov, jac, jp, oc, op, pt_grad, pt_damp, chunks, quarters, places):
    nblocks = jac.shape[1]
    tiles = nblocks // BPT
    col = call(
        terms_kernel,
        "point_terms",
        shape_of(tiles * point_stage_rows(6), BLK),
        (pos, jp, op),
        [pltpu.VMEM((point_stage_rows(6) * GROUP, BLK), F32)],
        smem=(0,),
        cost=pl.CostEstimate(flops=4 * 10**9, bytes_accessed=10**7, transcendentals=0),
    )
    return call(
        functools.partial(setup_kernel, chunks, quarters),
        "setup_pass",
        [
            *[shape_of(NP * places // chunks, BLK)] * chunks,
            shape_of(nblocks * cam_sum_rows(2 * NP), BLK),
            shape_of(6, tiles, BLK),
            shape_of(3, tiles, BLK),
            jax.ShapeDtypeStruct((nblocks // BLK, BLK), jnp.int32),
            jax.ShapeDtypeStruct((places, nblocks), BF16),
        ],
        (pos, entry.reshape(nblocks // BLK, BLK), cov, col, jac, jp, oc, op, pt_grad, pt_damp),
        [
            pltpu.VMEM((cam_stage_rows(2 * NP) * GROUP, BLK), F32),
            pltpu.VMEM((3 * tiles, BLK), F32),
            pltpu.VMEM((3 * tiles, BLK), F32),
            pltpu.VMEM((cov.shape[0], BLK), jnp.int32),
        ],
        smem=(0,),
    )


def operator_kernel(second, chunks, *refs):
    pos, jac, jp, oc, op, b_mat, bt, inv, pick_in = refs[:9]
    mine_in, other_in = refs[9 : 9 + chunks], refs[9 + chunks : 9 + 2 * chunks]
    refs = refs[9 + 2 * chunks :]
    if second:
        proj_in, state, image, norm_in = refs[:4]
        refs = refs[4:]
    others = refs[:chunks]
    pblk, sol_out, held_out, scal_out, extra = refs[chunks : chunks + 5]
    refs = refs[chunks + 5 :]
    if second:
        stage, stage2, pick, col, proj = refs
    else:
        proj, stage, stage2, pick, col = refs
    nblocks = jac.shape[1]
    tiles = nblocks // BPT
    stride = mine_in[0].shape[0] // CHUNK_PEERS
    for k0 in range(0, NP, 2):
        count = min(2, NP - k0)
        for n, value in enumerate(pick_half(b_mat, 1, other_in, k0, count)):
            pick[k0 + n] = pick_in[k0 + n] + value
    for h, msgs in enumerate((mine_in, other_in)):
        for x in range(CHUNK_PEERS // chunks):
            start = pl.multiple_of((x * chunks + pos[2 + h]) * stride, 8)
            held_out[h, x] = msgs[0][pl.ds(start, stride), :]
    total = extra_sum(mine_in + other_in, 0)
    if second:
        norm = norm_in[0:1, 0:1]
        step_len = norm / total
        scal_out[...] = jnp.broadcast_to(total, (8, BLK))
        rhs, precond, damp, direction = (state[i] for i in range(4))
        resid = rhs - step_len * image[...]
        z = resid / precond
        keep = lax.broadcasted_iota(jnp.int32, (stride, BLK), 0) < stride - EXTRA

        def lanes(v):
            return jnp.sum(jnp.where(keep, v, 0.0), axis=0, keepdims=True)

        owner_sums = [lanes(damp * z * z), lanes(damp * z * direction), lanes(resid * z)]
    else:
        scal_out[...] = jnp.broadcast_to(total, (8, BLK))

    def project(t, carry):
        rows = pl.ds(pl.multiple_of(t * GROUP, GROUP), GROUP)
        cidx = oc[rows, :]
        p0 = jnp.zeros((GROUP, BLK), F32)
        p1 = jnp.zeros((GROUP, BLK), F32)
        for k in range(NP):
            v = lane_pick(pick[k, rows, :], cidx)
            p0 += jac[k, rows, :] * v
            p1 += jac[NP + k, rows, :] * v
        if second:
            p0 = proj_in[0, rows, :] - step_len * p0
            p1 = proj_in[1, rows, :] - step_len * p1
        proj[0, rows, :] = p0
        proj[1, rows, :] = p1
        vals = [jp[j, rows, :] * p0 + jp[3 + j, rows, :] * p1 for j in range(3)]
        point_scatter(stage, vals, op, t, col)
        return carry

    lax.fori_loop(0, nblocks // GROUP, project, 0)
    sol = apply_three([inv[j] for j in range(6)], point_sums(col, 3, tiles))
    for j in range(3):
        sol_out[j] = sol[j]

    def correct(t, carry):
        rows = pl.ds(pl.multiple_of(t * GROUP, GROUP), GROUP)
        g = spread_points(sol_out, t, GROUP, op[rows, :])
        p0 = proj[0, rows, :]
        p1 = proj[1, rows, :]
        c0 = p0 - (jp[0, rows, :] * g[0] + jp[1, rows, :] * g[1] + jp[2, rows, :] * g[2])
        c1 = p1 - (jp[3, rows, :] * g[0] + jp[4, rows, :] * g[1] + jp[5, rows, :] * g[2])
        if second:
            zz, zd = carry
            zz = zz + (p0 * c0 + p1 * c1)
            zd = zd + (proj_in[0, rows, :] * c0 + proj_in[1, rows, :] * c1)
            carry = (zz, zd)
        vals = [jac[k, rows, :] * c0 + jac[NP + k, rows, :] * c1 for k in range(NP)]
        cam_scatter(stage2, vals, oc, t, pblk)
        return carry

    zero = jnp.zeros((GROUP, BLK), F32)
    sums = lax.fori_loop(0, nblocks // GROUP, correct, (zero, zero) if second else 0)
    blocks_to_dense(pblk, bt, 1, NP, others)
    rows = []
    if second:
        rows = [
            jnp.sum(sums[0], axis=0, keepdims=True) + owner_sums[0],
            jnp.sum(sums[1], axis=0, keepdims=True) + owner_sums[1],
            owner_sums[2],
        ]
    rows += [jnp.zeros((1, BLK), F32)] * (EXTRA - len(rows))
    fill_extra(others, rows)
    extra[...] = jnp.concatenate(rows, axis=0)


def operator_call(pos, jac, jp, oc, op, b_mat, bt, inv, pick, mine, other, later=()):
    nblocks = jac.shape[1]
    tiles = nblocks // BPT
    chunks = len(mine)
    stride = mine[0].shape[0] // CHUNK_PEERS
    proj = [] if later else [shape_of(2, nblocks, BLK)]
    proj_scratch = [pltpu.VMEM((2, nblocks, BLK), F32)] if later else []
    return call(
        functools.partial(operator_kernel, bool(later), chunks),
        "second_pass" if later else "first_pass",
        [
            *[shape_of(*mine[0].shape)] * chunks,
            shape_of(nblocks * cam_sum_rows(NP), BLK),
            shape_of(3, tiles, BLK),
            shape_of(2, CHUNK_PEERS // chunks, stride, BLK),
            shape_of(8, BLK),
            shape_of(EXTRA, BLK),
        ]
        + proj,
        (pos, jac, jp, oc, op, b_mat, bt, inv, pick) + mine + other + later,
        [
            pltpu.VMEM((point_stage_rows(3) * GROUP, BLK), F32),
            pltpu.VMEM((cam_stage_rows(NP) * GROUP, BLK), F32),
            pltpu.VMEM((NP, nblocks, BLK), F32),
            pltpu.VMEM((tiles * point_stage_rows(3), BLK), F32),
        ]
        + proj_scratch,
        smem=(0,),
    )


def message_sum(got):
    rows = got.shape[0] // CHUNK_PEERS
    total = got[0:rows, :]
    for d in range(1, CHUNK_PEERS):
        total = total + got[d * rows : (d + 1) * rows, :]
    return total


def send_all(msg, values, scalar):
    stride = values.shape[0]
    data = stride - EXTRA
    row = lax.broadcasted_iota(jnp.int32, values.shape, 0)
    lanes = jnp.sum(jnp.where(row < data, scalar, 0.0), axis=0, keepdims=True)
    out = jnp.where(row < data, values, jnp.where(row == data, lanes, 0.0))
    for d in range(CHUNK_PEERS):
        msg[d * stride : (d + 1) * stride, :] = out


def start_kernel(quarter, pos, got, grad, damp, msg, state, rows):
    data = NP * quarter
    rows[...] = jnp.ones(rows.shape, F32)
    for i in range(quarter):
        lanes = pl.ds(pl.multiple_of((pos[1] * quarter + i) * BLK, BLK), BLK)
        rows[0, pl.ds(i, NP, stride=quarter), :] = grad[:, lanes]
        rows[1, pl.ds(i, NP, stride=quarter), :] = damp[:, lanes]
    total = message_sum(got)
    ones = jnp.ones((EXTRA, BLK), F32)
    rhs = rows[0] - jnp.concatenate([total[:data], ones], axis=0)
    precond = rows[1] + jnp.concatenate([total[data:], ones], axis=0)
    direction = rhs / precond
    state[0] = rhs
    state[1] = precond
    state[2] = rows[1]
    state[3] = direction
    send_all(msg, direction, rhs * direction)


def image_kernel(got, state, msg, image):
    direction = state[3]
    value = state[2] * direction + message_sum(got)
    image[...] = value
    send_all(msg, value / state[1], direction * value)


def last_kernel(got, state, image, norm_in, curv_in, resid_out, scal_out):
    norm = norm_in[0:1, 0:1]
    curv = curv_in[0:1, 0:1]
    step0 = norm / curv
    total = message_sum(got)
    stride = total.shape[0]
    sums = jnp.sum(total[stride - EXTRA :], axis=1, keepdims=True)
    zz, zd, norm1 = (sums[i : i + 1] for i in range(3))
    beta = norm1 / norm
    curv1 = zz + 2.0 * beta * zd + beta * beta * curv
    step1 = norm1 / curv1
    resid = state[0] - step0 * image[...]
    z = resid / state[1]
    image1 = (state[2] * z + total) + beta * image[...]
    resid_out[...] = resid - step1 * image1
    for i, s in enumerate((step0, step1, beta)):
        scal_out[i * 8 : (i + 1) * 8, :] = jnp.broadcast_to(s, (8, BLK))


def step_kernel(pos, scal, held0, held1, pg, sol0, sol1, cam_out, pt_out, pts_rows, cams_rows):
    step0, step1, beta = (scal[i * 8 : i * 8 + 1, 0:1] for i in range(3))
    tiles = pg.shape[1]
    for j in range(3):
        first = sol0[j]
        pts_rows[j * tiles : (j + 1) * tiles, :] = (
            pg[j] - step0 * first - step1 * (sol1[j] + beta * first)
        )
    for t in range(tiles):
        pt_out[:, t * BLK : (t + 1) * BLK] = pts_rows[pl.ds(t, 3, stride=tiles), :]
    quarters, stride = held0.shape[1], held0.shape[2]
    quarter = (stride - EXTRA) // NP
    for h in range(2):
        for x in range(quarters):
            d0 = held0[h, x]
            z = d0 - step0 * held1[h, x]
            cams_rows[...] = step0 * d0 + step1 * (z + beta * d0)
            put_cams(cam_out, cams_rows, pos[0] ^ h, x, quarters, quarter)


def put_cams(out, rows, core, x, quarters, quarter):
    for i in range(quarter):
        block = (core * quarters + x) * quarter + i
        lanes = pl.ds(pl.multiple_of(block * BLK, BLK), BLK)
        out[:, lanes] = rows[pl.ds(i, NP, stride=quarter), :]


def resid_kernel(pos, *refs):
    *pieces, out, rows = refs
    quarters, stride = len(pieces), pieces[0].shape[1]
    quarter = (stride - EXTRA) // NP
    for h in range(2):
        for s in range(quarters):
            x = (pos[4] + quarters - (s ^ (s >> 1))) % quarters
            rows[...] = pieces[s][h]
            put_cams(out, rows, pos[0] ^ h, x, quarters, quarter)


def local(jac, jp, oc, op, entry, cov, cam_grad, cam_damp, pt_grad, pt_damp):
    quarters = lax.axis_size("x")
    owners = lax.axis_size("z") * lax.axis_size("y")
    peers = quarters * owners
    core = lax.axis_index("core")
    x = lax.axis_index("x")
    side = lax.axis_size("z")
    z, y = lax.axis_index("z"), lax.axis_index("y")

    pos = jnp.stack(
        [
            core,
            core * quarters + x,
            jnp.where(core == 0, y, z),
            jnp.where(core == 0, z, y),
            x,
            z,
            y,
        ]
    ).astype(jnp.int32)
    shard = cam_grad.shape[1]
    quarter = shard // BLK // 2 // quarters
    half = peers * quarter

    def exchange(v):
        return lax.ppermute(v, "core", [(0, 1), (1, 0)])

    def rank(x, c, z, y):
        return ((x * 2 + c) * side + z) * side + y

    xs, ss = range(quarters), range(side)
    every = ("x", "core", "z", "y")
    last_axes = [[rank(x, 0, z, y) for x in xs for y in ss] for z in ss]
    last_axes += [[rank(x, 1, z, y) for x in xs for z in ss] for y in ss]

    def shift(v, s):
        pairs = []
        for x in xs:
            for z in ss:
                for y in ss:
                    pairs.append((rank(x, 0, z, y), rank(x, 0, (z + s) % side, y)))
                    pairs.append((rank(x, 1, z, y), rank(x, 1, z, (y + s) % side)))
        return lax.ppermute(v, every, pairs)

    def over_last(v):
        shaped = v.reshape(CHUNK_PEERS, -1, BLK)
        got = lax.all_to_all(shaped, every, 0, 0, axis_index_groups=last_axes, tiled=False)
        return got.reshape(-1, BLK)

    stride = NP * quarter + EXTRA
    msg = shape_of(CHUNK_PEERS * stride, BLK)
    distance = [s ^ (s >> 1) for s in range(side)]
    chunk_order = sorted(range(1, side), key=lambda c: abs(distance[c] - side // 2)) + [0]

    def reduce_parts(others, pblk, bt, count, rows, *extra):
        theirs = {s: exchange(others[s]) for s in chunk_order[:-1]}
        own = list(half_call(pblk, bt, side, count, rows, extra))
        late, own[0] = lax.optimization_barrier((others[0], own[0]))
        theirs[0] = exchange(late)
        moved = [shift(own[s] + theirs[s], -distance[s]) for s in chunk_order[:-1]]
        total = own[0] + theirs[0]
        for part in moved:
            total = total + part
        return over_last(total)

    def fetch(msg_out, b_mat):
        first = over_last(msg_out)
        moved = {s: shift(first, distance[s]) for s in chunk_order[:-1]}
        mine = (first,) + tuple(moved[s] for s in range(1, side))
        other = tuple(exchange(part) for part in mine)
        return pick_call(b_mat, mine), mine, other

    *others, pblk, inv, pg, place, bt = setup_call(
        pos, entry, cov, jac, jp, oc, op, pt_grad, pt_damp, side, quarters, 2 * half
    )
    places = jnp.arange(2 * half, dtype=jnp.int32)
    b_mat = (place.reshape(-1, 1) == places[None, :]).astype(BF16)
    got = reduce_parts(others, pblk, bt, 2 * NP, 2 * NP * quarter)
    msg_out, state = call(
        functools.partial(start_kernel, quarter),
        "start_step",
        [msg, shape_of(4, stride, BLK)],
        (pos, got, cam_grad, cam_damp),
        [pltpu.VMEM((2, stride, BLK), F32)],
        smem=(0,),
    )
    pick, mine, other = fetch(msg_out, b_mat)
    *others, pblk, sol0, held0, norm, extra, proj0 = operator_call(
        pos, jac, jp, oc, op, b_mat, bt, inv, pick, mine, other
    )
    got = reduce_parts(others, pblk, bt, NP, stride, extra)
    msg_out, image = call(
        image_kernel, "image_step", [msg, shape_of(stride, BLK)], (got, state)
    )
    pick, mine, other = fetch(msg_out, b_mat)
    *others, pblk, sol1, held1, curv, extra = operator_call(
        pos, jac, jp, oc, op, b_mat, bt, inv, pick, mine, other, (proj0, state, image, norm)
    )
    got = reduce_parts(others, pblk, bt, NP, stride, extra)
    resid, scal = call(
        last_kernel,
        "last_step",
        [shape_of(stride, BLK), shape_of(24, BLK)],
        (got, state, image, norm, curv),
    )
    both = jnp.stack([resid, exchange(resid)])
    pieces = [both] + [
        lax.ppermute(both, "x", [(i, (i + (s ^ (s >> 1))) % quarters) for i in range(quarters)])
        for s in range(1, quarters)
    ]
    cam_step, pt_step = call(
        step_kernel,
        "result_step",
        [shape_of(NP, shard), shape_of(3, pt_grad.shape[1])],
        (pos, scal, held0, held1, pg, sol0, sol1),
        [pltpu.VMEM((3 * pg.shape[1], BLK), F32), pltpu.VMEM((stride, BLK), F32)],
        smem=(0,),
        cost=pl.CostEstimate(flops=10**9, bytes_accessed=4 * 10**6, transcendentals=0),
    )
    cam_resid = call(
        resid_kernel,
        "result_resid",
        shape_of(NP, shard),
        (pos, *pieces),
        [pltpu.VMEM((stride, BLK), F32)],
        smem=(0,),
    )
    return cam_step, cam_resid, pt_step


def solution(mesh):
    fine = Mesh(mesh.devices.reshape(4, 2, 4, 4), ("x", "core", "z", "y"))
    pts, cam = ("x", "core"), ("z", "y")
    every = pts + cam
    in_specs = (
        P(None, every, None),
        P(None, every, None),
        P(every, None),
        P(every, None),
        P(every),
        P(every, None),
        P(None, cam),
        P(None, cam),
        P(None, every),
        P(None, every),
    )
    out_specs = (P(None, cam), P(None, cam), P(None, every))
    return jax.shard_map(local, mesh=fine, in_specs=in_specs, out_specs=out_specs, check_vma=False)
```
